32 devices in a mesh: groups: 2 (over x), blk: 16 (over z, y, core).
Axes of the slice: x: 2, y: 2, z: 4, core: 2. Of those that a mesh axis runs over, the one named last changes fastest.
Arguments:
- tokens: bfloat16 [4096, 2048], P(('groups', 'blk')), parts along dimension 0, may hold values from -6 to 6
- expert_ids: int32 [4096, 4], P(('groups', 'blk')), parts along dimension 0, may hold values from 0 to 7, all different within a row; in each aligned block of 128 rows (0 to 127, 128 to 255, ...) at most 96 rows name the same one
- route_gate: float32 [4096, 4], P(('groups', 'blk')), parts along dimension 0, may hold values from 0.1 to 1
- gate_up: bfloat16 [2, 12288, 2048], P(None, 'blk'), may hold values from -0.125 to 0.125
- down_proj: bfloat16 [12288, 2048], P('blk'), may hold values from -0.15625 to 0.15625
Outputs:
- combined: bfloat16 [4096, 2048], P(('groups', 'blk')), parts along dimension 0
The draws below stay inside these ranges and needn't reach their ends.
There are 2 independent parts, one for each index of `groups`. The reference program is written for one: setup_inputs(seed, part) draws one part's arguments, and reference() takes and returns one part's arrays. A program takes and returns all parts, laid end to end along the dimension named above; an argument that names none is the same for every part. Nothing has to cross between parts.
Inputs may be any that keep to these rules, and one draw needn't show every extreme that they name: `expert_ids`: each row names 4 different experts. Among the 128 rows of one device, no expert is named more than 96 times, and in every draw some expert reaches 96 on some device.
All inputs are finite; a program needn't handle non-finite values.
Results may differ from the reference program's by a relative error of at most 0.0057.
Values may be sent and summed in bfloat16 or wider, within the bound.
No kernel may reach another device: no remote copies, remote signals or barrier semaphores. Data moves between devices by JAX's collectives and lax.ppermute only.
A program may use at most 64 MiB of HBM per device.

```python
import math
import jax
import jax.numpy as jnp
import numpy as np
from jax import lax

D = 2048
FF = 1536
TOPK = 4
TOK_DEV = 128
EXPERTS = 8
CAP = 96
TOKENS = 2048
N_BLK = 16


def levels(key, shape, split, low, top_value):
    factor_of = 1.0
    for dim, parts in split:
        heights = jax.random.uniform(jax.random.fold_in(jax.random.fold_in(key, 6), dim), (parts,), jnp.float32, low / len(split), top_value / len(split))
        factor_of = factor_of * jnp.repeat(jnp.exp(heights), shape[dim] // parts).reshape((-1,) + (1,) * (len(shape) - 1 - dim))
    return factor_of


def shared_out(key, own, number, rows, count, top, bound, lean):
    sequence = jax.random.permutation(key, count)
    heavy_load, ordinary = shares(count, rows * top, bound, lean, True), shares(count, rows * top, bound, lean, False)
    places = jnp.arange(count)

    def named(sizes, rotation):
        used = int((sizes > 0).sum())
        fixed = max(1, used // 4)
        passed = fixed + (places - fixed + rotation * (used - fixed)) % max(1, count - fixed)
        return jnp.zeros((count,), jnp.int32).at[sequence[jnp.where(places < fixed, places, passed)]].set(jnp.asarray(sizes, jnp.int32))

    sizes = jnp.where(number % 4 == 0, named(heavy_load, number // 4), named(ordinary, number - number // 4 - 1))
    mixed = jax.random.permutation(jax.random.fold_in(own, 3), count)
    source_of, sink = mixed[0:count // 2 * 2:2], mixed[1:count // 2 * 2:2]
    room = jnp.minimum(sizes[source_of] - 1, bound - sizes[sink]) // 2
    room = jnp.where((source_of == sequence[0]) | (sink == sequence[0]) | (sizes[sink] == 0), 0, jnp.maximum(room, 0))
    passed = jax.random.randint(jax.random.fold_in(own, 4), (count // 2,), 0, 1 << 20) % (room + 1)
    sizes = sizes.at[source_of].add(-passed).at[sink].add(passed)
    labels = jnp.searchsorted(jnp.cumsum(sizes), jnp.arange(rows * top), side="right").astype(jnp.int32)
    grid = labels.reshape(top, rows).T
    grid = grid[jax.random.permutation(jax.random.fold_in(own, 1), rows)]
    rotation = jax.random.randint(jax.random.fold_in(own, 2), (rows, 1), 0, top)
    return jnp.take_along_axis(grid, (jnp.arange(top)[None, :] + rotation) % top, axis=1)


def shares(number_of, total, limit, lean, full):
    portions = [(1 << 20) // math.isqrt(standing ** lean) + 1 for standing in range(1, number_of + 1)]
    largest = limit if full else min(limit, max(-(-total // number_of), total * portions[0] // sum(portions)))
    least = 1 if total - largest >= number_of - 1 else 0
    holding, surplus = [largest] + [least] * (number_of - 1), total - largest - least * (number_of - 1)
    while surplus > 0:
        free = [i for i in range(1, number_of) if holding[i] < largest] or [i for i in range(1, number_of) if holding[i] < limit]
        pool, remaining = sum([portions[i] for i in free]), surplus
        for i in free:
            more = min(limit - holding[i], max(1, remaining * portions[i] // pool), surplus)
            holding[i] = holding[i] + more
            surplus = surplus - more
    return np.array(holding)


def scatter_about(rng, dims, width, limit, pieces=(), held_as=jnp.bfloat16):
    values = width * jax.random.normal(rng, dims, jnp.float32)
    if pieces:
        values = values * levels(rng, dims, pieces, -0.22, 0.18)
    return jnp.clip(values, -limit, limit).astype(held_as)


def setup_inputs(seed: int = 0, part: int = 0) -> dict:
    arg_keys = jax.random.split(jax.random.key(seed), 6)
    own_keys = jax.random.split(jax.random.fold_in(arg_keys[5], part), 6)
    tokens = scatter_about(own_keys[0], (TOKENS, D), 1.0, 6.0, ((0, 16),))
    expert_ids_keys = jax.random.split(jax.random.fold_in(own_keys[1], 1), TOKENS // TOK_DEV)
    expert_ids_turns = jax.random.permutation(jax.random.fold_in(own_keys[1], 3), TOKENS // TOK_DEV)
    expert_ids = jax.vmap(lambda own, number: shared_out(jax.random.fold_in(own_keys[1], 2), own, number, TOK_DEV, EXPERTS, TOPK, CAP, 2))(expert_ids_keys, expert_ids_turns).reshape((TOKENS, TOPK))
    route_gate = jnp.clip(jnp.exp(math.log(1.0) - 2.3025851 * jax.random.uniform(own_keys[2], (TOKENS, TOPK), jnp.float32) ** levels(own_keys[2], (TOKENS, TOPK), ((0, 16),), -0.2, 0.2)), 0.1, 1.0)
    gate_up = scatter_about(arg_keys[3], (2, EXPERTS * FF, D), D ** -0.5, 0.125, ((1, 16),))
    down_proj = scatter_about(arg_keys[4], (EXPERTS * FF, D), FF ** -0.5, 0.15625, ((0, 16),))
    return {"tokens": tokens, "expert_ids": expert_ids, "route_gate": route_gate, "gate_up": gate_up, "down_proj": down_proj}


def pick_rows(source, index_list):
    return source[index_list]


def reference(tokens, expert_ids, route_gate, gate_up, down_proj):
    half_units = FF // 2
    placements = TOK_DEV * TOPK
    chosen_ids = expert_ids.reshape(N_BLK, placements)
    onehot = (chosen_ids[:, :, None] == jnp.arange(EXPERTS, dtype=jnp.int32)[None, None, :]).astype(jnp.int32)
    ranked = jnp.sum((jnp.cumsum(onehot, axis=1) - 1) * onehot, axis=2).astype(jnp.int32)
    slot_index = (chosen_ids * CAP + ranked).astype(jnp.int32)
    token_of = (jnp.arange(placements, dtype=jnp.int32) // TOPK).astype(jnp.int32)
    device_row = jnp.arange(N_BLK, dtype=jnp.int32)[:, None]
    slot_table = jnp.full((N_BLK, EXPERTS * CAP), TOK_DEV, jnp.int32)
    slot_table = slot_table.at[device_row, slot_index].set(jnp.broadcast_to(token_of, (N_BLK, placements)))
    per_device = tokens.reshape(N_BLK, TOK_DEV, D)

    def per_expert(expert):
        listed = lax.dynamic_slice_in_dim(slot_table, (expert * CAP).astype(jnp.int32), CAP, 1)
        filled = listed < TOK_DEV
        safe_rows = jnp.where(filled, listed, 0).astype(jnp.int32)
        picked = jax.vmap(pick_rows)(per_device, safe_rows)
        picked = jnp.where(filled[:, :, None], picked, jnp.zeros((), jnp.bfloat16)).reshape(N_BLK * CAP, D)
        total = jnp.zeros((N_BLK * CAP, D), jnp.float32)
        for half_index in range(2):
            offset = (expert * FF + half_index * half_units).astype(jnp.int32)
            weights_in = lax.dynamic_slice_in_dim(gate_up, offset, half_units, 1)
            weights_out = lax.dynamic_slice_in_dim(down_proj, offset, half_units, 0)
            gating = jnp.dot(picked, weights_in[0].T, preferred_element_type=jnp.float32)
            lifted = jnp.dot(picked, weights_in[1].T, preferred_element_type=jnp.float32)
            hidden = (jax.nn.silu(gating) * lifted).astype(jnp.bfloat16)
            partial_value = jnp.dot(hidden, weights_out, preferred_element_type=jnp.float32).astype(jnp.bfloat16)
            total = total + partial_value.astype(jnp.float32)
        return total.reshape(N_BLK, CAP, D)

    outputs = lax.map(per_expert, jnp.arange(EXPERTS, dtype=jnp.int32))
    flattened = jnp.transpose(outputs, (1, 0, 2, 3)).reshape(N_BLK, EXPERTS * CAP, D)
    gathered = jax.vmap(pick_rows)(flattened, slot_index)
    weighted = gathered.reshape(N_BLK, TOK_DEV, TOPK, D) * route_gate.reshape(N_BLK, TOK_DEV, TOPK)[:, :, :, None]
    return jnp.sum(weighted, axis=2).reshape(TOKENS, D).astype(jnp.bfloat16)
```

```python
import jax
import jax.numpy as jnp
from jax import lax
from jax.sharding import PartitionSpec as P


def expert_half(slot_block, gate_up, down_proj):
    contract = (((1,), (1,)), ((), ()))
    gating = lax.dot_general(slot_block, gate_up[0], contract, preferred_element_type=jnp.float32)
    lifted = lax.dot_general(slot_block, gate_up[1], contract, preferred_element_type=jnp.float32)
    hidden = (jax.nn.silu(gating) * lifted).astype(jnp.bfloat16)
    return jnp.dot(hidden, down_proj, preferred_element_type=jnp.float32).astype(jnp.bfloat16)


def by_slots(tokens, expert_ids, route_gate, gate_up, down_proj):
    tok_count, per_token = expert_ids.shape
    feature_width = tokens.shape[1]
    devices = lax.axis_size("blk")
    experts = devices // 2
    capacity = 3 * tok_count * per_token // devices
    placements = tok_count * per_token
    chosen_ids = expert_ids.reshape(placements)
    onehot = (chosen_ids[:, None] == jnp.arange(experts, dtype=jnp.int32)[None, :]).astype(
        jnp.int32
    )
    ranked = jnp.sum((jnp.cumsum(onehot, axis=0) - 1) * onehot, axis=1)
    slot_index = chosen_ids * capacity + ranked
    token_of = jnp.arange(placements, dtype=jnp.int32) // per_token
    slot_table = jnp.full((experts * capacity,), tok_count, jnp.int32).at[slot_index].set(token_of)
    outgoing = jnp.take(tokens, slot_table, axis=0, mode="fill", fill_value=0)
    outgoing = outgoing.reshape(experts, capacity, feature_width)
    doubled = jnp.repeat(outgoing, 2, axis=0)
    received = lax.all_to_all(doubled, "blk", split_axis=0, concat_axis=0, tiled=True)
    item_count = received.shape[1]
    partial_value = expert_half(received.reshape(-1, feature_width), gate_up, down_proj)
    partial_value = partial_value.reshape(devices, item_count, feature_width)
    returned_rows = lax.all_to_all(partial_value, "blk", split_axis=0, concat_axis=0, tiled=True)
    halves = returned_rows.reshape(experts, 2, capacity, feature_width).astype(jnp.float32)
    results = halves[:, 0] + halves[:, 1]
    flattened = results.reshape(experts * capacity, feature_width)
    picked = jnp.take(flattened, slot_index, axis=0)
    weighted = picked.reshape(tok_count, per_token, feature_width) * route_gate[:, :, None]
    return jnp.sum(weighted, axis=1).astype(jnp.bfloat16)


def by_tokens(tokens, expert_ids, route_gate, gate_up, down_proj):
    devices = lax.axis_size("blk")
    experts = devices // 2
    mine = lax.axis_index("blk") // 2
    chosen = expert_ids[:, :, None] == jnp.arange(experts, dtype=jnp.int32)[None, None, :]
    weight = jnp.sum(jnp.where(chosen, route_gate[:, :, None], 0.0), axis=1)
    weights = lax.all_gather(weight.T, "blk", axis=0, tiled=False)
    weights = lax.dynamic_index_in_dim(weights, mine, 1, keepdims=False).reshape(-1, 1)
    rows = lax.all_gather(tokens, "blk", axis=0, tiled=True)
    contract = (((1,), (1,)), ((), ()))
    gating = lax.dot_general(rows, gate_up[0], contract, preferred_element_type=jnp.float32)
    lifted = lax.dot_general(rows, gate_up[1], contract, preferred_element_type=jnp.float32)
    hidden = (jax.nn.silu(gating) * lifted * weights).astype(jnp.bfloat16)
    partial_value = jnp.dot(hidden, down_proj, preferred_element_type=jnp.float32).astype(jnp.bfloat16)
    return lax.psum_scatter(partial_value, "blk", scatter_dimension=0, tiled=True)


def solution(mesh):
    placed = (
        P(("groups", "blk"), None),
        P(("groups", "blk"), None),
        P(("groups", "blk"), None),
        P(None, "blk", None),
        P("blk", None),
    )

    def per_device(tokens, expert_ids, route_gate, gate_up, down_proj):
        experts = mesh.shape["blk"] // 2
        body = by_tokens if experts <= 2 * expert_ids.shape[1] else by_slots
        return body(tokens, expert_ids, route_gate, gate_up, down_proj)

    return jax.shard_map(
        per_device,
        mesh=mesh,
        in_specs=placed,
        out_specs=P(("groups", "blk"), None),
        check_vma=False,
    )
```

```python
import functools

import jax
import jax.numpy as jnp
from jax import lax
from jax.experimental import pallas as pl
from jax.experimental.pallas import tpu as pltpu
from jax.sharding import PartitionSpec as P


def expert_half(slot_block, gate_up, down_proj):
    contract = (((1,), (1,)), ((), ()))
    gating = lax.dot_general(slot_block, gate_up[0], contract, preferred_element_type=jnp.float32)
    lifted = lax.dot_general(slot_block, gate_up[1], contract, preferred_element_type=jnp.float32)
    hidden = (jax.nn.silu(gating) * lifted).astype(jnp.bfloat16)
    return jnp.dot(hidden, down_proj, preferred_element_type=jnp.float32).astype(jnp.bfloat16)


def by_slots(tokens, expert_ids, route_gate, gate_up, down_proj):
    tok_count, per_token = expert_ids.shape
    feature_width = tokens.shape[1]
    devices = lax.axis_size("blk")
    experts = devices // 2
    capacity = 3 * tok_count * per_token // devices
    placements = tok_count * per_token
    chosen_ids = expert_ids.reshape(placements)
    onehot = (chosen_ids[:, None] == jnp.arange(experts, dtype=jnp.int32)[None, :]).astype(
        jnp.int32
    )
    ranked = jnp.sum((jnp.cumsum(onehot, axis=0) - 1) * onehot, axis=1)
    slot_index = chosen_ids * capacity + ranked
    token_of = jnp.arange(placements, dtype=jnp.int32) // per_token
    slot_table = jnp.full((experts * capacity,), tok_count, jnp.int32).at[slot_index].set(token_of)
    outgoing = jnp.take(tokens, slot_table, axis=0, mode="fill", fill_value=0)
    outgoing = outgoing.reshape(experts, capacity, feature_width)
    doubled = jnp.repeat(outgoing, 2, axis=0)
    received = lax.all_to_all(doubled, "blk", split_axis=0, concat_axis=0, tiled=True)
    item_count = received.shape[1]
    partial_value = expert_half(received.reshape(-1, feature_width), gate_up, down_proj)
    partial_value = partial_value.reshape(devices, item_count, feature_width)
    returned_rows = lax.all_to_all(partial_value, "blk", split_axis=0, concat_axis=0, tiled=True)
    halves = returned_rows.reshape(experts, 2, capacity, feature_width).astype(jnp.float32)
    results = halves[:, 0] + halves[:, 1]
    flattened = results.reshape(experts * capacity, feature_width)
    picked = jnp.take(flattened, slot_index, axis=0)
    weighted = picked.reshape(tok_count, per_token, feature_width) * route_gate[:, :, None]
    return jnp.sum(weighted, axis=1).astype(jnp.bfloat16)


def snake(chips):
    return list(range(0, chips, 2)) + list(range(chips - 1, 0, -2))


def half_expert_kernel(count, mine_ref, *refs):
    blocks, gates = refs[:count], refs[count : count + 2]
    gate_up_ref, down_ref, out_own, out_other, rows, total = refs[count + 2 :]
    step, steps = pl.program_id(0), pl.num_programs(0)

    @pl.when(step == 0)
    def _():
        at = 0
        for block in blocks:
            rows[at : at + block.shape[0], :] = block[...]
            at += block.shape[0]

    contract = (((1,), (1,)), ((), ()))
    taken = rows[...]
    gating = lax.dot_general(taken, gate_up_ref[0], contract, preferred_element_type=jnp.float32)
    lifted = lax.dot_general(taken, gate_up_ref[1], contract, preferred_element_type=jnp.float32)
    hidden = (gating / (1.0 + jnp.exp(-gating)) * lifted).astype(jnp.bfloat16)
    product = jnp.dot(hidden, down_ref[...], preferred_element_type=jnp.float32)

    @pl.when(step == 0)
    def _():
        total[...] = product

    @pl.when(step > 0)
    def _():
        total[...] += product

    @pl.when(step == steps - 1)
    def _():
        tokens = gates[0].shape[1]
        experts = gates[0].shape[0] // 2
        for core, out in enumerate((out_own, out_other)):
            for place in range(out.shape[0] // tokens):
                columns = gates[place][...].T
                column = lax.broadcasted_iota(jnp.int32, columns.shape, 1)
                wanted = column == mine_ref[0] + core * experts
                weight = jnp.sum(jnp.where(wanted, columns, 0.0), axis=1, keepdims=True)
                low = place * tokens
                here = core * out.shape[0] + low
                out[low : low + tokens, :] = (total[here : here + tokens, :] * weight).astype(out.dtype)


def half_expert(mine, blocks, gates, gate_up, down_proj):
    if len(gates) == 1:
        gates = gates * 2
    height = sum(block.shape[0] for block in blocks)
    units, width = down_proj.shape
    tile = 256 if units % 256 == 0 else units
    whole = pl.BlockSpec(memory_space=pltpu.VMEM)
    out = jax.ShapeDtypeStruct((height // 2, width), jnp.bfloat16)
    return pl.pallas_call(
        functools.partial(half_expert_kernel, len(blocks)),
        grid=(units // tile,),
        out_shape=(out, out),
        in_specs=[pl.BlockSpec(memory_space=pltpu.SMEM)]
        + [whole] * (len(blocks) + 2)
        + [
            pl.BlockSpec((2, tile, width), lambda i: (0, i, 0)),
            pl.BlockSpec((tile, width), lambda i: (i, 0)),
        ],
        out_specs=(whole, whole),
        scratch_shapes=[
            pltpu.VMEM((height, width), jnp.bfloat16),
            pltpu.VMEM((height, width), jnp.float32),
        ],
        compiler_params=pltpu.CompilerParams(vmem_limit_bytes=32 << 20),
        cost_estimate=pl.CostEstimate(
            flops=6 * height * units * width,
            bytes_accessed=6 * units * width + 4 * height * width,
            transcendentals=height * units,
        ),
    )(mine, *blocks, *gates, gate_up, down_proj)


def by_tokens(tokens, expert_ids, route_gate, gate_up, down_proj):
    chips = lax.axis_size("blk") // 2
    order = snake(chips)
    far = chips // 2
    up = [(2 * order[r] + c, 2 * order[(r + 1) % chips] + c) for r in range(chips) for c in (0, 1)]
    down = [(b, a) for a, b in up]
    cores = [(d, d ^ 1) for d in range(2 * chips)]

    def send(value, pairs):
        return lax.ppermute(value, "blk", pairs)

    mine = (lax.axis_index("blk") // 2).astype(jnp.int32).reshape(1)
    chosen = jnp.arange(chips, dtype=jnp.int32)[:, None, None] == expert_ids.T[None]
    weight = jnp.sum(jnp.where(chosen, route_gate.T[None], 0.0), axis=1)
    gates = jnp.concatenate([weight, send(weight, cores)])
    middle = tokens.shape[0] // 2

    def partials(blocks, weights):
        others = [send(block, cores) for block in blocks]
        own, other = half_expert(mine, blocks + others, weights, gate_up, down_proj)
        return own, send(other, cores)

    results = [partials([tokens], [gates])]
    above, below, gates_above, gates_below = tokens, tokens, gates, gates
    for step in range(1, far):
        above, below = send(above, down), send(below, up)
        gates_above, gates_below = send(gates_above, down), send(gates_below, up)
        results.append(partials([above, below], [gates_above, gates_below]))
    above, below = send(above[:middle], down), send(below[middle:], up)
    gates_above = send(gates_above, down)
    results.append(partials([above, below], [gates_above]))

    def both(pair, low, high):
        return pair[0][low:high].astype(jnp.float32) + pair[1][low:high].astype(jnp.float32)

    rows = tokens.shape[0]
    above = send(both(results[far], 0, middle).astype(jnp.bfloat16), up)
    below = send(both(results[far], middle, rows).astype(jnp.bfloat16), down)
    for step in range(far - 1, 0, -1):
        to_above, to_below = both(results[step], 0, rows), both(results[step], rows, 2 * rows)
        if step == far - 1:
            to_above = jnp.concatenate([to_above[:middle] + above, to_above[middle:]])
            to_below = jnp.concatenate([to_below[:middle], to_below[middle:] + below])
        else:
            to_above, to_below = to_above + above, to_below + below
        above, below = send(to_above.astype(jnp.bfloat16), up), send(to_below.astype(jnp.bfloat16), down)
    return (both(results[0], 0, rows) + above + below).astype(jnp.bfloat16)


def solution(mesh):
    placed = (
        P(("groups", "blk"), None),
        P(("groups", "blk"), None),
        P(("groups", "blk"), None),
        P(None, "blk", None),
        P("blk", None),
    )

    def per_device(tokens, expert_ids, route_gate, gate_up, down_proj):
        experts = mesh.shape["blk"] // 2
        body = by_tokens if experts <= 2 * expert_ids.shape[1] else by_slots
        return body(tokens, expert_ids, route_gate, gate_up, down_proj)

    return jax.shard_map(
        per_device,
        mesh=mesh,
        in_specs=placed,
        out_specs=P(("groups", "blk"), None),
        check_vma=False,
    )
```

```python
import functools

import jax
import jax.numpy as jnp
import numpy as np
from jax import lax
from jax.experimental import pallas as pl
from jax.experimental.pallas import tpu as pltpu
from jax.sharding import PartitionSpec as P


def expert_half(slot_block, gate_up, down_proj):
    contract = (((1,), (1,)), ((), ()))
    gating = lax.dot_general(slot_block, gate_up[0], contract, preferred_element_type=jnp.float32)
    lifted = lax.dot_general(slot_block, gate_up[1], contract, preferred_element_type=jnp.float32)
    hidden = (jax.nn.silu(gating) * lifted).astype(jnp.bfloat16)
    return jnp.dot(hidden, down_proj, preferred_element_type=jnp.float32).astype(jnp.bfloat16)


def by_slots(tokens, expert_ids, route_gate, gate_up, down_proj):
    tok_count, per_token = expert_ids.shape
    feature_width = tokens.shape[1]
    devices = lax.axis_size("blk")
    experts = devices // 2
    capacity = 3 * tok_count * per_token // devices
    placements = tok_count * per_token
    chosen_ids = expert_ids.reshape(placements)
    onehot = (chosen_ids[:, None] == jnp.arange(experts, dtype=jnp.int32)[None, :]).astype(
        jnp.int32
    )
    ranked = jnp.sum((jnp.cumsum(onehot, axis=0) - 1) * onehot, axis=1)
    slot_index = chosen_ids * capacity + ranked
    token_of = jnp.arange(placements, dtype=jnp.int32) // per_token
    slot_table = jnp.full((experts * capacity,), tok_count, jnp.int32).at[slot_index].set(token_of)
    outgoing = jnp.take(tokens, slot_table, axis=0, mode="fill", fill_value=0)
    outgoing = outgoing.reshape(experts, capacity, feature_width)
    doubled = jnp.repeat(outgoing, 2, axis=0)
    received = lax.all_to_all(doubled, "blk", split_axis=0, concat_axis=0, tiled=True)
    item_count = received.shape[1]
    partial_value = expert_half(received.reshape(-1, feature_width), gate_up, down_proj)
    partial_value = partial_value.reshape(devices, item_count, feature_width)
    returned_rows = lax.all_to_all(partial_value, "blk", split_axis=0, concat_axis=0, tiled=True)
    halves = returned_rows.reshape(experts, 2, capacity, feature_width).astype(jnp.float32)
    results = halves[:, 0] + halves[:, 1]
    flattened = results.reshape(experts * capacity, feature_width)
    picked = jnp.take(flattened, slot_index, axis=0)
    weighted = picked.reshape(tok_count, per_token, feature_width) * route_gate[:, :, None]
    return jnp.sum(weighted, axis=1).astype(jnp.bfloat16)


def snake(chips):
    return list(range(0, chips, 2)) + list(range(chips - 1, 0, -2))


def sources(chips):
    order = snake(chips)
    table = np.zeros((2 * chips, 2 * chips), np.int32)
    for place in range(chips):
        for core in (0, 1):
            turn = 1 - 2 * core
            row = [(0, core), (0, 1 - core)]
            for step in range(1, chips // 2):
                row += [(-step, core), (-step, 1 - core), (step, 1 - core), (step, core)]
            row += [(chips // 2, core), (chips // 2, 1 - core)]
            table[2 * order[place] + core] = [2 * order[(place + turn * d) % chips] + c for d, c in row]
    return table


def half_expert_kernel(pieces, keep, sources_ref, gates_ref, *refs):
    blocks, (gate_up_ref, down_ref, out_keep, out_give, rows, hidden) = refs[:-6], refs[-6:]
    weights = []
    at = 0
    for operand, first, count, source, token in pieces:
        rows[at : at + count, :] = blocks[operand][first : first + count, :]
        at += count
        line = gates_ref[pl.ds(sources_ref[source], 1), :]
        column = jnp.broadcast_to(line, (8, line.shape[1])).T[:, :1]
        weights.append(column[token : token + count])
    weight = jnp.concatenate(weights)

    units, width = down_ref.shape
    tile = 256 if units % 256 == 0 else units
    contract = (((1,), (1,)), ((), ()))
    taken = rows[...]
    for low in range(0, units, tile):
        gating = lax.dot_general(taken, gate_up_ref[0, low : low + tile], contract, preferred_element_type=jnp.float32)
        lifted = lax.dot_general(taken, gate_up_ref[1, low : low + tile], contract, preferred_element_type=jnp.float32)
        hidden[:, low : low + tile] = (gating / (1.0 + jnp.exp(-gating)) * lifted).astype(jnp.bfloat16)
    inner = hidden[...]
    tile = 512 if width % 512 == 0 else width
    for low in range(0, width, tile):
        product = jnp.dot(inner, down_ref[:, low : low + tile], preferred_element_type=jnp.float32) * weight
        product = product.astype(jnp.bfloat16)
        out_keep[:, low : low + tile] = product[:keep]
        out_give[:, low : low + tile] = product[keep:]


def half_expert(places, gates, pieces, keep, blocks, gate_up, down_proj):
    height = sum(piece[2] for piece in pieces)
    units, width = down_proj.shape
    whole = pl.BlockSpec(memory_space=pltpu.VMEM)
    return pl.pallas_call(
        functools.partial(half_expert_kernel, tuple(pieces), keep),
        out_shape=(
            jax.ShapeDtypeStruct((keep, width), jnp.bfloat16),
            jax.ShapeDtypeStruct((height - keep, width), jnp.bfloat16),
        ),
        in_specs=[pl.BlockSpec(memory_space=pltpu.SMEM)] + [whole] * (len(blocks) + 3),
        out_specs=(whole, whole),
        scratch_shapes=[
            pltpu.VMEM((height, width), jnp.bfloat16),
            pltpu.VMEM((height, units), jnp.bfloat16),
        ],
        compiler_params=pltpu.CompilerParams(vmem_limit_bytes=32 << 20),
        cost_estimate=pl.CostEstimate(
            flops=6 * height * units * width,
            bytes_accessed=6 * units * width + 4 * height * width,
            transcendentals=height * units,
        ),
    )(places, gates, *blocks, gate_up, down_proj)


def by_tokens(tokens, expert_ids, route_gate, gate_up, down_proj):
    chips = lax.axis_size("blk") // 2
    order, far = snake(chips), chips // 2
    rows = tokens.shape[0]
    half = rows // 2
    chains = (0, 1)
    forth, back, across, home, cores = [], [], [], [], []
    for place in range(chips):
        for core in (0, 1):
            device = 2 * order[place] + core
            ahead, behind = order[(place + 1 - 2 * core) % chips], order[(place - 1 + 2 * core) % chips]
            forth.append((device, 2 * ahead + core))
            back.append((device, 2 * behind + core))
            across.append((device, 2 * behind + 1 - core))
            home.append((device, 2 * behind + 1 - core))
            cores.append((device, device ^ 1))

    def send(value, pairs):
        return lax.ppermute(value, "blk", pairs)

    def total(*terms):
        return sum(term.astype(jnp.float32) for term in terms)

    def rounded(value):
        return value.astype(jnp.bfloat16)

    def after(value, *earlier):
        return lax.optimization_barrier((value, *earlier))[0]

    parts = [tokens[c * half : (c + 1) * half] for c in chains]
    ring = [jnp.concatenate([send(part, forth), send(part, across)]) for part in parts]

    places = lax.dynamic_index_in_dim(jnp.asarray(sources(chips)), lax.axis_index("blk"), 0, keepdims=False)
    chosen = jnp.arange(chips, dtype=jnp.int32)[:, None, None] == expert_ids.T[None]
    weight = jnp.sum(jnp.where(chosen, route_gate.T[None], 0.0), axis=1)
    gates = lax.all_to_all(jnp.repeat(weight, 2, axis=0), "blk", split_axis=0, concat_axis=0, tiled=True)
    gates = gates.reshape(-1, rows)

    def partials(pieces, keep, blocks):
        kept, given = half_expert(places, gates, pieces, keep, blocks, gate_up, down_proj)
        return kept, send(given, cores)

    def of(chain, operand, source):
        return [(operand, i * half, half, source + i, chain * half) for i in (0, 1)]

    own = partials([(0, 0, rows, 0, 0), (1, 0, rows, 1, 0)], rows, [tokens, send(tokens, cores)])
    ring[0] = after(ring[0], own[0])

    results = {}
    for step in range(1, far):
        swapped = [send(block, cores) for block in ring]
        base = 2 + 4 * (step - 1)
        blocks = ring + swapped
        ring = [send(block if step < far - 1 else block[:half], forth) for block in ring]
        if step < far - 1:
            pieces = of(0, 0, base) + of(1, 1, base) + of(0, 2, base + 2) + of(1, 3, base + 2)
            kept, given = partials(pieces, 2 * rows, blocks)
            for c in chains:
                results[step, c] = kept[c * rows : (c + 1) * rows], given[c * rows : (c + 1) * rows]
            ring[0] = after(ring[0], kept)
        else:
            last = blocks
    earlier = ring[0]
    base = 2 + 4 * (far - 2)
    for c in chains:
        block = ring[c]
        swapped = send(block, cores)
        inputs = [after(last[c], earlier), last[2 + c]]
        results[far - 1, c] = partials(of(c, 0, base) + of(c, 1, base + 2), rows, inputs)
        swapped = after(swapped, results[far - 1, c][0])
        pieces = [(0, 0, half, base + 4, c * half), (1, 0, half, base + 5, c * half)]
        results[far, c] = partials(pieces, half, [block, swapped])
        earlier = results[far, c][0]

    sums = [None, None]
    earlier = tokens
    for step in range(far, 1, -1):
        for c in chains:
            kept, given = results[step, c]
            value = total(after(kept, earlier), given)
            if step == far - 1:
                value = jnp.concatenate([value[:half] + total(sums[c]), value[half:]])
            elif step < far - 1:
                value = value + total(sums[c])
            earlier = rounded(value)
            sums[c] = send(earlier, back)
    outs = []
    for c in chains:
        kept, given = results[1, c]
        kept = after(kept, earlier)
        mine = [part[c * half : (c + 1) * half] for part in own]
        for low, pairs in ((half, home), (0, back)):
            earlier = rounded(sum(total(term[low : low + half]) for term in (kept, given, sums[c])))
            mine.append(send(earlier, pairs))
        outs.append(rounded(total(*mine)))
    return jnp.concatenate(outs)


def solution(mesh):
    placed = (
        P(("groups", "blk"), None),
        P(("groups", "blk"), None),
        P(("groups", "blk"), None),
        P(None, "blk", None),
        P("blk", None),
    )

    def per_device(tokens, expert_ids, route_gate, gate_up, down_proj):
        experts = mesh.shape["blk"] // 2
        body = by_tokens if experts <= 2 * expert_ids.shape[1] else by_slots
        return body(tokens, expert_ids, route_gate, gate_up, down_proj)

    return jax.shard_map(
        per_device,
        mesh=mesh,
        in_specs=placed,
        out_specs=P(("groups", "blk"), None),
        check_vma=False,
    )
```

```python
import functools

import jax
import jax.numpy as jnp
import numpy as np
from jax import lax
from jax.experimental import pallas as pl
from jax.experimental.pallas import tpu as pltpu
from jax.sharding import PartitionSpec as P


def expert_half(slot_block, gate_up, down_proj):
    contract = (((1,), (1,)), ((), ()))
    gating = lax.dot_general(slot_block, gate_up[0], contract, preferred_element_type=jnp.float32)
    lifted = lax.dot_general(slot_block, gate_up[1], contract, preferred_element_type=jnp.float32)
    hidden = (jax.nn.silu(gating) * lifted).astype(jnp.bfloat16)
    return jnp.dot(hidden, down_proj, preferred_element_type=jnp.float32).astype(jnp.bfloat16)


def by_slots(tokens, expert_ids, route_gate, gate_up, down_proj):
    tok_count, per_token = expert_ids.shape
    feature_width = tokens.shape[1]
    devices = lax.axis_size("blk")
    experts = devices // 2
    capacity = 3 * tok_count * per_token // devices
    placements = tok_count * per_token
    chosen_ids = expert_ids.reshape(placements)
    onehot = (chosen_ids[:, None] == jnp.arange(experts, dtype=jnp.int32)[None, :]).astype(
        jnp.int32
    )
    ranked = jnp.sum((jnp.cumsum(onehot, axis=0) - 1) * onehot, axis=1)
    slot_index = chosen_ids * capacity + ranked
    token_of = jnp.arange(placements, dtype=jnp.int32) // per_token
    slot_table = jnp.full((experts * capacity,), tok_count, jnp.int32).at[slot_index].set(token_of)
    outgoing = jnp.take(tokens, slot_table, axis=0, mode="fill", fill_value=0)
    outgoing = outgoing.reshape(experts, capacity, feature_width)
    doubled = jnp.repeat(outgoing, 2, axis=0)
    received = lax.all_to_all(doubled, "blk", split_axis=0, concat_axis=0, tiled=True)
    item_count = received.shape[1]
    partial_value = expert_half(received.reshape(-1, feature_width), gate_up, down_proj)
    partial_value = partial_value.reshape(devices, item_count, feature_width)
    returned_rows = lax.all_to_all(partial_value, "blk", split_axis=0, concat_axis=0, tiled=True)
    halves = returned_rows.reshape(experts, 2, capacity, feature_width).astype(jnp.float32)
    results = halves[:, 0] + halves[:, 1]
    flattened = results.reshape(experts * capacity, feature_width)
    picked = jnp.take(flattened, slot_index, axis=0)
    weighted = picked.reshape(tok_count, per_token, feature_width) * route_gate[:, :, None]
    return jnp.sum(weighted, axis=1).astype(jnp.bfloat16)


def snake(chips):
    return list(range(0, chips, 2)) + list(range(chips - 1, 0, -2))


def sources(chips):
    order = snake(chips)
    table = np.zeros((2 * chips, 2 + 2 * chips), np.int32)
    for place in range(chips):
        for core in (0, 1):
            turn = 1 - 2 * core
            row = [(0, core), (0, 1 - core)]
            for step in range(1, chips // 2 + 1):
                row += [(-step, core), (-step, 1 - core), (step, 1 - core), (step, core)]
            table[2 * order[place] + core] = [2 * order[(place + turn * d) % chips] + c for d, c in row]
    return table


def half_expert_kernel(pieces, load, sources_ref, gates_ref, *refs):
    blocks, refs = refs[: len(pieces)], refs[len(pieces) :]
    if load:
        gate_up_far, down_far, out_keep, out_give, gate_up_ref, down_ref, rows, hidden, arrived = refs
    else:
        gate_up_ref, down_ref, out_keep, out_give, rows, hidden = refs
    units, width = down_ref.shape
    tile = 256 if units % 256 == 0 else units
    tiles = units // tile
    copies = []
    if load:
        for t in range(tiles):
            near = pl.ds(t * tile, tile)
            copies.append(pltpu.make_async_copy(gate_up_far.at[:, near], gate_up_ref.at[:, near], arrived.at[t]))
        copies.append(pltpu.make_async_copy(down_far, down_ref, arrived.at[tiles]))
        for copy in copies:
            copy.start()

    weights = []
    at = 0
    for block, (source, token) in zip(blocks, pieces):
        count = block.shape[0]
        rows[at : at + count, :] = block[...]
        at += count
        line = gates_ref[pl.ds(sources_ref[source], 1), :]
        column = jnp.broadcast_to(line, (8, line.shape[1])).T[:, :1]
        weights.append(column[token : token + count])
    weight = jnp.concatenate(weights)

    contract = (((1,), (1,)), ((), ()))
    taken = rows[...]
    for t in range(tiles):
        if load:
            copies[t].wait()
        near = slice(t * tile, (t + 1) * tile)
        gating = lax.dot_general(taken, gate_up_ref[0, near], contract, preferred_element_type=jnp.float32)
        lifted = lax.dot_general(taken, gate_up_ref[1, near], contract, preferred_element_type=jnp.float32)
        hidden[:, near] = (gating / (1.0 + jnp.exp(-gating)) * lifted).astype(jnp.bfloat16)
    if load:
        copies[tiles].wait()
    inner = hidden[...]
    keep = out_keep.shape[0]
    tile = 512 if width % 512 == 0 else width
    for low in range(0, width, tile):
        product = jnp.dot(inner, down_ref[:, low : low + tile], preferred_element_type=jnp.float32) * weight
        product = product.astype(jnp.bfloat16)
        out_keep[:, low : low + tile] = product[:keep]
        out_give[:, low : low + tile] = product[keep:]


def half_expert(places, gates, pieces, blocks, gate_up, down_proj, load=False):
    height = sum(block.shape[0] for block in blocks)
    units, width = down_proj.shape
    whole = pl.BlockSpec(memory_space=pltpu.VMEM)
    out = jax.ShapeDtypeStruct((height // 2, width), jnp.bfloat16)
    weights = [jax.ShapeDtypeStruct(array.shape, array.dtype) for array in (gate_up, down_proj)] if load else []
    scratch = [pltpu.VMEM((height, width), jnp.bfloat16), pltpu.VMEM((height, units), jnp.bfloat16)]
    if load:
        scratch.append(pltpu.SemaphoreType.DMA((units // 256 + 1 if units % 256 == 0 else 2,)))
    return pl.pallas_call(
        functools.partial(half_expert_kernel, tuple(pieces), load),
        out_shape=[out, out] + weights,
        in_specs=[pl.BlockSpec(memory_space=pltpu.SMEM)]
        + [whole] * (len(blocks) + 1)
        + [pl.BlockSpec(memory_space=pltpu.HBM) if load else whole] * 2,
        out_specs=[whole] * (2 + len(weights)),
        scratch_shapes=scratch,
        compiler_params=pltpu.CompilerParams(vmem_limit_bytes=(34 if load else 14) << 20),
        cost_estimate=pl.CostEstimate(
            flops=6 * height * units * width,
            bytes_accessed=6 * units * width + 4 * height * width,
            transcendentals=height * units,
        ),
    )(places, gates, *blocks, gate_up, down_proj)


def sum_kernel(*refs):
    *terms, out = refs
    out[...] = sum(term[...].astype(jnp.float32) for term in terms)


def summed(*terms):
    whole = pl.BlockSpec(memory_space=pltpu.VMEM)
    size = terms[0].size
    return pl.pallas_call(
        sum_kernel,
        out_shape=jax.ShapeDtypeStruct(terms[0].shape, jnp.float32),
        in_specs=[whole] * len(terms),
        out_specs=whole,
        compiler_params=pltpu.CompilerParams(vmem_limit_bytes=8 << 20),
        cost_estimate=pl.CostEstimate(flops=size * 20000, bytes_accessed=size * 100, transcendentals=0),
    )(*terms)


def by_tokens(tokens, expert_ids, route_gate, gate_up, down_proj):
    chips = lax.axis_size("blk") // 2
    order, far = snake(chips), chips // 2
    rows = tokens.shape[0]
    half = rows // 2
    chains = (0, 1)
    forth, back, across, cores = [], [], [], []
    for place in range(chips):
        for core in (0, 1):
            device = 2 * order[place] + core
            ahead, behind = order[(place + 1 - 2 * core) % chips], order[(place - 1 + 2 * core) % chips]
            forth.append((device, 2 * ahead + core))
            back.append((device, 2 * behind + core))
            across.append((device, 2 * behind + 1 - core))
            cores.append((device, device ^ 1))

    def send(value, pairs):
        return lax.ppermute(value, "blk", pairs)

    def total(*terms):
        return sum(term.astype(jnp.float32) for term in terms)

    def rounded(value):
        return value.astype(jnp.bfloat16)

    def after(value, *earlier):
        return lax.optimization_barrier((value, *earlier))[0]

    ring = [send(tokens, forth), send(tokens, across)]
    other = send(tokens, cores)

    places = lax.dynamic_index_in_dim(jnp.asarray(sources(chips)), lax.axis_index("blk"), 0, keepdims=False)
    chosen = jnp.arange(chips, dtype=jnp.int32)[:, None, None] == expert_ids.T[None]
    weight = jnp.sum(jnp.where(chosen, route_gate.T[None], 0.0), axis=1)
    gates = lax.all_to_all(jnp.repeat(weight, 2, axis=0), "blk", split_axis=0, concat_axis=0, tiled=True)
    gates = gates.reshape(-1, rows)
    ring[0] = after(ring[0], gates)

    near = None
    results = {}
    for step in range(1, far - 1):
        swapped = [send(block, cores) for block in ring]
        pieces = [(4 * step - 2 + i, 0) for i in range(4)]
        blocks = ring + swapped
        ring = [send(block, forth) for block in ring]
        if near is None:
            kept, given, *near = half_expert(places, gates, pieces, blocks, gate_up, down_proj, load=True)
        else:
            kept, given = half_expert(places, gates, pieces, blocks, *near)
        given = send(given, cores)
        for c in chains:
            results[step, c] = kept[c * rows : (c + 1) * rows], given[c * rows : (c + 1) * rows]
        ring[0] = after(ring[0], kept)

    first, second = slice(0, half), slice(half, rows)
    swapped = [send(block, cores) for block in ring]
    blocks = ring + swapped
    ring = [send(ring[0][first], forth), send(ring[1][second], forth)]
    for c in chains:
        pieces = [(4 * far - 6 + c, 0), (4 * far - 4 + c, 0)]
        mine, theirs = half_expert(places, gates, pieces, [blocks[c], blocks[2 + c]], *near)
        results[far - 1, c] = mine, send(theirs, cores)
        if c == 0:
            ring[0] = after(ring[0], mine)
            blocks[1] = after(blocks[1], ring[0])
    swapped = [send(block, cores) for block in ring]
    mine, theirs = results[far - 1, 0]
    earlier = rounded(total(after(mine, results[far - 1, 1][0])[second], theirs[second]))
    early = [send(earlier, back)]
    swapped[0] = after(swapped[0], earlier)
    base = 4 * far - 2
    pieces = [(base, 0), (base + 1, half), (base + 2, 0), (base + 3, half)]
    kept, given = half_expert(places, gates, pieces, ring + swapped, *near)
    given = send(given, cores)
    mine, theirs = results[far - 1, 1]
    earlier = rounded(total(after(mine, kept)[first], theirs[first]))
    early.append(send(earlier, back))

    late = []
    for part in (first, second):
        earlier = rounded(total(after(kept[part], earlier, early[0]), given[part]))
        late.append(send(earlier, back))
    sums = []
    for c in chains:
        mine, theirs = results[far - 1, c]
        part = (first, second)[c]
        earlier = rounded(total(after(mine[part], earlier, early[1]), theirs[part], late[c]))
        pair = [send(earlier, back), early[c]]
        sums.append(jnp.concatenate(pair if c == 0 else pair[::-1]))
    for step in range(far - 2, 1, -1):
        for c in chains:
            mine, theirs = results[step, c]
            earlier = rounded(total(after(mine, earlier), theirs, sums[c]))
            sums[c] = send(earlier, back)
    kept, given = half_expert(places, gates, [(0, 0), (1, 0)], [after(tokens, earlier), other], *near)
    given = send(given, cores)
    earlier = kept
    for c, pairs in zip(chains, (back, across)):
        mine, theirs = results[1, c]
        earlier = rounded(total(after(mine, earlier), theirs, sums[c]))
        sums[c] = send(earlier, pairs)
    return rounded(total(summed(kept, given, sums[0]), sums[1]))


def solution(mesh):
    placed = (
        P(("groups", "blk"), None),
        P(("groups", "blk"), None),
        P(("groups", "blk"), None),
        P(None, "blk", None),
        P("blk", None),
    )

    def per_device(tokens, expert_ids, route_gate, gate_up, down_proj):
        experts = mesh.shape["blk"] // 2
        body = by_tokens if experts <= 2 * expert_ids.shape[1] else by_slots
        return body(tokens, expert_ids, route_gate, gate_up, down_proj)

    return jax.shard_map(
        per_device,
        mesh=mesh,
        in_specs=placed,
        out_specs=P(("groups", "blk"), None),
        check_vma=False,
    )
```

```python
import functools

import jax
import jax.numpy as jnp
import numpy as np
from jax import lax
from jax.experimental import pallas as pl
from jax.experimental.pallas import tpu as pltpu
from jax.sharding import PartitionSpec as P


def expert_half(slot_block, gate_up, down_proj):
    contract = (((1,), (1,)), ((), ()))
    gating = lax.dot_general(slot_block, gate_up[0], contract, preferred_element_type=jnp.float32)
    lifted = lax.dot_general(slot_block, gate_up[1], contract, preferred_element_type=jnp.float32)
    hidden = (jax.nn.silu(gating) * lifted).astype(jnp.bfloat16)
    return jnp.dot(hidden, down_proj, preferred_element_type=jnp.float32).astype(jnp.bfloat16)


def by_slots(tokens, expert_ids, route_gate, gate_up, down_proj):
    tok_count, per_token = expert_ids.shape
    feature_width = tokens.shape[1]
    devices = lax.axis_size("blk")
    experts = devices // 2
    capacity = 3 * tok_count * per_token // devices
    placements = tok_count * per_token
    chosen_ids = expert_ids.reshape(placements)
    onehot = (chosen_ids[:, None] == jnp.arange(experts, dtype=jnp.int32)[None, :]).astype(
        jnp.int32
    )
    ranked = jnp.sum((jnp.cumsum(onehot, axis=0) - 1) * onehot, axis=1)
    slot_index = chosen_ids * capacity + ranked
    token_of = jnp.arange(placements, dtype=jnp.int32) // per_token
    slot_table = jnp.full((experts * capacity,), tok_count, jnp.int32).at[slot_index].set(token_of)
    outgoing = jnp.take(tokens, slot_table, axis=0, mode="fill", fill_value=0)
    outgoing = outgoing.reshape(experts, capacity, feature_width)
    doubled = jnp.repeat(outgoing, 2, axis=0)
    received = lax.all_to_all(doubled, "blk", split_axis=0, concat_axis=0, tiled=True)
    item_count = received.shape[1]
    partial_value = expert_half(received.reshape(-1, feature_width), gate_up, down_proj)
    partial_value = partial_value.reshape(devices, item_count, feature_width)
    returned_rows = lax.all_to_all(partial_value, "blk", split_axis=0, concat_axis=0, tiled=True)
    halves = returned_rows.reshape(experts, 2, capacity, feature_width).astype(jnp.float32)
    results = halves[:, 0] + halves[:, 1]
    flattened = results.reshape(experts * capacity, feature_width)
    picked = jnp.take(flattened, slot_index, axis=0)
    weighted = picked.reshape(tok_count, per_token, feature_width) * route_gate[:, :, None]
    return jnp.sum(weighted, axis=1).astype(jnp.bfloat16)


def snake(chips):
    return list(range(0, chips, 2)) + list(range(chips - 1, 0, -2))


def sources(chips):
    order = snake(chips)
    table = np.zeros((2 * chips, 2 + 2 * chips), np.int32)
    for place in range(chips):
        for core in (0, 1):
            turn = 1 - 2 * core
            row = [(0, core), (0, 1 - core)]
            for step in range(1, chips // 2 + 1):
                row += [(-step, core), (-step, 1 - core), (step, 1 - core), (step, core)]
            table[2 * order[place] + core] = [2 * order[(place + turn * d) % chips] + c for d, c in row]
    return table


def half_expert_kernel(pieces, load, split, sources_ref, gates_ref, *refs):
    blocks, refs = refs[: len(pieces)], refs[len(pieces) :]
    if load:
        (gate_up_far, down_far), refs = refs[:2], refs[2:]
        outs, (gate_up_ref, down_ref, rows, hidden, arrived) = refs[:split], refs[split:]
    else:
        (gate_up_ref, down_ref), outs, (rows, hidden) = refs[:2], refs[2:-2], refs[-2:]
    units, width = down_ref.shape
    tile = 256 if units % 256 == 0 else units
    tiles = units // tile
    copies = []
    if load:
        for t in range(tiles):
            near = pl.ds(t * tile, tile)
            copies.append(pltpu.make_async_copy(gate_up_far.at[:, near], gate_up_ref.at[:, near], arrived.at[t]))
        copies.append(pltpu.make_async_copy(down_far, down_ref, arrived.at[tiles]))
        for copy in copies:
            copy.start()

    weights = []
    at = 0
    for block, (source, token) in zip(blocks, pieces):
        count = block.shape[0]
        rows[at : at + count, :] = block[...]
        at += count
        line = gates_ref[pl.ds(sources_ref[source], 1), :]
        column = jnp.broadcast_to(line, (8, line.shape[1])).T[:, :1]
        weights.append(column[token : token + count])
    weight = jnp.concatenate(weights)

    contract = (((1,), (1,)), ((), ()))
    taken = rows[...]
    for t in range(tiles):
        if load:
            copies[t].wait()
        near = slice(t * tile, (t + 1) * tile)
        gating = lax.dot_general(taken, gate_up_ref[0, near], contract, preferred_element_type=jnp.float32)
        lifted = lax.dot_general(taken, gate_up_ref[1, near], contract, preferred_element_type=jnp.float32)
        hidden[:, near] = (gating / (1.0 + jnp.exp(-gating)) * lifted).astype(jnp.bfloat16)
    if load:
        copies[tiles].wait()
    inner = hidden[...]
    share = outs[0].shape[0]
    tile = 512 if width % 512 == 0 else width
    for low in range(0, width, tile):
        product = jnp.dot(inner, down_ref[:, low : low + tile], preferred_element_type=jnp.float32) * weight
        product = product.astype(jnp.bfloat16)
        for i, out in enumerate(outs):
            out[:, low : low + tile] = product[i * share : (i + 1) * share]


def half_expert(places, gates, pieces, blocks, gate_up, down_proj, load=False, cost=6, split=2):
    height = sum(block.shape[0] for block in blocks)
    units, width = down_proj.shape
    whole = pl.BlockSpec(memory_space=pltpu.VMEM)
    outs = [jax.ShapeDtypeStruct((height // split, width), jnp.bfloat16)] * split
    weights = [jax.ShapeDtypeStruct(array.shape, array.dtype) for array in (gate_up, down_proj)] if load else []
    scratch = [pltpu.VMEM((height, width), jnp.bfloat16), pltpu.VMEM((height, units), jnp.bfloat16)]
    if load:
        scratch.append(pltpu.SemaphoreType.DMA((units // 256 + 1 if units % 256 == 0 else 2,)))
    return pl.pallas_call(
        functools.partial(half_expert_kernel, tuple(pieces), load, split),
        out_shape=outs + weights,
        in_specs=[pl.BlockSpec(memory_space=pltpu.SMEM)]
        + [whole] * (len(blocks) + 1)
        + [pl.BlockSpec(memory_space=pltpu.HBM) if load else whole] * 2,
        out_specs=[whole] * (split + len(weights)),
        scratch_shapes=scratch,
        compiler_params=pltpu.CompilerParams(vmem_limit_bytes=(34 if load else 14) << 20),
        cost_estimate=pl.CostEstimate(
            flops=cost * height * units * width,
            bytes_accessed=cost * units * width,
            transcendentals=height * units,
        ),
    )(places, gates, *blocks, gate_up, down_proj)


def sum_kernel(*refs):
    *terms, out = refs
    out[...] = sum(term[...].astype(jnp.float32) for term in terms)


def summed(*terms):
    whole = pl.BlockSpec(memory_space=pltpu.VMEM)
    size = terms[0].size
    return pl.pallas_call(
        sum_kernel,
        out_shape=jax.ShapeDtypeStruct(terms[0].shape, jnp.float32),
        in_specs=[whole] * len(terms),
        out_specs=whole,
        compiler_params=pltpu.CompilerParams(vmem_limit_bytes=8 << 20),
        cost_estimate=pl.CostEstimate(flops=size * 20000, bytes_accessed=size * 100, transcendentals=0),
    )(*terms)


def by_tokens(tokens, expert_ids, route_gate, gate_up, down_proj):
    chips = lax.axis_size("blk") // 2
    order, far = snake(chips), chips // 2
    rows = tokens.shape[0]
    half = rows // 2
    chains = (0, 1)
    forth, back, across, cores = [], [], [], []
    for place in range(chips):
        for core in (0, 1):
            device = 2 * order[place] + core
            ahead, behind = order[(place + 1 - 2 * core) % chips], order[(place - 1 + 2 * core) % chips]
            forth.append((device, 2 * ahead + core))
            back.append((device, 2 * behind + core))
            across.append((device, 2 * behind + 1 - core))
            cores.append((device, device ^ 1))

    def send(value, pairs):
        return lax.ppermute(value, "blk", pairs)

    def total(*terms):
        return sum(term.astype(jnp.float32) for term in terms)

    def rounded(value):
        return value.astype(jnp.bfloat16)

    def after(value, *earlier):
        return lax.optimization_barrier((value, *earlier))[0]

    ring = [send(tokens, forth), send(tokens, across)]
    other = send(tokens, cores)

    places = lax.dynamic_index_in_dim(jnp.asarray(sources(chips)), lax.axis_index("blk"), 0, keepdims=False)
    chosen = jnp.arange(chips, dtype=jnp.int32)[:, None, None] == expert_ids.T[None]
    weight = jnp.sum(jnp.where(chosen, route_gate.T[None], 0.0), axis=1)
    gates = lax.all_to_all(jnp.repeat(weight, 2, axis=0), "blk", split_axis=0, concat_axis=0, tiled=True)
    gates = gates.reshape(-1, rows)

    results, near = {}, None
    earlier = ring[1]
    for step in range(1, far):
        swapped = [send(block, cores) for block in ring]
        blocks = ring
        if step < far - 1:
            ring = [send(block, forth) for block in ring]
        else:
            ring = [send(ring[0][:half], forth), send(ring[1][half:], forth)]
        for c in chains:
            pieces = [(4 * step - 2 + c, 0), (4 * step + c, 0)]
            inputs = [after(blocks[c], earlier), swapped[c]]
            if near is None:
                kept, given, *near = half_expert(places, gates, pieces, inputs, gate_up, down_proj, load=True)
            elif (step, c) != (far - 1, 1):
                kept, given = half_expert(places, gates, pieces, inputs, *near)
            else:
                last = pieces, [blocks[c], swapped[c]]
                break
            results[step, c] = kept, send(given, cores)
            ring[c] = earlier = after(ring[c], kept)

    base = 4 * far - 2
    pieces = [(base, 0), (base + 1, half)]
    (given,) = half_expert(places, gates, pieces, ring, *near, split=1)
    swapped = [send(block, cores) for block in ring]
    swapped[0] = after(swapped[0], given)
    given = send(given, cores)
    pieces = [(base + 2, 0), (base + 3, half)]
    (kept,) = half_expert(places, gates, pieces, swapped, *near, split=1)

    first, second = slice(0, half), slice(half, rows)
    late = []
    earlier = kept
    for part in (second, first):
        earlier = rounded(total(after(kept[part], earlier), given[part]))
        late.append(send(earlier, back))
    pieces, inputs = last
    inputs[0] = after(inputs[0], earlier)
    kept, given = half_expert(places, gates, pieces, inputs, *near, cost=1)
    results[far - 1, 1] = kept, send(given, cores)

    sums = []
    earlier = kept
    for c in chains:
        mine, theirs = results[far - 1, c]
        value = total(after(mine, earlier), theirs)
        if c == 0:
            value = jnp.concatenate([value[first], value[second] + total(late[c])])
        else:
            value = jnp.concatenate([value[first] + total(late[c]), value[second]])
        earlier = rounded(value)
        sums.append(send(earlier, back))
    for step in range(far - 2, 1, -1):
        for c in chains:
            mine, theirs = results[step, c]
            earlier = rounded(total(after(mine, earlier), theirs, sums[c]))
            sums[c] = send(earlier, back)
    kept, given = half_expert(places, gates, [(0, 0), (1, 0)], [after(tokens, earlier), other], *near)
    given = send(given, cores)
    earlier = kept
    for c, pairs in zip(chains, (back, across)):
        mine, theirs = results[1, c]
        earlier = rounded(total(after(mine, earlier), theirs, sums[c]))
        sums[c] = send(earlier, pairs)
    return rounded(total(summed(kept, given, sums[0]), sums[1]))


def solution(mesh):
    placed = (
        P(("groups", "blk"), None),
        P(("groups", "blk"), None),
        P(("groups", "blk"), None),
        P(None, "blk", None),
        P("blk", None),
    )

    def per_device(tokens, expert_ids, route_gate, gate_up, down_proj):
        experts = mesh.shape["blk"] // 2
        body = by_tokens if experts <= 2 * expert_ids.shape[1] else by_slots
        return body(tokens, expert_ids, route_gate, gate_up, down_proj)

    return jax.shard_map(
        per_device,
        mesh=mesh,
        in_specs=placed,
        out_specs=P(("groups", "blk"), None),
        check_vma=False,
    )
```

```python
import functools

import jax
import jax.numpy as jnp
import numpy as np
from jax import lax
from jax.experimental import pallas as pl
from jax.experimental.pallas import tpu as pltpu
from jax.sharding import PartitionSpec as P


def expert_half(slot_block, gate_up, down_proj):
    contract = (((1,), (1,)), ((), ()))
    gating = lax.dot_general(slot_block, gate_up[0], contract, preferred_element_type=jnp.float32)
    lifted = lax.dot_general(slot_block, gate_up[1], contract, preferred_element_type=jnp.float32)
    hidden = (jax.nn.silu(gating) * lifted).astype(jnp.bfloat16)
    return jnp.dot(hidden, down_proj, preferred_element_type=jnp.float32).astype(jnp.bfloat16)


def by_slots(tokens, expert_ids, route_gate, gate_up, down_proj):
    tok_count, per_token = expert_ids.shape
    feature_width = tokens.shape[1]
    devices = lax.axis_size("blk")
    experts = devices // 2
    capacity = 3 * tok_count * per_token // devices
    placements = tok_count * per_token
    chosen_ids = expert_ids.reshape(placements)
    onehot = (chosen_ids[:, None] == jnp.arange(experts, dtype=jnp.int32)[None, :]).astype(
        jnp.int32
    )
    ranked = jnp.sum((jnp.cumsum(onehot, axis=0) - 1) * onehot, axis=1)
    slot_index = chosen_ids * capacity + ranked
    token_of = jnp.arange(placements, dtype=jnp.int32) // per_token
    slot_table = jnp.full((experts * capacity,), tok_count, jnp.int32).at[slot_index].set(token_of)
    outgoing = jnp.take(tokens, slot_table, axis=0, mode="fill", fill_value=0)
    outgoing = outgoing.reshape(experts, capacity, feature_width)
    doubled = jnp.repeat(outgoing, 2, axis=0)
    received = lax.all_to_all(doubled, "blk", split_axis=0, concat_axis=0, tiled=True)
    item_count = received.shape[1]
    partial_value = expert_half(received.reshape(-1, feature_width), gate_up, down_proj)
    partial_value = partial_value.reshape(devices, item_count, feature_width)
    returned_rows = lax.all_to_all(partial_value, "blk", split_axis=0, concat_axis=0, tiled=True)
    halves = returned_rows.reshape(experts, 2, capacity, feature_width).astype(jnp.float32)
    results = halves[:, 0] + halves[:, 1]
    flattened = results.reshape(experts * capacity, feature_width)
    picked = jnp.take(flattened, slot_index, axis=0)
    weighted = picked.reshape(tok_count, per_token, feature_width) * route_gate[:, :, None]
    return jnp.sum(weighted, axis=1).astype(jnp.bfloat16)


def snake(chips):
    return list(range(0, chips, 2)) + list(range(chips - 1, 0, -2))


def half_expert_kernel(pieces, gate_count, load, split, mine_ref, *refs):
    gates, refs = refs[:gate_count], refs[gate_count:]
    blocks, refs = refs[: len(pieces)], refs[len(pieces) :]
    if load:
        (gate_up_far, down_far), refs = refs[:2], refs[2:]
        outs, (gate_up_ref, down_ref, rows, hidden, arrived) = refs[:split], refs[split:]
    else:
        (gate_up_ref, down_ref), outs, (rows, hidden) = refs[:2], refs[2:-2], refs[-2:]
    units, width = down_ref.shape
    tile = 256 if units % 256 == 0 else units
    tiles = units // tile
    copies = []
    if load:
        for t in range(tiles):
            near = pl.ds(t * tile, tile)
            copies.append(pltpu.make_async_copy(gate_up_far.at[:, near], gate_up_ref.at[:, near], arrived.at[t]))
        copies.append(pltpu.make_async_copy(down_far, down_ref, arrived.at[tiles]))
        for copy in copies:
            copy.start()

    weights = []
    at = 0
    for block, (place, kind, token) in zip(blocks, pieces):
        count = block.shape[0]
        rows[at : at + count, :] = block[...]
        at += count
        experts = gates[place].shape[0] // 2
        line = gates[place][pl.ds(mine_ref[0] + kind * experts, 1), :]
        column = jnp.broadcast_to(line, (8, line.shape[1])).T[:, :1]
        weights.append(column[token : token + count])
    weight = jnp.concatenate(weights)

    contract = (((1,), (1,)), ((), ()))
    taken = rows[...]
    for t in range(tiles):
        if load:
            copies[t].wait()
        near = slice(t * tile, (t + 1) * tile)
        gating = lax.dot_general(taken, gate_up_ref[0, near], contract, preferred_element_type=jnp.float32)
        lifted = lax.dot_general(taken, gate_up_ref[1, near], contract, preferred_element_type=jnp.float32)
        hidden[:, near] = (gating / (1.0 + jnp.exp(-gating)) * lifted).astype(jnp.bfloat16)
    if load:
        copies[tiles].wait()
    inner = hidden[...]
    share = outs[0].shape[0]
    tile = 512 if width % 512 == 0 else width
    for low in range(0, width, tile):
        product = jnp.dot(inner, down_ref[:, low : low + tile], preferred_element_type=jnp.float32) * weight
        product = product.astype(jnp.bfloat16)
        for i, out in enumerate(outs):
            out[:, low : low + tile] = product[i * share : (i + 1) * share]


def half_expert(mine, gates, pieces, blocks, gate_up, down_proj, load=False, cost=2, split=2):
    height = sum(block.shape[0] for block in blocks)
    units, width = down_proj.shape
    whole = pl.BlockSpec(memory_space=pltpu.VMEM)
    outs = [jax.ShapeDtypeStruct((height // split, width), jnp.bfloat16)] * split
    weights = [jax.ShapeDtypeStruct(array.shape, array.dtype) for array in (gate_up, down_proj)] if load else []
    scratch = [pltpu.VMEM((height, width), jnp.bfloat16), pltpu.VMEM((height, units), jnp.bfloat16)]
    if load:
        scratch.append(pltpu.SemaphoreType.DMA((units // 256 + 1 if units % 256 == 0 else 2,)))
    return pl.pallas_call(
        functools.partial(half_expert_kernel, tuple(pieces), len(gates), load, split),
        out_shape=outs + weights,
        in_specs=[pl.BlockSpec(memory_space=pltpu.SMEM)]
        + [whole] * (len(gates) + len(blocks))
        + [pl.BlockSpec(memory_space=pltpu.HBM) if load else whole] * 2,
        out_specs=[whole] * (split + len(weights)),
        scratch_shapes=scratch,
        compiler_params=pltpu.CompilerParams(vmem_limit_bytes=(34 if load else 14) << 20),
        cost_estimate=pl.CostEstimate(
            flops=cost * height * units * width,
            bytes_accessed=cost * units * width,
            transcendentals=height * units,
        ),
    )(mine, *gates, *blocks, gate_up, down_proj)


def sum_kernel(*refs):
    *terms, out = refs
    out[...] = sum(term[...].astype(jnp.float32) for term in terms)


def summed(*terms):
    whole = pl.BlockSpec(memory_space=pltpu.VMEM)
    size = terms[0].size
    return pl.pallas_call(
        sum_kernel,
        out_shape=jax.ShapeDtypeStruct(terms[0].shape, jnp.float32),
        in_specs=[whole] * len(terms),
        out_specs=whole,
        compiler_params=pltpu.CompilerParams(vmem_limit_bytes=8 << 20),
        cost_estimate=pl.CostEstimate(flops=size * 20000, bytes_accessed=size * 100, transcendentals=0),
    )(*terms)


def by_tokens(tokens, expert_ids, route_gate, gate_up, down_proj):
    chips = lax.axis_size("blk") // 2
    order, far = snake(chips), chips // 2
    rows = tokens.shape[0]
    half = rows // 2
    chains = (0, 1)

    def moved(steps, swap=False):
        pairs = []
        for place in range(chips):
            for core in (0, 1):
                target = order[(place + steps * (1 - 2 * core)) % chips]
                pairs.append((2 * order[place] + core, 2 * target + (1 - core if swap else core)))
        return pairs

    forth, back, across, cores = moved(1), moved(-1), moved(-1, True), moved(0, True)

    def send(value, pairs):
        return lax.ppermute(value, "blk", pairs)

    def total(*terms):
        return sum(term.astype(jnp.float32) for term in terms)

    def rounded(value):
        return value.astype(jnp.bfloat16)

    def after(value, *earlier):
        return lax.optimization_barrier((value, *earlier))[0]

    ring = [send(tokens, forth), send(tokens, across)]
    other = send(tokens, cores)

    expert = (lax.axis_index("blk") // 2).astype(jnp.int32).reshape(1)
    chosen = jnp.arange(chips, dtype=jnp.int32)[:, None, None] == expert_ids.T[None]
    weight = jnp.sum(jnp.where(chosen, route_gate.T[None], 0.0), axis=1)
    weight = jnp.concatenate([weight, send(weight, cores)])
    gates = [[weight]]
    for step in range(1, far):
        gates.append([send(weight, moved(step)), send(weight, moved(-step))])
    gates.append([send(weight, moved(far))])
    ring[0] = after(ring[0], ring[1], *sum(gates, []))

    def expert_rows(step, c, inputs, **options):
        pieces = [(0, c, 0), (1, 1 - c, 0)]
        return half_expert(expert, gates[step], pieces, inputs, *near, **options)

    results, near = {}, (gate_up, down_proj)
    earlier = ring[1]
    for step in range(1, far):
        swapped = [send(block, cores) for block in ring]
        blocks = list(ring)
        if step < far - 1:
            ring = [send(block, forth) for block in ring]
        else:
            ring[0] = send(ring[0][:half], forth)
            ring[1] = send(after(ring[1], ring[0])[half:], forth)
        for c in chains:
            if c == 1 and step == 1:
                delayed = [blocks[c], swapped[c]]
                continue
            inputs = [after(blocks[c], earlier), swapped[c]]
            if step == 1:
                kept, given, *near = expert_rows(step, c, inputs, load=True)
            else:
                kept, given = expert_rows(step, c, inputs)
            results[step, c] = kept, send(given, cores)
            ring[c] = earlier = after(ring[c], kept)
        if step == 1:
            earlier = ring[1]

    (given,) = half_expert(expert, gates[far], [(0, 0, 0), (0, 1, half)], ring, *near, split=1)
    swapped = [send(block, cores) for block in ring]
    swapped[0] = after(swapped[0], given)
    given = send(given, cores)
    (kept,) = half_expert(expert, gates[far], [(0, 1, 0), (0, 0, half)], swapped, *near, split=1)

    first, second = slice(0, half), slice(half, rows)
    late = []
    earlier = kept
    for part in (second, first):
        earlier = rounded(total(after(kept[part], earlier), given[part]))
        late.append(send(earlier, back))

    sums = []
    for c in chains:
        mine, theirs = results[far - 1, c]
        value = total(after(mine, earlier), theirs)
        if c == 0:
            value = jnp.concatenate([value[first], value[second] + total(late[c])])
        else:
            value = jnp.concatenate([value[first] + total(late[c]), value[second]])
        earlier = rounded(value)
        sums.append(send(earlier, back))
    kept, given = expert_rows(1, 1, [after(delayed[0], earlier), delayed[1]])
    results[1, 1] = kept, send(given, cores)
    earlier = kept
    for step in range(far - 2, 1, -1):
        for c in chains:
            mine, theirs = results[step, c]
            earlier = rounded(total(after(mine, earlier), theirs, sums[c]))
            sums[c] = send(earlier, back)
    kept, given = half_expert(expert, gates[0], [(0, 0, 0), (0, 1, 0)], [after(tokens, earlier), other], *near)
    given = send(given, cores)
    earlier = kept
    for c, pairs in zip(chains, (back, across)):
        mine, theirs = results[1, c]
        earlier = rounded(total(after(mine, earlier), theirs, sums[c]))
        sums[c] = send(earlier, pairs)
    return rounded(total(summed(kept, given, sums[0]), sums[1]))


def solution(mesh):
    placed = (
        P(("groups", "blk"), None),
        P(("groups", "blk"), None),
        P(("groups", "blk"), None),
        P(None, "blk", None),
        P("blk", None),
    )

    def per_device(tokens, expert_ids, route_gate, gate_up, down_proj):
        experts = mesh.shape["blk"] // 2
        body = by_tokens if experts <= 2 * expert_ids.shape[1] else by_slots
        return body(tokens, expert_ids, route_gate, gate_up, down_proj)

    return jax.shard_map(
        per_device,
        mesh=mesh,
        in_specs=placed,
        out_specs=P(("groups", "blk"), None),
        check_vma=False,
    )
```

```python
import functools

import jax
import jax.numpy as jnp
import numpy as np
from jax import lax
from jax.experimental import pallas as pl
from jax.experimental.pallas import tpu as pltpu
from jax.sharding import PartitionSpec as P


def expert_half(slot_block, gate_up, down_proj):
    contract = (((1,), (1,)), ((), ()))
    gating = lax.dot_general(slot_block, gate_up[0], contract, preferred_element_type=jnp.float32)
    lifted = lax.dot_general(slot_block, gate_up[1], contract, preferred_element_type=jnp.float32)
    hidden = (jax.nn.silu(gating) * lifted).astype(jnp.bfloat16)
    return jnp.dot(hidden, down_proj, preferred_element_type=jnp.float32).astype(jnp.bfloat16)


def by_slots(tokens, expert_ids, route_gate, gate_up, down_proj):
    tok_count, per_token = expert_ids.shape
    feature_width = tokens.shape[1]
    devices = lax.axis_size("blk")
    experts = devices // 2
    capacity = 3 * tok_count * per_token // devices
    placements = tok_count * per_token
    chosen_ids = expert_ids.reshape(placements)
    onehot = (chosen_ids[:, None] == jnp.arange(experts, dtype=jnp.int32)[None, :]).astype(
        jnp.int32
    )
    ranked = jnp.sum((jnp.cumsum(onehot, axis=0) - 1) * onehot, axis=1)
    slot_index = chosen_ids * capacity + ranked
    token_of = jnp.arange(placements, dtype=jnp.int32) // per_token
    slot_table = jnp.full((experts * capacity,), tok_count, jnp.int32).at[slot_index].set(token_of)
    outgoing = jnp.take(tokens, slot_table, axis=0, mode="fill", fill_value=0)
    outgoing = outgoing.reshape(experts, capacity, feature_width)
    doubled = jnp.repeat(outgoing, 2, axis=0)
    received = lax.all_to_all(doubled, "blk", split_axis=0, concat_axis=0, tiled=True)
    item_count = received.shape[1]
    partial_value = expert_half(received.reshape(-1, feature_width), gate_up, down_proj)
    partial_value = partial_value.reshape(devices, item_count, feature_width)
    returned_rows = lax.all_to_all(partial_value, "blk", split_axis=0, concat_axis=0, tiled=True)
    halves = returned_rows.reshape(experts, 2, capacity, feature_width).astype(jnp.float32)
    results = halves[:, 0] + halves[:, 1]
    flattened = results.reshape(experts * capacity, feature_width)
    picked = jnp.take(flattened, slot_index, axis=0)
    weighted = picked.reshape(tok_count, per_token, feature_width) * route_gate[:, :, None]
    return jnp.sum(weighted, axis=1).astype(jnp.bfloat16)


def snake(chips):
    return list(range(0, chips, 2)) + list(range(chips - 1, 0, -2))


def sources(chips):
    order = snake(chips)
    table = np.zeros((2 * chips, 2 + 2 * chips), np.int32)
    for place in range(chips):
        for core in (0, 1):
            turn = 1 - 2 * core
            row = [(0, core), (0, 1 - core)]
            for step in range(1, chips // 2 + 1):
                row += [(-step, core), (-step, 1 - core), (step, 1 - core), (step, core)]
            table[2 * order[place] + core] = [2 * order[(place + turn * d) % chips] + c for d, c in row]
    return table


def half_expert_kernel(pieces, load, split, *refs):
    blocks, refs = refs[: len(pieces)], refs[len(pieces) :]
    if load:
        (places, gates, gate_up_far, down_far), refs = refs[:4], refs[4:]
        outs, (gate_up_ref, down_ref, columns, rows, hidden, lines, arrived) = refs[:split], refs[split:]
    else:
        (gate_up_ref, down_ref, columns), outs, (rows, hidden) = refs[:3], refs[3:-2], refs[-2:]
    units, width = down_ref.shape
    tile = 256 if units % 256 == 0 else units
    tiles = units // tile
    copies = []
    if load:
        for t in range(tiles):
            near = pl.ds(t * tile, tile)
            copies.append(pltpu.make_async_copy(gate_up_far.at[:, near], gate_up_ref.at[:, near], arrived.at[t]))
        copies.append(pltpu.make_async_copy(down_far, down_ref, arrived.at[tiles]))
        for copy in copies:
            copy.start()
        lines[...] = jnp.zeros_like(lines)
        for i in range(places.shape[0]):
            lines[i : i + 1, :] = gates[pl.ds(places[i], 1), :]
        columns[...] = lines[...].T

    at = 0
    weights = []
    for block, (column, token) in zip(blocks, pieces):
        count = block.shape[0]
        rows[at : at + count, :] = block[...]
        at += count
        weights.append(columns[token : token + count, column : column + 1])
    weight = jnp.concatenate(weights)

    contract = (((1,), (1,)), ((), ()))
    taken = rows[...]
    for t in range(tiles):
        if load:
            copies[t].wait()
        near = slice(t * tile, (t + 1) * tile)
        gating = lax.dot_general(taken, gate_up_ref[0, near], contract, preferred_element_type=jnp.float32)
        lifted = lax.dot_general(taken, gate_up_ref[1, near], contract, preferred_element_type=jnp.float32)
        hidden[:, near] = (gating / (1.0 + jnp.exp(-gating)) * lifted).astype(jnp.bfloat16)
    if load:
        copies[tiles].wait()
    inner = hidden[...]
    share = outs[0].shape[0]
    tile = 512 if width % 512 == 0 else width
    for low in range(0, width, tile):
        product = jnp.dot(inner, down_ref[:, low : low + tile], preferred_element_type=jnp.float32) * weight
        product = product.astype(jnp.bfloat16)
        for i, out in enumerate(outs):
            out[:, low : low + tile] = product[i * share : (i + 1) * share]


def half_expert(pieces, blocks, weights, load=False, cost=2, split=2):
    height = sum(block.shape[0] for block in blocks)
    gate_up, down_proj = weights[2:] if load else weights[:2]
    units, width = down_proj.shape
    whole = pl.BlockSpec(memory_space=pltpu.VMEM)
    far = pl.BlockSpec(memory_space=pltpu.HBM)
    outs = [jax.ShapeDtypeStruct((height // split, width), jnp.bfloat16)] * split
    scratch = [pltpu.VMEM((height, width), jnp.bfloat16), pltpu.VMEM((height, units), jnp.bfloat16)]
    specs = [whole] * 3
    if load:
        tokens = weights[1].shape[1]
        outs += [jax.ShapeDtypeStruct(array.shape, array.dtype) for array in (gate_up, down_proj)]
        outs.append(jax.ShapeDtypeStruct((tokens, 128), jnp.float32))
        scratch.append(pltpu.VMEM((128, tokens), jnp.float32))
        scratch.append(pltpu.SemaphoreType.DMA((units // 256 + 1 if units % 256 == 0 else 2,)))
        specs = [pl.BlockSpec(memory_space=pltpu.SMEM), whole, far, far]
    return pl.pallas_call(
        functools.partial(half_expert_kernel, tuple(pieces), load, split),
        out_shape=outs,
        in_specs=[whole] * len(blocks) + specs,
        out_specs=[whole] * len(outs),
        scratch_shapes=scratch,
        compiler_params=pltpu.CompilerParams(vmem_limit_bytes=(34 if load else 14) << 20),
        cost_estimate=pl.CostEstimate(
            flops=int(cost * height * units * width),
            bytes_accessed=int(cost * units * width),
            transcendentals=0,
        ),
    )(*blocks, *weights)


def sum_kernel(*refs):
    *terms, out = refs
    out[...] = sum(term[...].astype(jnp.float32) for term in terms)


def summed(*terms):
    whole = pl.BlockSpec(memory_space=pltpu.VMEM)
    size = terms[0].size
    return pl.pallas_call(
        sum_kernel,
        out_shape=jax.ShapeDtypeStruct(terms[0].shape, jnp.float32),
        in_specs=[whole] * len(terms),
        out_specs=whole,
        compiler_params=pltpu.CompilerParams(vmem_limit_bytes=8 << 20),
        cost_estimate=pl.CostEstimate(flops=size * 20000, bytes_accessed=size * 100, transcendentals=0),
    )(*terms)


def by_tokens(tokens, expert_ids, route_gate, gate_up, down_proj):
    chips = lax.axis_size("blk") // 2
    order, far = snake(chips), chips // 2
    rows = tokens.shape[0]
    half = rows // 2
    chains = (0, 1)

    def moved(steps, swap=False):
        pairs = []
        for place in range(chips):
            for core in (0, 1):
                target = order[(place + steps * (1 - 2 * core)) % chips]
                pairs.append((2 * order[place] + core, 2 * target + (1 - core if swap else core)))
        return pairs

    forth, back, across, cores = moved(1), moved(-1), moved(-1, True), moved(0, True)

    def send(value, pairs):
        return lax.ppermute(value, "blk", pairs)

    def total(*terms):
        return sum(term.astype(jnp.float32) for term in terms)

    def rounded(value):
        return value.astype(jnp.bfloat16)

    def after(value, *earlier):
        return lax.optimization_barrier((value, *earlier))[0]

    ring = [send(tokens, forth), send(tokens, across)]

    places = lax.dynamic_index_in_dim(jnp.asarray(sources(chips)), lax.axis_index("blk"), 0, keepdims=False)
    chosen = jnp.arange(chips, dtype=jnp.int32)[:, None, None] == expert_ids.T[None]
    weight = jnp.sum(jnp.where(chosen, route_gate.T[None], 0.0), axis=1)
    gates = lax.all_to_all(jnp.repeat(weight, 2, axis=0), "blk", split_axis=0, concat_axis=0, tiled=True)
    gates = gates.reshape(-1, rows)
    ring[1] = after(ring[1], gates)

    def swapped_columns(step, c):
        return [(4 * step - 2 + c, 0), (4 * step + c, 0)]

    results = {}
    near, delayed = None, None
    for step in range(1, far):
        swapped = [send(block, cores) for block in ring[: 1 if step == 1 else 2]]
        blocks = ring
        if step < far - 1:
            ring = [send(block, forth) for block in ring]
        else:
            ring = [send(ring[0][:half], forth), send(ring[1][half:], forth)]
        if step == 1:
            load = [places, gates, gate_up, down_proj]
            kept, given, *near = half_expert(swapped_columns(1, 0), [blocks[0], swapped[0]], load, load=True)
            results[1, 0] = kept, send(given, cores)
            delayed = blocks[1]
        else:
            pieces = [(4 * step - 2 + i, 0) for i in range(4)]
            kept, given = half_expert(pieces, blocks + swapped, near)
            given = send(given, cores)
            for c in chains:
                results[step, c] = kept[c * rows : (c + 1) * rows], given[c * rows : (c + 1) * rows]
        ring[0] = after(ring[0], kept)
        if step == far - 1:
            ring[1] = after(ring[1], kept)

    base = 4 * far - 2
    (given,) = half_expert([(base, 0), (base + 1, half)], ring, near, split=1)
    swapped = [send(block, cores) for block in ring]
    swapped[0] = after(swapped[0], given)
    given = send(given, cores)
    (kept,) = half_expert([(base + 2, 0), (base + 3, half)], swapped, near, split=1)

    first, second = slice(0, half), slice(half, rows)
    late = []
    earlier = kept
    for part in (second, first):
        earlier = rounded(total(after(kept[part], earlier), given[part]))
        late.append(send(earlier, back))

    late_value, sums = earlier, []
    for c in chains:
        mine, theirs = results[far - 1, c]
        value = total(after(mine, earlier), theirs)
        if c == 0:
            value = jnp.concatenate([value[first], value[second] + total(late[c])])
        else:
            value = jnp.concatenate([value[first] + total(late[c]), value[second]])
        earlier = rounded(value)
        sums.append(send(earlier, back))
    swapped = send(after(delayed, late_value), cores)
    kept, given = half_expert(swapped_columns(1, 1), [after(delayed, earlier), swapped], near)
    results[1, 1] = kept, send(given, cores)
    other = send(after(tokens, earlier), cores)
    earlier = kept
    for step in range(far - 2, 1, -1):
        for c in chains:
            mine, theirs = results[step, c]
            earlier = rounded(total(after(mine, earlier), theirs, sums[c]))
            sums[c] = send(earlier, back)
    kept, given = half_expert([(0, 0), (1, 0)], [after(tokens, earlier), other], near)
    given = send(given, cores)
    earlier = kept
    for c, pairs in zip(chains, (back, across)):
        mine, theirs = results[1, c]
        earlier = rounded(total(after(mine, earlier), theirs, sums[c]))
        sums[c] = send(earlier, pairs)
    return rounded(total(summed(kept, given, sums[0]), sums[1]))


def solution(mesh):
    placed = (
        P(("groups", "blk"), None),
        P(("groups", "blk"), None),
        P(("groups", "blk"), None),
        P(None, "blk", None),
        P("blk", None),
    )

    def per_device(tokens, expert_ids, route_gate, gate_up, down_proj):
        experts = mesh.shape["blk"] // 2
        body = by_tokens if experts <= 2 * expert_ids.shape[1] else by_slots
        return body(tokens, expert_ids, route_gate, gate_up, down_proj)

    return jax.shard_map(
        per_device,
        mesh=mesh,
        in_specs=placed,
        out_specs=P(("groups", "blk"), None),
        check_vma=False,
    )
```

```python
import functools

import jax
import jax.numpy as jnp
import numpy as np
from jax import lax
from jax.experimental import pallas as pl
from jax.experimental.pallas import tpu as pltpu
from jax.sharding import PartitionSpec as P

GATE_ROWS, LANES = 8, 128


def expert_half(slot_block, gate_up, down_proj):
    contract = (((1,), (1,)), ((), ()))
    gating = lax.dot_general(slot_block, gate_up[0], contract, preferred_element_type=jnp.float32)
    lifted = lax.dot_general(slot_block, gate_up[1], contract, preferred_element_type=jnp.float32)
    hidden = (jax.nn.silu(gating) * lifted).astype(jnp.bfloat16)
    return jnp.dot(hidden, down_proj, preferred_element_type=jnp.float32).astype(jnp.bfloat16)


def by_slots(tokens, expert_ids, route_gate, gate_up, down_proj):
    tok_count, per_token = expert_ids.shape
    feature_width = tokens.shape[1]
    devices = lax.axis_size("blk")
    experts = devices // 2
    capacity = 3 * tok_count * per_token // devices
    placements = tok_count * per_token
    chosen_ids = expert_ids.reshape(placements)
    onehot = (chosen_ids[:, None] == jnp.arange(experts, dtype=jnp.int32)[None, :]).astype(
        jnp.int32
    )
    ranked = jnp.sum((jnp.cumsum(onehot, axis=0) - 1) * onehot, axis=1)
    slot_index = chosen_ids * capacity + ranked
    token_of = jnp.arange(placements, dtype=jnp.int32) // per_token
    slot_table = jnp.full((experts * capacity,), tok_count, jnp.int32).at[slot_index].set(token_of)
    outgoing = jnp.take(tokens, slot_table, axis=0, mode="fill", fill_value=0)
    outgoing = outgoing.reshape(experts, capacity, feature_width)
    doubled = jnp.repeat(outgoing, 2, axis=0)
    received = lax.all_to_all(doubled, "blk", split_axis=0, concat_axis=0, tiled=True)
    item_count = received.shape[1]
    partial_value = expert_half(received.reshape(-1, feature_width), gate_up, down_proj)
    partial_value = partial_value.reshape(devices, item_count, feature_width)
    returned_rows = lax.all_to_all(partial_value, "blk", split_axis=0, concat_axis=0, tiled=True)
    halves = returned_rows.reshape(experts, 2, capacity, feature_width).astype(jnp.float32)
    results = halves[:, 0] + halves[:, 1]
    flattened = results.reshape(experts * capacity, feature_width)
    picked = jnp.take(flattened, slot_index, axis=0)
    weighted = picked.reshape(tok_count, per_token, feature_width) * route_gate[:, :, None]
    return jnp.sum(weighted, axis=1).astype(jnp.bfloat16)


def snake(chips):
    return list(range(0, chips, 2)) + list(range(chips - 1, 0, -2))


def half_expert_kernel(first_tokens, load, split, expert_ref, *refs):
    blocks, refs = refs[: len(first_tokens)], refs[len(first_tokens) :]
    if load:
        (gate_up_far, down_far), refs = refs[:2], refs[2:]
        outs, (gate_up_ref, down_ref, rows, hidden, arrived) = refs[:split], refs[split:]
    else:
        (gate_up_ref, down_ref), outs, (rows, hidden) = refs[:2], refs[2:-2], refs[-2:]
    units, width = down_ref.shape
    tile = 256 if units % 256 == 0 else units
    tiles = units // tile
    copies = []
    if load:
        for t in range(tiles):
            near = pl.ds(t * tile, tile)
            copies.append(pltpu.make_async_copy(gate_up_far.at[:, near], gate_up_ref.at[:, near], arrived.at[t]))
        copies.append(pltpu.make_async_copy(down_far, down_ref, arrived.at[tiles]))
        for copy in copies:
            copy.start()

    at = 0
    weights = []
    for block, token in zip(blocks, first_tokens):
        count = block.shape[0] - GATE_ROWS
        rows[at : at + count, :] = block[:count, :]
        at += count
        high, low = (block[count:, i * LANES : (i + 1) * LANES].astype(jnp.float32) for i in (0, 1))
        wanted = lax.broadcasted_iota(jnp.int32, high.shape, 0) == expert_ref[0]
        line = jnp.sum(jnp.where(wanted, high + low, 0.0), axis=0, keepdims=True)
        weights.append(jnp.broadcast_to(line, high.shape).T[token : token + count, :1])
    weight = jnp.concatenate(weights)

    contract = (((1,), (1,)), ((), ()))
    taken = rows[...]
    for t in range(tiles):
        if load:
            copies[t].wait()
        near = slice(t * tile, (t + 1) * tile)
        gating = lax.dot_general(taken, gate_up_ref[0, near], contract, preferred_element_type=jnp.float32)
        lifted = lax.dot_general(taken, gate_up_ref[1, near], contract, preferred_element_type=jnp.float32)
        hidden[:, near] = (gating / (1.0 + jnp.exp(-gating)) * lifted).astype(jnp.bfloat16)
    if load:
        copies[tiles].wait()
    inner = hidden[...]
    share = outs[0].shape[0]
    tile = 512 if width % 512 == 0 else width
    for low in range(0, width, tile):
        product = jnp.dot(inner, down_ref[:, low : low + tile], preferred_element_type=jnp.float32) * weight
        product = product.astype(jnp.bfloat16)
        for i, out in enumerate(outs):
            out[:, low : low + tile] = product[i * share : (i + 1) * share]


def half_expert(first_tokens, blocks, expert, weights, load=False, cost=2, split=2):
    height = sum(block.shape[0] - GATE_ROWS for block in blocks)
    units, width = weights[1].shape
    whole = pl.BlockSpec(memory_space=pltpu.VMEM)
    far = pl.BlockSpec(memory_space=pltpu.HBM)
    outs = [jax.ShapeDtypeStruct((height // split, width), jnp.bfloat16)] * split
    scratch = [pltpu.VMEM((height, width), jnp.bfloat16), pltpu.VMEM((height, units), jnp.bfloat16)]
    if load:
        outs += [jax.ShapeDtypeStruct(array.shape, array.dtype) for array in weights]
        scratch.append(pltpu.SemaphoreType.DMA((units // 256 + 1 if units % 256 == 0 else 2,)))
    return pl.pallas_call(
        functools.partial(half_expert_kernel, tuple(first_tokens), load, split),
        out_shape=outs,
        in_specs=[pl.BlockSpec(memory_space=pltpu.SMEM)] + [whole] * len(blocks) + [far if load else whole] * 2,
        out_specs=[whole] * len(outs),
        scratch_shapes=scratch,
        compiler_params=pltpu.CompilerParams(vmem_limit_bytes=(34 if load else 14) << 20),
        cost_estimate=pl.CostEstimate(
            flops=int(cost * height * units * width),
            bytes_accessed=int(cost * units * width),
            transcendentals=0,
        ),
    )(expert, *blocks, *weights)


def sum_kernel(*refs):
    *terms, out = refs
    out[...] = sum(term[...].astype(jnp.float32) for term in terms)


def summed(*terms):
    whole = pl.BlockSpec(memory_space=pltpu.VMEM)
    size = terms[0].size
    return pl.pallas_call(
        sum_kernel,
        out_shape=jax.ShapeDtypeStruct(terms[0].shape, jnp.float32),
        in_specs=[whole] * len(terms),
        out_specs=whole,
        compiler_params=pltpu.CompilerParams(vmem_limit_bytes=8 << 20),
        cost_estimate=pl.CostEstimate(flops=size * 20000, bytes_accessed=size * 100, transcendentals=0),
    )(*terms)


def by_tokens(tokens, expert_ids, route_gate, gate_up, down_proj):
    chips = lax.axis_size("blk") // 2
    order, far = snake(chips), chips // 2
    rows = tokens.shape[0]
    half = rows // 2
    chains = (0, 1)

    def moved(steps, swap=False):
        pairs = []
        for place in range(chips):
            for core in (0, 1):
                target = order[(place + steps * (1 - 2 * core)) % chips]
                pairs.append((2 * order[place] + core, 2 * target + (1 - core if swap else core)))
        return pairs

    forth, back, across, cores = moved(1), moved(-1), moved(-1, True), moved(0, True)

    def send(value, pairs):
        return lax.ppermute(value, "blk", pairs)

    def total(*terms):
        return sum(term.astype(jnp.float32) for term in terms)

    def rounded(value):
        return value.astype(jnp.bfloat16)

    def after(value, *earlier):
        return lax.optimization_barrier((value, *earlier))[0]

    expert = jnp.right_shift(lax.axis_index("blk"), 1).astype(jnp.int32).reshape(1)
    chosen = jnp.arange(GATE_ROWS, dtype=jnp.int32)[:, None, None] == expert_ids.T[None]
    weight = jnp.sum(jnp.where(chosen, route_gate.T[None], 0.0), axis=1)
    high = lax.reduce_precision(weight, 8, 7)
    gates = jnp.concatenate([high, weight - high], axis=1).astype(jnp.bfloat16)
    packed = jnp.concatenate([tokens, jnp.pad(gates, ((0, 0), (0, tokens.shape[1] - 2 * LANES)))])

    ring = [send(packed, forth), send(packed, across)]
    results = {}
    near, delayed = None, None
    for step in range(1, far):
        swapped = [send(block, cores) for block in ring[: 1 if step == 1 else 2]]
        blocks = ring
        if step < far - 1:
            ring = [send(block, forth) for block in ring]
        else:
            ring = [send(jnp.concatenate([ring[0][:half], ring[0][rows:]]), forth), send(ring[1][half:], forth)]
        if step == 1:
            delayed = blocks[1]
            kept, given, *near = half_expert([0, 0], [blocks[0], swapped[0]], expert, [gate_up, down_proj], load=True)
            results[1, 0] = kept, send(given, cores)
        else:
            kept, given = half_expert([0] * 4, blocks + swapped, expert, near)
            given = send(given, cores)
            for c in chains:
                results[step, c] = kept[c * rows : (c + 1) * rows], given[c * rows : (c + 1) * rows]
        ring[0] = after(ring[0], kept)
        if step == far - 1:
            ring[1] = after(ring[1], kept)

    (given,) = half_expert([0, half], ring, expert, near, split=1)
    swapped = [send(block, cores) for block in ring]
    swapped[0] = after(swapped[0], given)
    given = send(given, cores)
    (kept,) = half_expert([0, half], swapped, expert, near, split=1)

    first, second = slice(0, half), slice(half, rows)
    late = []
    earlier = kept
    for part in (second, first):
        earlier = rounded(total(after(kept[part], earlier), given[part]))
        late.append(send(earlier, back))

    late_value, sums = earlier, []
    for c in chains:
        mine, theirs = results[far - 1, c]
        value = total(after(mine, earlier), theirs)
        if c == 0:
            value = jnp.concatenate([value[first], value[second] + total(late[c])])
        else:
            value = jnp.concatenate([value[first] + total(late[c]), value[second]])
        earlier = rounded(value)
        sums.append(send(earlier, back))
    swapped = send(after(delayed, late_value), cores)
    kept, given = half_expert([0, 0], [after(delayed, earlier), swapped], expert, near)
    results[1, 1] = kept, send(given, cores)
    other = send(after(packed, earlier), cores)
    earlier = kept
    for step in range(far - 2, 1, -1):
        for c in chains:
            mine, theirs = results[step, c]
            earlier = rounded(total(after(mine, earlier), theirs, sums[c]))
            sums[c] = send(earlier, back)
    kept, given = half_expert([0, 0], [after(packed, earlier), other], expert, near)
    given = send(given, cores)
    earlier = kept
    for c, pairs in zip(chains, (back, across)):
        mine, theirs = results[1, c]
        earlier = rounded(total(after(mine, earlier), theirs, sums[c]))
        sums[c] = send(earlier, pairs)
    return rounded(total(summed(kept, given, sums[0]), sums[1]))


def solution(mesh):
    placed = (
        P(("groups", "blk"), None),
        P(("groups", "blk"), None),
        P(("groups", "blk"), None),
        P(None, "blk", None),
        P("blk", None),
    )

    def per_device(tokens, expert_ids, route_gate, gate_up, down_proj):
        experts = mesh.shape["blk"] // 2
        dense = experts <= min(GATE_ROWS, 2 * expert_ids.shape[1]) and tokens.shape[0] == LANES
        body = by_tokens if dense else by_slots
        return body(tokens, expert_ids, route_gate, gate_up, down_proj)

    return jax.shard_map(
        per_device,
        mesh=mesh,
        in_specs=placed,
        out_specs=P(("groups", "blk"), None),
        check_vma=False,
    )
```

```python
import functools

import jax
import jax.numpy as jnp
import numpy as np
from jax import lax
from jax.experimental import pallas as pl
from jax.experimental.pallas import tpu as pltpu
from jax.sharding import PartitionSpec as P

GATE_ROWS, LANES = 8, 128


def expert_half(slot_block, gate_up, down_proj):
    contract = (((1,), (1,)), ((), ()))
    gating = lax.dot_general(slot_block, gate_up[0], contract, preferred_element_type=jnp.float32)
    lifted = lax.dot_general(slot_block, gate_up[1], contract, preferred_element_type=jnp.float32)
    hidden = (jax.nn.silu(gating) * lifted).astype(jnp.bfloat16)
    return jnp.dot(hidden, down_proj, preferred_element_type=jnp.float32).astype(jnp.bfloat16)


def by_slots(tokens, expert_ids, route_gate, gate_up, down_proj):
    tok_count, per_token = expert_ids.shape
    feature_width = tokens.shape[1]
    devices = lax.axis_size("blk")
    experts = devices // 2
    capacity = 3 * tok_count * per_token // devices
    placements = tok_count * per_token
    chosen_ids = expert_ids.reshape(placements)
    onehot = (chosen_ids[:, None] == jnp.arange(experts, dtype=jnp.int32)[None, :]).astype(
        jnp.int32
    )
    ranked = jnp.sum((jnp.cumsum(onehot, axis=0) - 1) * onehot, axis=1)
    slot_index = chosen_ids * capacity + ranked
    token_of = jnp.arange(placements, dtype=jnp.int32) // per_token
    slot_table = jnp.full((experts * capacity,), tok_count, jnp.int32).at[slot_index].set(token_of)
    outgoing = jnp.take(tokens, slot_table, axis=0, mode="fill", fill_value=0)
    outgoing = outgoing.reshape(experts, capacity, feature_width)
    doubled = jnp.repeat(outgoing, 2, axis=0)
    received = lax.all_to_all(doubled, "blk", split_axis=0, concat_axis=0, tiled=True)
    item_count = received.shape[1]
    partial_value = expert_half(received.reshape(-1, feature_width), gate_up, down_proj)
    partial_value = partial_value.reshape(devices, item_count, feature_width)
    returned_rows = lax.all_to_all(partial_value, "blk", split_axis=0, concat_axis=0, tiled=True)
    halves = returned_rows.reshape(experts, 2, capacity, feature_width).astype(jnp.float32)
    results = halves[:, 0] + halves[:, 1]
    flattened = results.reshape(experts * capacity, feature_width)
    picked = jnp.take(flattened, slot_index, axis=0)
    weighted = picked.reshape(tok_count, per_token, feature_width) * route_gate[:, :, None]
    return jnp.sum(weighted, axis=1).astype(jnp.bfloat16)


def snake(chips):
    return list(range(0, chips, 2)) + list(range(chips - 1, 0, -2))


def half_expert_kernel(first_tokens, load, split, expert_ref, *refs):
    blocks, refs = refs[: len(first_tokens)], refs[len(first_tokens) :]
    if load:
        (gate_up_far, down_far), refs = refs[:2], refs[2:]
        outs, (gate_up_ref, down_ref, rows, hidden, arrived) = refs[:split], refs[split:]
    else:
        (gate_up_ref, down_ref), outs, (rows, hidden) = refs[:2], refs[2:-2], refs[-2:]
    units, width = down_ref.shape
    tile = 256 if units % 256 == 0 else units
    tiles = units // tile
    copies = []
    if load:
        for t in range(tiles):
            near = pl.ds(t * tile, tile)
            copies.append(pltpu.make_async_copy(gate_up_far.at[:, near], gate_up_ref.at[:, near], arrived.at[t]))
        copies.append(pltpu.make_async_copy(down_far, down_ref, arrived.at[tiles]))
        for copy in copies:
            copy.start()

    at = 0
    weights = []
    for block, token in zip(blocks, first_tokens):
        count = block.shape[0] - GATE_ROWS
        rows[at : at + count, :] = block[:count, :]
        at += count
        high, low = (block[count:, i * LANES : (i + 1) * LANES].astype(jnp.float32) for i in (0, 1))
        wanted = lax.broadcasted_iota(jnp.int32, high.shape, 0) == expert_ref[0]
        line = jnp.sum(jnp.where(wanted, high + low, 0.0), axis=0, keepdims=True)
        weights.append(jnp.broadcast_to(line, high.shape).T[token : token + count, :1])
    weight = jnp.concatenate(weights)

    contract = (((1,), (1,)), ((), ()))
    taken = rows[...]
    for t in range(tiles):
        if load:
            copies[t].wait()
        near = slice(t * tile, (t + 1) * tile)
        gating = lax.dot_general(taken, gate_up_ref[0, near], contract, preferred_element_type=jnp.float32)
        lifted = lax.dot_general(taken, gate_up_ref[1, near], contract, preferred_element_type=jnp.float32)
        hidden[:, near] = (gating / (1.0 + jnp.exp(-gating)) * lifted).astype(jnp.bfloat16)
    if load:
        copies[tiles].wait()
    inner = hidden[...]
    share = outs[0].shape[0]
    tile = 512 if width % 512 == 0 else width
    for low in range(0, width, tile):
        product = jnp.dot(inner, down_ref[:, low : low + tile], preferred_element_type=jnp.float32) * weight
        product = product.astype(jnp.bfloat16)
        for i, out in enumerate(outs):
            out[:, low : low + tile] = product[i * share : (i + 1) * share]


def half_expert(first_tokens, blocks, expert, weights, load=False, cost=2, split=2):
    height = sum(block.shape[0] - GATE_ROWS for block in blocks)
    units, width = weights[1].shape
    whole = pl.BlockSpec(memory_space=pltpu.VMEM)
    far = pl.BlockSpec(memory_space=pltpu.HBM)
    outs = [jax.ShapeDtypeStruct((height // split, width), jnp.bfloat16)] * split
    scratch = [pltpu.VMEM((height, width), jnp.bfloat16), pltpu.VMEM((height, units), jnp.bfloat16)]
    if load:
        outs += [jax.ShapeDtypeStruct(array.shape, array.dtype) for array in weights]
        scratch.append(pltpu.SemaphoreType.DMA((units // 256 + 1 if units % 256 == 0 else 2,)))
    return pl.pallas_call(
        functools.partial(half_expert_kernel, tuple(first_tokens), load, split),
        out_shape=outs,
        in_specs=[pl.BlockSpec(memory_space=pltpu.SMEM)] + [whole] * len(blocks) + [far if load else whole] * 2,
        out_specs=[whole] * len(outs),
        scratch_shapes=scratch,
        compiler_params=pltpu.CompilerParams(vmem_limit_bytes=(34 if load else 14) << 20),
        cost_estimate=pl.CostEstimate(
            flops=int(cost * height * units * width),
            bytes_accessed=int(cost * units * width),
            transcendentals=0,
        ),
    )(expert, *blocks, *weights)


def sum_kernel(*refs):
    *terms, out = refs
    out[...] = sum(term[...].astype(jnp.float32) for term in terms)


def summed(*terms):
    whole = pl.BlockSpec(memory_space=pltpu.VMEM)
    size = terms[0].size
    return pl.pallas_call(
        sum_kernel,
        out_shape=jax.ShapeDtypeStruct(terms[0].shape, jnp.float32),
        in_specs=[whole] * len(terms),
        out_specs=whole,
        compiler_params=pltpu.CompilerParams(vmem_limit_bytes=8 << 20),
        cost_estimate=pl.CostEstimate(flops=size * 20000, bytes_accessed=size * 100, transcendentals=0),
    )(*terms)


def by_tokens(tokens, expert_ids, route_gate, gate_up, down_proj):
    chips = lax.axis_size("blk") // 2
    order, far = snake(chips), chips // 2
    rows = tokens.shape[0]
    half = rows // 2
    chains = (0, 1)

    def moved(steps, swap=False):
        pairs = []
        for place in range(chips):
            for core in (0, 1):
                target = order[(place + steps * (1 - 2 * core)) % chips]
                pairs.append((2 * order[place] + core, 2 * target + (1 - core if swap else core)))
        return pairs

    forth, back, across, cores = moved(1), moved(-1), moved(-1, True), moved(0, True)

    def send(value, pairs, name):
        with jax.named_scope(name):
            return lax.ppermute(value, "blk", pairs)

    def total(*terms):
        return sum(term.astype(jnp.float32) for term in terms)

    def rounded(value):
        return value.astype(jnp.bfloat16)

    def after(value, *earlier):
        return lax.optimization_barrier((value, *earlier))[0]

    expert = jnp.right_shift(lax.axis_index("blk"), 1).astype(jnp.int32).reshape(1)
    chosen = jnp.arange(GATE_ROWS, dtype=jnp.int32)[:, None, None] == expert_ids.T[None]
    weight = jnp.sum(jnp.where(chosen, route_gate.T[None], 0.0), axis=1)
    high = lax.reduce_precision(weight, 8, 7)
    gates = jnp.concatenate([high, weight - high], axis=1).astype(jnp.bfloat16)
    packed = jnp.concatenate([tokens, jnp.pad(gates, ((0, 0), (0, tokens.shape[1] - 2 * LANES)))])

    ring = [send(packed, forth, "ring_1_0"), send(packed, across, "ring_1_1")]

    def expert_rows(step, c, inputs, **options):
        with jax.named_scope(f"expert_{step}_{c}"):
            kept, given = half_expert([0, 0], inputs, expert, near, **options)
        results[step, c] = kept, given
        if step == far - 1 or (step, c) == (1, 1):
            give(step, c)
        return kept

    def give(step, c, *earlier):
        kept, given = results[step, c]
        results[step, c] = kept, send(after(given, *earlier) if earlier else given, cores, f"give_{step}_{c}")

    results = {}
    with jax.named_scope("expert_0"):
        own, given, *near = half_expert([0, 0], [packed, send(packed, cores, "swap_0")], expert, [gate_up, down_proj], load=True)
    results[0, 0] = own, given
    ring[0] = after(ring[0], own)
    delayed = None
    earlier = ring[1]
    for step in range(1, far):
        swapped = [send(block, cores, f"swap_{step}_{c}") for c, block in enumerate(ring[: 1 if step == 1 else 2])]
        blocks = list(ring)
        if step < far - 1:
            ring = [send(block, forth, f"ring_{step + 1}_{c}") for c, block in enumerate(ring)]
        else:
            ring[0] = send(jnp.concatenate([ring[0][:half], ring[0][rows:]]), forth, f"ring_{far}_0")
            ring[1] = send(ring[1][half:], forth, f"ring_{far}_1")
        for c in chains:
            if (step, c) == (1, 1):
                delayed = blocks[1]
                earlier = ring[1]
                continue
            if (step, c) == (far - 1, 1):
                last = blocks[1], swapped[1]
                continue
            kept = expert_rows(step, c, [after(blocks[c], earlier), swapped[c]])
            ring[c] = after(ring[c], kept)
            earlier = ring[c]

    with jax.named_scope("expert_far_ring"):
        (given,) = half_expert([0, half], ring, expert, near, split=1)
    swapped = [send(block, cores, f"swap_{far}_{c}") for c, block in enumerate(ring)]
    swapped[0] = after(swapped[0], given)
    given = send(given, cores, "give_far")
    with jax.named_scope("expert_far_swapped"):
        (kept,) = half_expert([0, half], swapped, expert, near, split=1)

    first, second = slice(0, half), slice(half, rows)
    late = []
    earlier = kept
    for c, part in enumerate((second, first)):
        earlier = rounded(total(after(kept[part], earlier), given[part]))
        late.append(send(earlier, back, f"back_{far}_{c}"))
    earlier = expert_rows(far - 1, 1, [after(last[0], earlier), last[1]], cost=0.2)
    late_value, sums = earlier, []
    for step in range(far - 2, 1, -1):
        for c in chains:
            give(step, c, late_value)
    for c in chains:
        mine, theirs = results[far - 1, c]
        value = total(after(mine, earlier), theirs)
        if c == 0:
            value = jnp.concatenate([value[first], value[second] + total(late[c])])
        else:
            value = jnp.concatenate([value[first] + total(late[c]), value[second]])
        earlier = rounded(value)
        sums.append(send(earlier, back, f"back_{far - 1}_{c}"))
    swapped = send(after(delayed, late_value), cores, "swap_1_1")
    give(1, 0, earlier)
    give(0, 0, earlier)
    earlier = expert_rows(1, 1, [after(delayed, earlier), swapped])
    for step in range(far - 2, 1, -1):
        for c in chains:
            mine, theirs = results[step, c]
            earlier = rounded(total(after(mine, earlier), theirs, sums[c]))
            sums[c] = send(earlier, back, f"back_{step}_{c}")
    for c, pairs in zip(chains, (back, across)):
        mine, theirs = results[1, c]
        earlier = rounded(total(after(mine, earlier), theirs, sums[c]))
        sums[c] = send(earlier, pairs, f"back_1_{c}")
    return rounded(total(summed(*results[0, 0], sums[0]), sums[1]))


def solution(mesh):
    placed = (
        P(("groups", "blk"), None),
        P(("groups", "blk"), None),
        P(("groups", "blk"), None),
        P(None, "blk", None),
        P("blk", None),
    )

    def per_device(tokens, expert_ids, route_gate, gate_up, down_proj):
        experts = mesh.shape["blk"] // 2
        dense = experts <= min(GATE_ROWS, 2 * expert_ids.shape[1]) and tokens.shape[0] == LANES
        body = by_tokens if dense else by_slots
        return body(tokens, expert_ids, route_gate, gate_up, down_proj)

    return jax.shard_map(
        per_device,
        mesh=mesh,
        in_specs=placed,
        out_specs=P(("groups", "blk"), None),
        check_vma=False,
    )
```

```python
import functools

import jax
import jax.numpy as jnp
import numpy as np
from jax import lax
from jax.experimental import pallas as pl
from jax.experimental.pallas import tpu as pltpu
from jax.sharding import PartitionSpec as P

GATE_ROWS, LANES = 8, 128


def expert_half(slot_block, gate_up, down_proj):
    contract = (((1,), (1,)), ((), ()))
    gating = lax.dot_general(slot_block, gate_up[0], contract, preferred_element_type=jnp.float32)
    lifted = lax.dot_general(slot_block, gate_up[1], contract, preferred_element_type=jnp.float32)
    hidden = (jax.nn.silu(gating) * lifted).astype(jnp.bfloat16)
    return jnp.dot(hidden, down_proj, preferred_element_type=jnp.float32).astype(jnp.bfloat16)


def by_slots(tokens, expert_ids, route_gate, gate_up, down_proj):
    tok_count, per_token = expert_ids.shape
    feature_width = tokens.shape[1]
    devices = lax.axis_size("blk")
    experts = devices // 2
    capacity = 3 * tok_count * per_token // devices
    placements = tok_count * per_token
    chosen_ids = expert_ids.reshape(placements)
    onehot = (chosen_ids[:, None] == jnp.arange(experts, dtype=jnp.int32)[None, :]).astype(
        jnp.int32
    )
    ranked = jnp.sum((jnp.cumsum(onehot, axis=0) - 1) * onehot, axis=1)
    slot_index = chosen_ids * capacity + ranked
    token_of = jnp.arange(placements, dtype=jnp.int32) // per_token
    slot_table = jnp.full((experts * capacity,), tok_count, jnp.int32).at[slot_index].set(token_of)
    outgoing = jnp.take(tokens, slot_table, axis=0, mode="fill", fill_value=0)
    outgoing = outgoing.reshape(experts, capacity, feature_width)
    doubled = jnp.repeat(outgoing, 2, axis=0)
    received = lax.all_to_all(doubled, "blk", split_axis=0, concat_axis=0, tiled=True)
    item_count = received.shape[1]
    partial_value = expert_half(received.reshape(-1, feature_width), gate_up, down_proj)
    partial_value = partial_value.reshape(devices, item_count, feature_width)
    returned_rows = lax.all_to_all(partial_value, "blk", split_axis=0, concat_axis=0, tiled=True)
    halves = returned_rows.reshape(experts, 2, capacity, feature_width).astype(jnp.float32)
    results = halves[:, 0] + halves[:, 1]
    flattened = results.reshape(experts * capacity, feature_width)
    picked = jnp.take(flattened, slot_index, axis=0)
    weighted = picked.reshape(tok_count, per_token, feature_width) * route_gate[:, :, None]
    return jnp.sum(weighted, axis=1).astype(jnp.bfloat16)


def snake(chips):
    return list(range(0, chips, 2)) + list(range(chips - 1, 0, -2))


def half_expert_kernel(first_tokens, load, split, expert_ref, *refs):
    blocks, refs = refs[: len(first_tokens)], refs[len(first_tokens) :]
    if load:
        (gate_up_far, down_far), refs = refs[:2], refs[2:]
        outs, (gate_up_ref, down_ref, rows, hidden, arrived) = refs[:split], refs[split:]
    else:
        (gate_up_ref, down_ref), outs, (rows, hidden) = refs[:2], refs[2:-2], refs[-2:]
    units, width = down_ref.shape
    tile = 256 if units % 256 == 0 else units
    tiles = units // tile
    copies = []
    if load:
        for t in range(tiles):
            near = pl.ds(t * tile, tile)
            copies.append(pltpu.make_async_copy(gate_up_far.at[:, near], gate_up_ref.at[:, near], arrived.at[t]))
        copies.append(pltpu.make_async_copy(down_far, down_ref, arrived.at[tiles]))
        for copy in copies:
            copy.start()

    at = 0
    weights = []
    for block, token in zip(blocks, first_tokens):
        count = block.shape[0] - GATE_ROWS
        rows[at : at + count, :] = block[:count, :]
        at += count
        high, low = (block[count:, i * LANES : (i + 1) * LANES].astype(jnp.float32) for i in (0, 1))
        wanted = lax.broadcasted_iota(jnp.int32, high.shape, 0) == expert_ref[0]
        line = jnp.sum(jnp.where(wanted, high + low, 0.0), axis=0, keepdims=True)
        weights.append(jnp.broadcast_to(line, high.shape).T[token : token + count, :1])
    weight = jnp.concatenate(weights)

    contract = (((1,), (1,)), ((), ()))
    taken = rows[...]
    for t in range(tiles):
        if load:
            copies[t].wait()
        near = slice(t * tile, (t + 1) * tile)
        gating = lax.dot_general(taken, gate_up_ref[0, near], contract, preferred_element_type=jnp.float32)
        lifted = lax.dot_general(taken, gate_up_ref[1, near], contract, preferred_element_type=jnp.float32)
        hidden[:, near] = (gating / (1.0 + jnp.exp(-gating)) * lifted).astype(jnp.bfloat16)
    if load:
        copies[tiles].wait()
    inner = hidden[...]
    share = outs[0].shape[0]
    tile = 512 if width % 512 == 0 else width
    for low in range(0, width, tile):
        product = jnp.dot(inner, down_ref[:, low : low + tile], preferred_element_type=jnp.float32) * weight
        product = product.astype(jnp.bfloat16)
        for i, out in enumerate(outs):
            out[:, low : low + tile] = product[i * share : (i + 1) * share]


def half_expert(first_tokens, blocks, expert, weights, load=False, cost=2, split=2):
    height = sum(block.shape[0] - GATE_ROWS for block in blocks)
    units, width = weights[1].shape
    whole = pl.BlockSpec(memory_space=pltpu.VMEM)
    far = pl.BlockSpec(memory_space=pltpu.HBM)
    outs = [jax.ShapeDtypeStruct((height // split, width), jnp.bfloat16)] * split
    scratch = [pltpu.VMEM((height, width), jnp.bfloat16), pltpu.VMEM((height, units), jnp.bfloat16)]
    if load:
        outs += [jax.ShapeDtypeStruct(array.shape, array.dtype) for array in weights]
        scratch.append(pltpu.SemaphoreType.DMA((units // 256 + 1 if units % 256 == 0 else 2,)))
    return pl.pallas_call(
        functools.partial(half_expert_kernel, tuple(first_tokens), load, split),
        out_shape=outs,
        in_specs=[pl.BlockSpec(memory_space=pltpu.SMEM)] + [whole] * len(blocks) + [far if load else whole] * 2,
        out_specs=[whole] * len(outs),
        scratch_shapes=scratch,
        compiler_params=pltpu.CompilerParams(vmem_limit_bytes=(34 if load else 14) << 20),
        cost_estimate=pl.CostEstimate(
            flops=int(cost * height * units * width),
            bytes_accessed=int(cost * units * width),
            transcendentals=0,
        ),
    )(expert, *blocks, *weights)


def sum_kernel(low, *refs):
    *terms, part, out = refs
    value = sum(term[...].astype(jnp.float32) for term in terms)
    out[...] = value.astype(out.dtype)
    near = slice(low, low + part.shape[0])
    out[near, :] = (value[near] + part[...].astype(jnp.float32)).astype(out.dtype)


def summed(*terms, low=0, dtype=jnp.bfloat16, cost=1):
    whole = pl.BlockSpec(memory_space=pltpu.VMEM)
    size = terms[0].size
    return pl.pallas_call(
        functools.partial(sum_kernel, low),
        out_shape=jax.ShapeDtypeStruct(terms[0].shape, dtype),
        in_specs=[whole] * len(terms),
        out_specs=whole,
        compiler_params=pltpu.CompilerParams(vmem_limit_bytes=8 << 20),
        cost_estimate=pl.CostEstimate(flops=size * cost, bytes_accessed=size, transcendentals=0),
    )(*terms)


def by_tokens(tokens, expert_ids, route_gate, gate_up, down_proj):
    chips = lax.axis_size("blk") // 2
    order, far = snake(chips), chips // 2
    rows = tokens.shape[0]
    half = rows // 2
    chains = (0, 1)

    def moved(steps, swap=False):
        pairs = []
        for place in range(chips):
            for core in (0, 1):
                target = order[(place + steps * (1 - 2 * core)) % chips]
                pairs.append((2 * order[place] + core, 2 * target + (1 - core if swap else core)))
        return pairs

    forth, back, across, cores = moved(1), moved(-1), moved(-1, True), moved(0, True)

    def send(value, pairs, name):
        with jax.named_scope(name):
            return lax.ppermute(value, "blk", pairs)

    def total(*terms):
        return sum(term.astype(jnp.float32) for term in terms)

    def rounded(value):
        return value.astype(jnp.bfloat16)

    def after(value, *earlier):
        return lax.optimization_barrier((value, *earlier))[0]

    expert = jnp.right_shift(lax.axis_index("blk"), 1).astype(jnp.int32).reshape(1)
    chosen = jnp.arange(GATE_ROWS, dtype=jnp.int32)[:, None, None] == expert_ids.T[None]
    weight = jnp.sum(jnp.where(chosen, route_gate.T[None], 0.0), axis=1)
    high = lax.reduce_precision(weight, 8, 7)
    gates = jnp.concatenate([high, weight - high], axis=1).astype(jnp.bfloat16)
    packed = jnp.concatenate([tokens, jnp.pad(gates, ((0, 0), (0, tokens.shape[1] - 2 * LANES)))])

    other = send(packed, cores, "swap_0")
    ring = [send(packed, forth, "ring_1_0"), send(other, forth, "ring_1_1")]

    def expert_rows(step, c, inputs, **options):
        with jax.named_scope(f"expert_{step}_{c}"):
            kept, given = half_expert([0, 0], inputs, expert, near, **options)
        results[step, c] = kept, given
        if step == far - 1 or (step, c) == (1, 1):
            give(step, c)
        return kept

    def give(step, c, *earlier):
        kept, given = results[step, c]
        results[step, c] = kept, send(after(given, *earlier) if earlier else given, cores, f"give_{step}_{c}")

    results = {}
    with jax.named_scope("expert_0"):
        own, given, *near = half_expert([0, 0], [packed, other], expert, [gate_up, down_proj], load=True)
    results[0, 0] = own, given
    ring[0] = after(ring[0], own)
    delayed = None
    earlier = ring[1]
    for step in range(1, far):
        swapped = [send(block, cores, f"swap_{step}_{c}") for c, block in enumerate(ring[: 1 if step == 1 else 2])]
        blocks = list(ring)
        if step < far - 1:
            ring = [send(block, forth, f"ring_{step + 1}_{c}") for c, block in enumerate(ring)]
        else:
            ring[0] = send(jnp.concatenate([ring[0][:half], ring[0][rows:]]), forth, f"ring_{far}_0")
            ring[1] = send(ring[1][half:], forth, f"ring_{far}_1")
        for c in chains:
            if (step, c) == (1, 1):
                delayed = blocks[1]
                earlier = ring[1]
                continue
            if (step, c) == (far - 1, 1):
                last = blocks[1], swapped[1]
                continue
            kept = expert_rows(step, c, [after(blocks[c], earlier), swapped[c]])
            ring[c] = after(ring[c], kept)
            earlier = ring[c]

    with jax.named_scope("expert_far_ring"):
        (given,) = half_expert([0, half], ring, expert, near, split=1)
    swapped = [send(block, cores, f"swap_{far}_{c}") for c, block in enumerate(ring)]
    swapped[0] = after(swapped[0], given)
    given = send(given, cores, "give_far")
    with jax.named_scope("expert_far_swapped"):
        (kept,) = half_expert([0, half], swapped, expert, near, split=1)

    first, second = slice(0, half), slice(half, rows)
    late = []
    earlier = kept
    for c, part in enumerate((second, first)):
        earlier = rounded(total(after(kept[part], earlier), given[part]))
        late.append(send(earlier, back, f"back_{far}_{c}"))
    earlier = expert_rows(far - 1, 1, [after(last[0], earlier), last[1]], cost=0.2)
    sums = []
    for c in chains:
        mine, theirs = results[far - 1, c]
        value = total(after(mine, earlier), theirs)
        if c == 0:
            value = jnp.concatenate([value[first], value[second] + total(late[c])])
        else:
            value = jnp.concatenate([value[first] + total(late[c]), value[second]])
        earlier = rounded(value)
        sums.append(send(earlier, back, f"back_{far - 1}_{c}"))
        if c == 0:
            swapped = send(after(delayed, earlier), cores, "swap_1_1")
            for step in range(far - 2, 1, -1):
                for c2 in chains:
                    give(step, c2, earlier)
    give(1, 0, earlier)
    give(0, 0, earlier)
    earlier = expert_rows(1, 1, [after(delayed, earlier), swapped])
    for step in range(far - 2, 1, -1):
        for c in chains:
            mine, theirs = results[step, c]
            earlier = rounded(total(after(mine, earlier), theirs, sums[c]))
            sums[c] = send(earlier, back, f"back_{step}_{c}")
    for c, pairs in zip(chains, (back, across)):
        mine, theirs = results[1, c]
        earlier = rounded(total(after(mine, earlier), theirs, sums[c]))
        sums[c] = send(earlier, pairs, f"back_1_{c}")
    return rounded(total(summed(*results[0, 0], sums[0], dtype=jnp.float32, cost=20000), sums[1]))


def solution(mesh):
    placed = (
        P(("groups", "blk"), None),
        P(("groups", "blk"), None),
        P(("groups", "blk"), None),
        P(None, "blk", None),
        P("blk", None),
    )

    def per_device(tokens, expert_ids, route_gate, gate_up, down_proj):
        experts = mesh.shape["blk"] // 2
        dense = experts <= min(GATE_ROWS, 2 * expert_ids.shape[1]) and tokens.shape[0] == LANES
        body = by_tokens if dense else by_slots
        return body(tokens, expert_ids, route_gate, gate_up, down_proj)

    return jax.shard_map(
        per_device,
        mesh=mesh,
        in_specs=placed,
        out_specs=P(("groups", "blk"), None),
        check_vma=False,
    )
```

```python
import functools

import jax
import jax.numpy as jnp
import numpy as np
from jax import lax
from jax.experimental import pallas as pl
from jax.experimental.pallas import tpu as pltpu
from jax.sharding import PartitionSpec as P

GATE_ROWS, LANES = 8, 128


def expert_half(slot_block, gate_up, down_proj):
    contract = (((1,), (1,)), ((), ()))
    gating = lax.dot_general(slot_block, gate_up[0], contract, preferred_element_type=jnp.float32)
    lifted = lax.dot_general(slot_block, gate_up[1], contract, preferred_element_type=jnp.float32)
    hidden = (jax.nn.silu(gating) * lifted).astype(jnp.bfloat16)
    return jnp.dot(hidden, down_proj, preferred_element_type=jnp.float32).astype(jnp.bfloat16)


def by_slots(tokens, expert_ids, route_gate, gate_up, down_proj):
    tok_count, per_token = expert_ids.shape
    feature_width = tokens.shape[1]
    devices = lax.axis_size("blk")
    experts = devices // 2
    capacity = 3 * tok_count * per_token // devices
    placements = tok_count * per_token
    chosen_ids = expert_ids.reshape(placements)
    onehot = (chosen_ids[:, None] == jnp.arange(experts, dtype=jnp.int32)[None, :]).astype(
        jnp.int32
    )
    ranked = jnp.sum((jnp.cumsum(onehot, axis=0) - 1) * onehot, axis=1)
    slot_index = chosen_ids * capacity + ranked
    token_of = jnp.arange(placements, dtype=jnp.int32) // per_token
    slot_table = jnp.full((experts * capacity,), tok_count, jnp.int32).at[slot_index].set(token_of)
    outgoing = jnp.take(tokens, slot_table, axis=0, mode="fill", fill_value=0)
    outgoing = outgoing.reshape(experts, capacity, feature_width)
    doubled = jnp.repeat(outgoing, 2, axis=0)
    received = lax.all_to_all(doubled, "blk", split_axis=0, concat_axis=0, tiled=True)
    item_count = received.shape[1]
    partial_value = expert_half(received.reshape(-1, feature_width), gate_up, down_proj)
    partial_value = partial_value.reshape(devices, item_count, feature_width)
    returned_rows = lax.all_to_all(partial_value, "blk", split_axis=0, concat_axis=0, tiled=True)
    halves = returned_rows.reshape(experts, 2, capacity, feature_width).astype(jnp.float32)
    results = halves[:, 0] + halves[:, 1]
    flattened = results.reshape(experts * capacity, feature_width)
    picked = jnp.take(flattened, slot_index, axis=0)
    weighted = picked.reshape(tok_count, per_token, feature_width) * route_gate[:, :, None]
    return jnp.sum(weighted, axis=1).astype(jnp.bfloat16)


def snake(chips):
    return list(range(0, chips, 2)) + list(range(chips - 1, 0, -2))


def half_expert_kernel(heights, load, split, *refs):
    blocks, refs = refs[: len(heights)], refs[len(heights) :]
    if load:
        (gate_up_far, down_far), refs = refs[:2], refs[2:]
        outs, (gate_up_ref, down_ref, rows, hidden, arrived) = refs[:split], refs[split:]
    else:
        (gate_up_ref, down_ref), outs, (rows, hidden) = refs[:2], refs[2:-2], refs[-2:]
    units, width = down_ref.shape
    tile = 256 if units % 256 == 0 else units
    tiles = units // tile
    copies = []
    if load:
        for t in range(tiles):
            near = pl.ds(t * tile, tile)
            copies.append(pltpu.make_async_copy(gate_up_far.at[:, near], gate_up_ref.at[:, near], arrived.at[t]))
        copies.append(pltpu.make_async_copy(down_far, down_ref, arrived.at[tiles]))
        for copy in copies:
            copy.start()

    at = 0
    for block, height in zip(blocks, heights):
        rows[at : at + height, :] = block[:height, :]
        at += height

    contract = (((1,), (1,)), ((), ()))
    taken = rows[...]
    for t in range(tiles):
        if load:
            copies[t].wait()
        near = slice(t * tile, (t + 1) * tile)
        gating = lax.dot_general(taken, gate_up_ref[0, near], contract, preferred_element_type=jnp.float32)
        lifted = lax.dot_general(taken, gate_up_ref[1, near], contract, preferred_element_type=jnp.float32)
        hidden[:, near] = (gating / (1.0 + jnp.exp(-gating)) * lifted).astype(jnp.bfloat16)
    if load:
        copies[tiles].wait()
    inner = hidden[...]
    share = outs[0].shape[0]
    tile = 512 if width % 512 == 0 else width
    for low in range(0, width, tile):
        product = jnp.dot(inner, down_ref[:, low : low + tile], preferred_element_type=jnp.float32)
        product = product.astype(jnp.bfloat16)
        for i, out in enumerate(outs):
            out[:, low : low + tile] = product[i * share : (i + 1) * share]


def half_expert(heights, blocks, weights, load=False, cost=2, split=2):
    height = sum(heights)
    units, width = weights[1].shape
    whole = pl.BlockSpec(memory_space=pltpu.VMEM)
    far = pl.BlockSpec(memory_space=pltpu.HBM)
    outs = [jax.ShapeDtypeStruct((height // split, width), jnp.bfloat16)] * split
    scratch = [pltpu.VMEM((height, width), jnp.bfloat16), pltpu.VMEM((height, units), jnp.bfloat16)]
    if load:
        outs += [jax.ShapeDtypeStruct(array.shape, array.dtype) for array in weights]
        scratch.append(pltpu.SemaphoreType.DMA((units // 256 + 1 if units % 256 == 0 else 2,)))
    return pl.pallas_call(
        functools.partial(half_expert_kernel, tuple(heights), load, split),
        out_shape=outs,
        in_specs=[whole] * len(blocks) + [far if load else whole] * 2,
        out_specs=[whole] * len(outs),
        scratch_shapes=scratch,
        compiler_params=pltpu.CompilerParams(vmem_limit_bytes=(34 if load else 14) << 20),
        cost_estimate=pl.CostEstimate(
            flops=int(cost * height * units * width),
            bytes_accessed=int(cost * units * width),
            transcendentals=0,
        ),
    )(*blocks, *weights)


def weighted_kernel(kind, token, low, part_rows, expert_ref, holder, mine, theirs, *refs):
    *arrived, out = refs
    height = mine.shape[0]
    last = holder.shape[0] - GATE_ROWS
    near, far = (holder[last:, (2 * kind + i) * LANES : (2 * kind + i + 1) * LANES].astype(jnp.float32) for i in (0, 1))
    wanted = lax.broadcasted_iota(jnp.int32, near.shape, 0) == expert_ref[0]
    line = jnp.sum(jnp.where(wanted, near + far, 0.0), axis=0, keepdims=True)
    weight = jnp.broadcast_to(line, near.shape).T[token : token + height, :1]
    value = weight * (mine[...].astype(jnp.float32) + theirs[...].astype(jnp.float32))
    out[:height, :] = value.astype(out.dtype)
    if height < out.shape[0]:
        out[height:, :] = jnp.zeros((out.shape[0] - height, out.shape[1]), out.dtype)
    if arrived:
        part = slice(low, low + part_rows)
        out[part, :] = (value[part] + arrived[0][:part_rows, :].astype(jnp.float32)).astype(out.dtype)


def weighted(expert, holder, kind, mine, theirs, *arrived, token=0, low=0, part=None, more=0, dtype=jnp.bfloat16):
    whole = pl.BlockSpec(memory_space=pltpu.VMEM)
    size = mine.size
    return pl.pallas_call(
        functools.partial(weighted_kernel, kind, token, low, part or mine.shape[0]),
        out_shape=jax.ShapeDtypeStruct((mine.shape[0] + more, mine.shape[1]), dtype),
        in_specs=[pl.BlockSpec(memory_space=pltpu.SMEM)] + [whole] * (3 + len(arrived)),
        out_specs=whole,
        compiler_params=pltpu.CompilerParams(vmem_limit_bytes=10 << 20),
        cost_estimate=pl.CostEstimate(flops=size * 20000, bytes_accessed=size, transcendentals=0),
    )(expert, holder, mine, theirs, *arrived)


def by_tokens(tokens, expert_ids, route_gate, gate_up, down_proj):
    chips = lax.axis_size("blk") // 2
    order, far = snake(chips), chips // 2
    rows = tokens.shape[0]
    half = rows // 2
    chains = (0, 1)

    def moved(steps, swap=False):
        pairs = []
        for place in range(chips):
            for core in (0, 1):
                target = order[(place + steps * (1 - 2 * core)) % chips]
                pairs.append((2 * order[place] + core, 2 * target + (1 - core if swap else core)))
        return pairs

    forth, back, across, cores = moved(1), moved(-1), moved(-1, True), moved(0, True)

    def send(value, pairs, name):
        with jax.named_scope(name):
            return lax.ppermute(value, "blk", pairs)

    def total(*terms):
        return sum(term.astype(jnp.float32) for term in terms)

    def rounded(value):
        return value.astype(jnp.bfloat16)

    def after(value, *earlier):
        return lax.optimization_barrier((value, *earlier))[0]

    expert = jnp.right_shift(lax.axis_index("blk"), 1).astype(jnp.int32).reshape(1)
    ring = [send(tokens, forth, "ring_1_0"), None]
    others = send(tokens, cores, "swap_0_0")
    chosen = jnp.arange(GATE_ROWS, dtype=jnp.int32)[:, None, None] == expert_ids.T[None]
    weight = jnp.sum(jnp.where(chosen, route_gate.T[None], 0.0), axis=1)
    high = lax.reduce_precision(weight, 8, 7)
    gates = jnp.concatenate([high, weight - high], axis=1).astype(jnp.bfloat16)
    gates = jnp.concatenate([gates, send(gates, cores, "swap_0_1")], axis=1)
    packed = jnp.concatenate([others, jnp.pad(gates, ((0, 0), (0, tokens.shape[1] - 4 * LANES)))])
    ring[1] = send(packed, forth, "ring_1_1")

    results, holders = {}, {0: packed}
    with jax.named_scope("expert_0"):
        inputs = [after(tokens, ring[0]), packed]
        own, given, *near = half_expert([rows] * 2, inputs, [gate_up, down_proj], load=True)
    results[0, 0] = own, given
    ring[1] = after(ring[1], own)

    def expert_rows(step, c, inputs, **options):
        with jax.named_scope(f"expert_{step}_{c}"):
            results[step, c] = half_expert([rows] * 2, inputs, near, **options)
        if step == far - 1 or (step, c) == (1, 1):
            give(step, c)
        return results[step, c][0]

    def give(step, c, *earlier):
        kept, given = results[step, c]
        results[step, c] = kept, send(after(given, *earlier) if earlier else given, cores, f"give_{step}_{c}")

    earlier = ring[1]
    for step in range(1, far):
        holders[step] = ring[1]
        swapped = [
            send(block[:rows], cores, f"swap_{step}_{c}") for c, block in enumerate(ring[: 1 if step == 1 else 2])
        ]
        blocks = list(ring)
        if step < far - 1:
            ring = [send(block, forth, f"ring_{step + 1}_{c}") for c, block in enumerate(ring)]
        else:
            ring = [send(ring[0][: half + GATE_ROWS], forth, f"ring_{far}_0"), send(ring[1][half:], forth, f"ring_{far}_1")]
        for c in chains:
            if (step, c) == (1, 1):
                delayed = blocks[1]
                earlier = ring[1]
                continue
            if (step, c) == (far - 1, 1):
                last = blocks[1], swapped[1]
                continue
            kept = expert_rows(step, c, [after(blocks[c], earlier), swapped[c]])
            ring[c] = after(ring[c], kept)
            earlier = ring[c]

    with jax.named_scope("expert_far_ring"):
        (given,) = half_expert([half] * 2, ring, near, split=1)
    swapped = [send(block[:half], cores, f"swap_{far}_{c}") for c, block in enumerate(ring)]
    swapped[0] = after(swapped[0], given)
    given = send(given, cores, "give_far")
    with jax.named_scope("expert_far_swapped"):
        (kept,) = half_expert([half] * 2, swapped, near, split=1)

    late = []
    earlier = kept
    for c, part in enumerate((slice(half, rows), slice(0, half))):
        mine = after(kept[part], earlier)
        earlier = weighted(expert, ring[1], c, mine, given[part], token=half if c == 0 else 0, more=GATE_ROWS)
        late.append(send(earlier, back, f"back_{far}_{c}"))
    earlier = expert_rows(far - 1, 1, [after(last[0], earlier), last[1]], cost=0.2)
    sums = []
    for c in chains:
        mine, theirs = results[far - 1, c]
        low = half if c == 0 else 0
        earlier = weighted(expert, holders[far - 1], c, after(mine, earlier), theirs, late[c], low=low, part=half)
        sums.append(send(earlier, back, f"back_{far - 1}_{c}"))
        if c == 0:
            for step in range(far - 2, 1, -1):
                for c2 in chains:
                    give(step, c2, earlier)
    swapped = send(after(delayed, earlier)[:rows], cores, "swap_1_1")
    give(1, 0, earlier)
    give(0, 0, earlier)
    earlier = expert_rows(1, 1, [after(delayed, earlier), swapped])
    for step in range(far - 2, 0, -1):
        for c in chains:
            mine, theirs = results[step, c]
            earlier = weighted(expert, holders[step], c, after(mine, earlier), theirs, sums[c])
            sums[c] = send(earlier, across if (step, c) == (1, 1) else back, f"back_{step}_{c}")
    own = weighted(expert, packed, 0, *results[0, 0], sums[0], dtype=jnp.float32)
    return rounded(total(own, sums[1]))


def solution(mesh):
    placed = (
        P(("groups", "blk"), None),
        P(("groups", "blk"), None),
        P(("groups", "blk"), None),
        P(None, "blk", None),
        P("blk", None),
    )

    def per_device(tokens, expert_ids, route_gate, gate_up, down_proj):
        experts = mesh.shape["blk"] // 2
        dense = experts <= min(GATE_ROWS, 2 * expert_ids.shape[1]) and tokens.shape[0] == LANES
        body = by_tokens if dense else by_slots
        return body(tokens, expert_ids, route_gate, gate_up, down_proj)

    return jax.shard_map(
        per_device,
        mesh=mesh,
        in_specs=placed,
        out_specs=P(("groups", "blk"), None),
        check_vma=False,
    )
```

```python
import functools

import jax
import jax.numpy as jnp
import numpy as np
from jax import lax
from jax.experimental import pallas as pl
from jax.experimental.pallas import tpu as pltpu
from jax.sharding import PartitionSpec as P

GATE_ROWS, LANES = 8, 128


def expert_half(slot_block, gate_up, down_proj):
    contract = (((1,), (1,)), ((), ()))
    gating = lax.dot_general(slot_block, gate_up[0], contract, preferred_element_type=jnp.float32)
    lifted = lax.dot_general(slot_block, gate_up[1], contract, preferred_element_type=jnp.float32)
    hidden = (jax.nn.silu(gating) * lifted).astype(jnp.bfloat16)
    return jnp.dot(hidden, down_proj, preferred_element_type=jnp.float32).astype(jnp.bfloat16)


def by_slots(tokens, expert_ids, route_gate, gate_up, down_proj):
    tok_count, per_token = expert_ids.shape
    feature_width = tokens.shape[1]
    devices = lax.axis_size("blk")
    experts = devices // 2
    capacity = 3 * tok_count * per_token // devices
    placements = tok_count * per_token
    chosen_ids = expert_ids.reshape(placements)
    onehot = (chosen_ids[:, None] == jnp.arange(experts, dtype=jnp.int32)[None, :]).astype(
        jnp.int32
    )
    ranked = jnp.sum((jnp.cumsum(onehot, axis=0) - 1) * onehot, axis=1)
    slot_index = chosen_ids * capacity + ranked
    token_of = jnp.arange(placements, dtype=jnp.int32) // per_token
    slot_table = jnp.full((experts * capacity,), tok_count, jnp.int32).at[slot_index].set(token_of)
    outgoing = jnp.take(tokens, slot_table, axis=0, mode="fill", fill_value=0)
    outgoing = outgoing.reshape(experts, capacity, feature_width)
    doubled = jnp.repeat(outgoing, 2, axis=0)
    received = lax.all_to_all(doubled, "blk", split_axis=0, concat_axis=0, tiled=True)
    item_count = received.shape[1]
    partial_value = expert_half(received.reshape(-1, feature_width), gate_up, down_proj)
    partial_value = partial_value.reshape(devices, item_count, feature_width)
    returned_rows = lax.all_to_all(partial_value, "blk", split_axis=0, concat_axis=0, tiled=True)
    halves = returned_rows.reshape(experts, 2, capacity, feature_width).astype(jnp.float32)
    results = halves[:, 0] + halves[:, 1]
    flattened = results.reshape(experts * capacity, feature_width)
    picked = jnp.take(flattened, slot_index, axis=0)
    weighted = picked.reshape(tok_count, per_token, feature_width) * route_gate[:, :, None]
    return jnp.sum(weighted, axis=1).astype(jnp.bfloat16)


def snake(chips):
    return list(range(0, chips, 2)) + list(range(chips - 1, 0, -2))


def half_expert_kernel(heights, load, split, *refs):
    blocks, refs = refs[: len(heights)], refs[len(heights) :]
    if load:
        (gate_up_far, down_far), refs = refs[:2], refs[2:]
        outs, (gate_up_ref, down_ref, rows, hidden, arrived) = refs[:split], refs[split:]
    else:
        (gate_up_ref, down_ref), outs, (rows, hidden) = refs[:2], refs[2:-2], refs[-2:]
    units, width = down_ref.shape
    tile = 256 if units % 256 == 0 else units
    tiles = units // tile
    copies = []
    if load:
        for t in range(tiles):
            near = pl.ds(t * tile, tile)
            copies.append(pltpu.make_async_copy(gate_up_far.at[:, near], gate_up_ref.at[:, near], arrived.at[t]))
        copies.append(pltpu.make_async_copy(down_far, down_ref, arrived.at[tiles]))
        for copy in copies:
            copy.start()

    at = 0
    for block, height in zip(blocks, heights):
        rows[at : at + height, :] = block[:height, :]
        at += height

    contract = (((1,), (1,)), ((), ()))
    taken = rows[...]
    for t in range(tiles):
        if load:
            copies[t].wait()
        near = slice(t * tile, (t + 1) * tile)
        gating = lax.dot_general(taken, gate_up_ref[0, near], contract, preferred_element_type=jnp.float32)
        lifted = lax.dot_general(taken, gate_up_ref[1, near], contract, preferred_element_type=jnp.float32)
        hidden[:, near] = (gating / (1.0 + jnp.exp(-gating)) * lifted).astype(jnp.bfloat16)
    if load:
        copies[tiles].wait()
    inner = hidden[...]
    share = outs[0].shape[0]
    tile = 512 if width % 512 == 0 else width
    for low in range(0, width, tile):
        product = jnp.dot(inner, down_ref[:, low : low + tile], preferred_element_type=jnp.float32)
        product = product.astype(jnp.bfloat16)
        for i, out in enumerate(outs):
            out[:, low : low + tile] = product[i * share : (i + 1) * share]


def half_expert(heights, blocks, weights, load=False, cost=2, split=2):
    height = sum(heights)
    units, width = weights[1].shape
    whole = pl.BlockSpec(memory_space=pltpu.VMEM)
    far = pl.BlockSpec(memory_space=pltpu.HBM)
    outs = [jax.ShapeDtypeStruct((height // split, width), jnp.bfloat16)] * split
    scratch = [pltpu.VMEM((height, width), jnp.bfloat16), pltpu.VMEM((height, units), jnp.bfloat16)]
    if load:
        outs += [jax.ShapeDtypeStruct(array.shape, array.dtype) for array in weights]
        scratch.append(pltpu.SemaphoreType.DMA((units // 256 + 1 if units % 256 == 0 else 2,)))
    return pl.pallas_call(
        functools.partial(half_expert_kernel, tuple(heights), load, split),
        out_shape=outs,
        in_specs=[whole] * len(blocks) + [far if load else whole] * 2,
        out_specs=[whole] * len(outs),
        scratch_shapes=scratch,
        compiler_params=pltpu.CompilerParams(vmem_limit_bytes=(34 if load else 14) << 20),
        cost_estimate=pl.CostEstimate(
            flops=int(cost * height * units * width),
            bytes_accessed=int(cost * units * width),
            transcendentals=0,
        ),
    )(*blocks, *weights)


def weighted_kernel(kind, first, height, low, part_rows, expert_ref, holder, mine, theirs, *refs):
    *arrived, out = refs
    last = holder.shape[0] - GATE_ROWS
    near, far = (holder[last:, (2 * kind + i) * LANES : (2 * kind + i + 1) * LANES].astype(jnp.float32) for i in (0, 1))
    wanted = lax.broadcasted_iota(jnp.int32, near.shape, 0) == expert_ref[0]
    line = jnp.sum(jnp.where(wanted, near + far, 0.0), axis=0, keepdims=True)
    weight = jnp.broadcast_to(line, near.shape).T[first : first + height, :1]
    value = mine[...].astype(jnp.float32) + theirs[first : first + height, :].astype(jnp.float32)
    value = weight * value
    out[:height, :] = value.astype(out.dtype)
    if height < out.shape[0]:
        out[height:, :] = jnp.zeros((out.shape[0] - height, out.shape[1]), out.dtype)
    if arrived:
        part = slice(low, low + part_rows)
        out[part, :] = (value[part] + arrived[0][:part_rows, :].astype(jnp.float32)).astype(out.dtype)


def weighted(expert, holder, kind, mine, theirs, *arrived, first=0, low=0, part=None, more=0, dtype=jnp.bfloat16):
    whole = pl.BlockSpec(memory_space=pltpu.VMEM)
    height = mine.shape[0]
    size = height * mine.shape[1]
    return pl.pallas_call(
        functools.partial(weighted_kernel, kind, first, height, low, part or height),
        out_shape=jax.ShapeDtypeStruct((height + more, mine.shape[1]), dtype),
        in_specs=[pl.BlockSpec(memory_space=pltpu.SMEM)] + [whole] * (3 + len(arrived)),
        out_specs=whole,
        compiler_params=pltpu.CompilerParams(vmem_limit_bytes=10 << 20),
        cost_estimate=pl.CostEstimate(flops=size * 20000, bytes_accessed=size, transcendentals=0),
    )(expert, holder, mine, theirs, *arrived)


def by_tokens(tokens, expert_ids, route_gate, gate_up, down_proj):
    chips = lax.axis_size("blk") // 2
    order, far = snake(chips), chips // 2
    rows = tokens.shape[0]
    half = rows // 2
    chains = (0, 1)

    def moved(steps, swap=False):
        pairs = []
        for place in range(chips):
            for core in (0, 1):
                target = order[(place + steps * (1 - 2 * core)) % chips]
                pairs.append((2 * order[place] + core, 2 * target + (1 - core if swap else core)))
        return pairs

    forth, back, across, cores = moved(1), moved(-1), moved(-1, True), moved(0, True)

    def send(value, pairs, name):
        with jax.named_scope(name):
            return lax.ppermute(value, "blk", pairs)

    def total(*terms):
        return sum(term.astype(jnp.float32) for term in terms)

    def rounded(value):
        return value.astype(jnp.bfloat16)

    def after(value, *earlier):
        return lax.optimization_barrier((value, *earlier))[0]

    expert = jnp.right_shift(lax.axis_index("blk"), 1).astype(jnp.int32).reshape(1)
    ring = [send(tokens, forth, "ring_1_0"), None]
    others = send(tokens, cores, "swap_0_0")
    chosen = jnp.arange(GATE_ROWS, dtype=jnp.int32)[:, None, None] == expert_ids.T[None]
    weight = jnp.sum(jnp.where(chosen, route_gate.T[None], 0.0), axis=1)
    high = lax.reduce_precision(weight, 8, 7)
    gates = jnp.concatenate([high, weight - high], axis=1).astype(jnp.bfloat16)
    gates = jnp.concatenate([gates, send(gates, cores, "swap_0_1")], axis=1)
    packed = jnp.concatenate([others, jnp.pad(gates, ((0, 0), (0, tokens.shape[1] - 4 * LANES)))])
    ring[1] = send(packed, forth, "ring_1_1")

    results, holders = {}, {0: packed}
    with jax.named_scope("expert_0"):
        inputs = [tokens, packed]
        own, given, *near = half_expert([rows] * 2, inputs, [gate_up, down_proj], load=True)
    results[0, 0] = own, given
    ring[0] = after(ring[0], own)

    def expert_rows(step, c, inputs, **options):
        with jax.named_scope(f"expert_{step}_{c}"):
            results[step, c] = half_expert([rows] * 2, inputs, near, **options)
        if step == far - 1 or (step, c) == (1, 1):
            give(step, c)
        return results[step, c][0]

    def give(step, c, *earlier):
        kept, given = results[step, c]
        results[step, c] = kept, send(after(given, *earlier) if earlier else given, cores, f"give_{step}_{c}")

    earlier = ring[1]
    for step in range(1, far):
        holders[step] = ring[1]
        swapped = [
            send(block, cores, f"swap_{step}_{c}") for c, block in enumerate(ring[: 1 if step == 1 else 2])
        ]
        blocks = list(ring)
        if step < far - 1:
            ring = [send(block, forth, f"ring_{step + 1}_{c}") for c, block in enumerate(ring)]
        else:
            ring = [send(ring[0][: half + GATE_ROWS], forth, f"ring_{far}_0"), send(ring[1][half:], forth, f"ring_{far}_1")]
        for c in chains:
            if (step, c) == (1, 1):
                delayed = blocks[1]
                earlier = ring[1]
                continue
            if (step, c) == (far - 1, 1):
                last = blocks[1], swapped[1]
                continue
            kept = expert_rows(step, c, [after(blocks[c], earlier), swapped[c]])
            ring[c] = after(ring[c], kept)
            earlier = ring[c]

    with jax.named_scope("expert_far_ring"):
        (given,) = half_expert([half] * 2, ring, near, split=1)
    swapped = [send(block, cores, f"swap_{far}_{c}") for c, block in enumerate(ring)]
    swapped[0] = after(swapped[0], given)
    given = send(given, cores, "give_far")
    with jax.named_scope("expert_far_swapped"):
        (kept,) = half_expert([half] * 2, swapped, near, split=1)

    late = []
    earlier = kept
    for c in chains:
        first = (1 - c) * half
        mine = after(kept[first : first + half], earlier)
        earlier = weighted(expert, ring[1], c, mine, given, first=first, more=GATE_ROWS)
        late.append(send(earlier, back, f"back_{far}_{c}"))
    earlier = expert_rows(far - 1, 1, [after(last[0], earlier), last[1]], cost=0.2)
    sums = []
    for c in chains:
        mine, theirs = results[far - 1, c]
        low = half if c == 0 else 0
        earlier = weighted(expert, holders[far - 1], c, after(mine, earlier), theirs, late[c], low=low, part=half)
        sums.append(send(earlier, back, f"back_{far - 1}_{c}"))
        if c == 0:
            swapped = send(after(delayed, earlier), cores, "swap_1_1")
            for step in range(far - 2, 1, -1):
                for c2 in chains:
                    give(step, c2, earlier)
    give(1, 0, earlier)
    give(0, 0, earlier)
    earlier = expert_rows(1, 1, [after(delayed, earlier), swapped])
    for step in range(far - 2, 0, -1):
        for c in chains:
            mine, theirs = results[step, c]
            earlier = weighted(expert, holders[step], c, after(mine, earlier), theirs, sums[c])
            sums[c] = send(earlier, across if (step, c) == (1, 1) else back, f"back_{step}_{c}")
    own = weighted(expert, packed, 0, *results[0, 0], sums[0], dtype=jnp.float32)
    return rounded(total(own, sums[1]))


def solution(mesh):
    placed = (
        P(("groups", "blk"), None),
        P(("groups", "blk"), None),
        P(("groups", "blk"), None),
        P(None, "blk", None),
        P("blk", None),
    )

    def per_device(tokens, expert_ids, route_gate, gate_up, down_proj):
        experts = mesh.shape["blk"] // 2
        dense = experts <= min(GATE_ROWS, 2 * expert_ids.shape[1]) and tokens.shape[0] == LANES
        body = by_tokens if dense else by_slots
        return body(tokens, expert_ids, route_gate, gate_up, down_proj)

    return jax.shard_map(
        per_device,
        mesh=mesh,
        in_specs=placed,
        out_specs=P(("groups", "blk"), None),
        check_vma=False,
    )
```

```python
import functools

import jax
import jax.numpy as jnp
import numpy as np
from jax import lax
from jax.experimental import pallas as pl
from jax.experimental.pallas import tpu as pltpu
from jax.sharding import PartitionSpec as P

GATE_ROWS, LANES = 8, 128


def expert_half(slot_block, gate_up, down_proj):
    contract = (((1,), (1,)), ((), ()))
    gating = lax.dot_general(slot_block, gate_up[0], contract, preferred_element_type=jnp.float32)
    lifted = lax.dot_general(slot_block, gate_up[1], contract, preferred_element_type=jnp.float32)
    hidden = (jax.nn.silu(gating) * lifted).astype(jnp.bfloat16)
    return jnp.dot(hidden, down_proj, preferred_element_type=jnp.float32).astype(jnp.bfloat16)


def by_slots(tokens, expert_ids, route_gate, gate_up, down_proj):
    tok_count, per_token = expert_ids.shape
    feature_width = tokens.shape[1]
    devices = lax.axis_size("blk")
    experts = devices // 2
    capacity = 3 * tok_count * per_token // devices
    placements = tok_count * per_token
    chosen_ids = expert_ids.reshape(placements)
    onehot = (chosen_ids[:, None] == jnp.arange(experts, dtype=jnp.int32)[None, :]).astype(
        jnp.int32
    )
    ranked = jnp.sum((jnp.cumsum(onehot, axis=0) - 1) * onehot, axis=1)
    slot_index = chosen_ids * capacity + ranked
    token_of = jnp.arange(placements, dtype=jnp.int32) // per_token
    slot_table = jnp.full((experts * capacity,), tok_count, jnp.int32).at[slot_index].set(token_of)
    outgoing = jnp.take(tokens, slot_table, axis=0, mode="fill", fill_value=0)
    outgoing = outgoing.reshape(experts, capacity, feature_width)
    doubled = jnp.repeat(outgoing, 2, axis=0)
    received = lax.all_to_all(doubled, "blk", split_axis=0, concat_axis=0, tiled=True)
    item_count = received.shape[1]
    partial_value = expert_half(received.reshape(-1, feature_width), gate_up, down_proj)
    partial_value = partial_value.reshape(devices, item_count, feature_width)
    returned_rows = lax.all_to_all(partial_value, "blk", split_axis=0, concat_axis=0, tiled=True)
    halves = returned_rows.reshape(experts, 2, capacity, feature_width).astype(jnp.float32)
    results = halves[:, 0] + halves[:, 1]
    flattened = results.reshape(experts * capacity, feature_width)
    picked = jnp.take(flattened, slot_index, axis=0)
    weighted = picked.reshape(tok_count, per_token, feature_width) * route_gate[:, :, None]
    return jnp.sum(weighted, axis=1).astype(jnp.bfloat16)


def snake(chips):
    return list(range(0, chips, 2)) + list(range(chips - 1, 0, -2))


def half_expert_kernel(heights, load, split, *refs):
    blocks, refs = refs[: len(heights)], refs[len(heights) :]
    if load:
        (gate_up_far, down_far), refs = refs[:2], refs[2:]
        outs, (gate_up_ref, down_ref, rows, hidden, arrived) = refs[:split], refs[split:]
    else:
        (gate_up_ref, down_ref), outs, (rows, hidden) = refs[:2], refs[2:-2], refs[-2:]
    units, width = down_ref.shape
    tile = 256 if units % 256 == 0 else units
    tiles = units // tile
    copies = []
    if load:
        for t in range(tiles):
            near = pl.ds(t * tile, tile)
            copies.append(pltpu.make_async_copy(gate_up_far.at[:, near], gate_up_ref.at[:, near], arrived.at[t]))
        copies.append(pltpu.make_async_copy(down_far, down_ref, arrived.at[tiles]))
        for copy in copies:
            copy.start()

    at = 0
    for block, height in zip(blocks, heights):
        rows[at : at + height, :] = block[:height, :]
        at += height

    contract = (((1,), (1,)), ((), ()))
    taken = rows[...]
    for t in range(tiles):
        if load:
            copies[t].wait()
        near = slice(t * tile, (t + 1) * tile)
        gating = lax.dot_general(taken, gate_up_ref[0, near], contract, preferred_element_type=jnp.float32)
        lifted = lax.dot_general(taken, gate_up_ref[1, near], contract, preferred_element_type=jnp.float32)
        hidden[:, near] = (gating / (1.0 + jnp.exp(-gating)) * lifted).astype(jnp.bfloat16)
    if load:
        copies[tiles].wait()
    inner = hidden[...]
    share = outs[0].shape[0]
    tile = 512 if width % 512 == 0 else width
    for low in range(0, width, tile):
        product = jnp.dot(inner, down_ref[:, low : low + tile], preferred_element_type=jnp.float32)
        product = product.astype(jnp.bfloat16)
        for i, out in enumerate(outs):
            out[:, low : low + tile] = product[i * share : (i + 1) * share]


def half_expert(heights, blocks, weights, load=False, cost=2, split=2):
    height = sum(heights)
    units, width = weights[1].shape
    whole = pl.BlockSpec(memory_space=pltpu.VMEM)
    far = pl.BlockSpec(memory_space=pltpu.HBM)
    outs = [jax.ShapeDtypeStruct((height // split, width), jnp.bfloat16)] * split
    scratch = [pltpu.VMEM((height, width), jnp.bfloat16), pltpu.VMEM((height, units), jnp.bfloat16)]
    if load:
        outs += [jax.ShapeDtypeStruct(array.shape, array.dtype) for array in weights]
        scratch.append(pltpu.SemaphoreType.DMA((units // 256 + 1 if units % 256 == 0 else 2,)))
    return pl.pallas_call(
        functools.partial(half_expert_kernel, tuple(heights), load, split),
        out_shape=outs,
        in_specs=[whole] * len(blocks) + [far if load else whole] * 2,
        out_specs=[whole] * len(outs),
        scratch_shapes=scratch,
        compiler_params=pltpu.CompilerParams(vmem_limit_bytes=(34 if load else 14) << 20),
        cost_estimate=pl.CostEstimate(
            flops=int(cost * height * units * width),
            bytes_accessed=int(cost * units * width),
            transcendentals=0,
        ),
    )(*blocks, *weights)


def weighted_kernel(kind, first, height, low, part_rows, expert_ref, holder, mine, theirs, *refs):
    *arrived, out = refs
    last = holder.shape[0] - GATE_ROWS
    near, far = (holder[last:, (2 * kind + i) * LANES : (2 * kind + i + 1) * LANES].astype(jnp.float32) for i in (0, 1))
    wanted = lax.broadcasted_iota(jnp.int32, near.shape, 0) == expert_ref[0]
    line = jnp.sum(jnp.where(wanted, near + far, 0.0), axis=0, keepdims=True)
    weight = jnp.broadcast_to(line, near.shape).T[first : first + height, :1]
    value = mine[...].astype(jnp.float32) + theirs[first : first + height, :].astype(jnp.float32)
    value = weight * value
    out[:height, :] = value.astype(out.dtype)
    if height < out.shape[0]:
        out[height:, :] = jnp.zeros((out.shape[0] - height, out.shape[1]), out.dtype)
    if arrived:
        part = slice(low, low + part_rows)
        out[part, :] = (value[part] + arrived[0][:part_rows, :].astype(jnp.float32)).astype(out.dtype)


def weighted(expert, holder, kind, mine, theirs, *arrived, first=0, low=0, part=None, more=0, dtype=jnp.bfloat16):
    whole = pl.BlockSpec(memory_space=pltpu.VMEM)
    height = mine.shape[0]
    size = height * mine.shape[1]
    return pl.pallas_call(
        functools.partial(weighted_kernel, kind, first, height, low, part or height),
        out_shape=jax.ShapeDtypeStruct((height + more, mine.shape[1]), dtype),
        in_specs=[pl.BlockSpec(memory_space=pltpu.SMEM)] + [whole] * (3 + len(arrived)),
        out_specs=whole,
        compiler_params=pltpu.CompilerParams(vmem_limit_bytes=10 << 20),
        cost_estimate=pl.CostEstimate(flops=size * 20000, bytes_accessed=size, transcendentals=0),
    )(expert, holder, mine, theirs, *arrived)


def by_tokens(tokens, expert_ids, route_gate, gate_up, down_proj):
    chips = lax.axis_size("blk") // 2
    order, far = snake(chips), chips // 2
    rows = tokens.shape[0]
    half = rows // 2
    chains = (0, 1)

    def moved(steps, swap=False):
        pairs = []
        for place in range(chips):
            for core in (0, 1):
                target = order[(place + steps * (1 - 2 * core)) % chips]
                pairs.append((2 * order[place] + core, 2 * target + (1 - core if swap else core)))
        return pairs

    forth, back, across, cores = moved(1), moved(-1), moved(-1, True), moved(0, True)

    def send(value, pairs, name):
        with jax.named_scope(name):
            return lax.ppermute(value, "blk", pairs)

    def total(*terms):
        return sum(term.astype(jnp.float32) for term in terms)

    def rounded(value):
        return value.astype(jnp.bfloat16)

    def after(value, *earlier):
        return lax.optimization_barrier((value, *earlier))[0]

    expert = jnp.right_shift(lax.axis_index("blk"), 1).astype(jnp.int32).reshape(1)
    ring = [send(tokens, forth, "ring_1_0"), None]
    others = send(tokens, cores, "swap_0_0")
    chosen = jnp.arange(GATE_ROWS, dtype=jnp.int32)[:, None, None] == expert_ids.T[None]
    weight = jnp.sum(jnp.where(chosen, route_gate.T[None], 0.0), axis=1)
    high = lax.reduce_precision(weight, 8, 7)
    gates = jnp.concatenate([high, weight - high], axis=1).astype(jnp.bfloat16)
    gates = jnp.concatenate([gates, send(gates, cores, "swap_0_1")], axis=1)
    packed = jnp.concatenate([others, jnp.pad(gates, ((0, 0), (0, tokens.shape[1] - 4 * LANES)))])
    ring[1] = send(packed, forth, "ring_1_1")

    results, holders = {}, {0: packed}
    with jax.named_scope("expert_0"):
        inputs = [after(tokens, expert), packed]
        own, given, *near = half_expert([rows] * 2, inputs, [gate_up, down_proj], load=True)
    results[0, 0] = own, given
    ring[0] = after(ring[0], own)

    def expert_rows(step, c, inputs, **options):
        with jax.named_scope(f"expert_{step}_{c}"):
            results[step, c] = half_expert([rows] * 2, inputs, near, **options)
        if step == far - 1 or (step, c) == (1, 1):
            give(step, c)
        return results[step, c][0]

    def give(step, c, *earlier):
        kept, given = results[step, c]
        results[step, c] = kept, send(after(given, *earlier) if earlier else given, cores, f"give_{step}_{c}")

    earlier = ring[1]
    for step in range(1, far):
        holders[step] = ring[1]
        swapped = [
            send(block, cores, f"swap_{step}_{c}") for c, block in enumerate(ring[: 1 if step == 1 else 2])
        ]
        blocks = list(ring)
        if step < far - 1:
            ring = [send(block, forth, f"ring_{step + 1}_{c}") for c, block in enumerate(ring)]
        else:
            ring = [send(ring[0][: half + GATE_ROWS], forth, f"ring_{far}_0"), send(ring[1][half:], forth, f"ring_{far}_1")]
        for c in chains:
            if (step, c) == (1, 1):
                delayed = blocks[1]
                earlier = ring[1]
                continue
            if (step, c) == (far - 1, 1):
                last = blocks[1], swapped[1]
                continue
            kept = expert_rows(step, c, [after(blocks[c], earlier), swapped[c]])
            ring[c] = after(ring[c], kept)
            earlier = ring[c]

    with jax.named_scope("expert_far_ring"):
        (given,) = half_expert([half] * 2, ring, near, split=1)
    swapped = [send(block, cores, f"swap_{far}_{c}") for c, block in enumerate(ring)]
    swapped[0] = after(swapped[0], given)
    given = send(given, cores, "give_far")
    with jax.named_scope("expert_far_swapped"):
        (kept,) = half_expert([half] * 2, swapped, near, split=1)

    late = []
    earlier = kept
    for c in chains:
        first = (1 - c) * half
        mine = after(kept[first : first + half], earlier)
        earlier = weighted(expert, ring[1], c, mine, given, first=first, more=GATE_ROWS)
        late.append(send(earlier, back, f"back_{far}_{c}"))
    earlier = expert_rows(far - 1, 1, [after(last[0], earlier), last[1]], cost=0.2)
    sums = []
    for c in chains:
        mine, theirs = results[far - 1, c]
        low = half if c == 0 else 0
        earlier = weighted(expert, holders[far - 1], c, after(mine, earlier), theirs, late[c], low=low, part=half)
        sums.append(send(earlier, back, f"back_{far - 1}_{c}"))
        if c == 0:
            swapped = send(after(delayed, earlier), cores, "swap_1_1")
            for step in range(far - 2, 1, -1):
                for c2 in chains:
                    give(step, c2, earlier)
    give(1, 0, earlier)
    give(0, 0, earlier)
    earlier = expert_rows(1, 1, [after(delayed, earlier), swapped])
    for step in range(far - 2, 0, -1):
        for c in chains:
            mine, theirs = results[step, c]
            earlier = weighted(expert, holders[step], c, after(mine, earlier), theirs, sums[c])
            sums[c] = send(earlier, across if (step, c) == (1, 1) else back, f"back_{step}_{c}")
    own = weighted(expert, packed, 0, *results[0, 0], sums[0], dtype=jnp.float32)
    return rounded(total(own, sums[1]))


def solution(mesh):
    placed = (
        P(("groups", "blk"), None),
        P(("groups", "blk"), None),
        P(("groups", "blk"), None),
        P(None, "blk", None),
        P("blk", None),
    )

    def per_device(tokens, expert_ids, route_gate, gate_up, down_proj):
        experts = mesh.shape["blk"] // 2
        dense = experts <= min(GATE_ROWS, 2 * expert_ids.shape[1]) and tokens.shape[0] == LANES
        body = by_tokens if dense else by_slots
        return body(tokens, expert_ids, route_gate, gate_up, down_proj)

    return jax.shard_map(
        per_device,
        mesh=mesh,
        in_specs=placed,
        out_specs=P(("groups", "blk"), None),
        check_vma=False,
    )
```

```python
import functools

import jax
import jax.numpy as jnp
import numpy as np
from jax import lax
from jax.experimental import pallas as pl
from jax.experimental.pallas import tpu as pltpu
from jax.sharding import PartitionSpec as P

GATE_ROWS, LANES = 8, 128


def expert_half(slot_block, gate_up, down_proj):
    contract = (((1,), (1,)), ((), ()))
    gating = lax.dot_general(slot_block, gate_up[0], contract, preferred_element_type=jnp.float32)
    lifted = lax.dot_general(slot_block, gate_up[1], contract, preferred_element_type=jnp.float32)
    hidden = (jax.nn.silu(gating) * lifted).astype(jnp.bfloat16)
    return jnp.dot(hidden, down_proj, preferred_element_type=jnp.float32).astype(jnp.bfloat16)


def by_slots(tokens, expert_ids, route_gate, gate_up, down_proj):
    tok_count, per_token = expert_ids.shape
    feature_width = tokens.shape[1]
    devices = lax.axis_size("blk")
    experts = devices // 2
    capacity = 3 * tok_count * per_token // devices
    placements = tok_count * per_token
    chosen_ids = expert_ids.reshape(placements)
    onehot = (chosen_ids[:, None] == jnp.arange(experts, dtype=jnp.int32)[None, :]).astype(
        jnp.int32
    )
    ranked = jnp.sum((jnp.cumsum(onehot, axis=0) - 1) * onehot, axis=1)
    slot_index = chosen_ids * capacity + ranked
    token_of = jnp.arange(placements, dtype=jnp.int32) // per_token
    slot_table = jnp.full((experts * capacity,), tok_count, jnp.int32).at[slot_index].set(token_of)
    outgoing = jnp.take(tokens, slot_table, axis=0, mode="fill", fill_value=0)
    outgoing = outgoing.reshape(experts, capacity, feature_width)
    doubled = jnp.repeat(outgoing, 2, axis=0)
    received = lax.all_to_all(doubled, "blk", split_axis=0, concat_axis=0, tiled=True)
    item_count = received.shape[1]
    partial_value = expert_half(received.reshape(-1, feature_width), gate_up, down_proj)
    partial_value = partial_value.reshape(devices, item_count, feature_width)
    returned_rows = lax.all_to_all(partial_value, "blk", split_axis=0, concat_axis=0, tiled=True)
    halves = returned_rows.reshape(experts, 2, capacity, feature_width).astype(jnp.float32)
    results = halves[:, 0] + halves[:, 1]
    flattened = results.reshape(experts * capacity, feature_width)
    picked = jnp.take(flattened, slot_index, axis=0)
    weighted = picked.reshape(tok_count, per_token, feature_width) * route_gate[:, :, None]
    return jnp.sum(weighted, axis=1).astype(jnp.bfloat16)


def snake(chips):
    return list(range(0, chips, 2)) + list(range(chips - 1, 0, -2))


def half_expert_kernel(heights, load, split, *refs):
    blocks, refs = refs[: len(heights)], refs[len(heights) :]
    if load:
        (gate_up_far, down_far), refs = refs[:2], refs[2:]
        outs, (gate_up_ref, down_ref, rows, hidden, arrived) = refs[:split], refs[split:]
    else:
        (gate_up_ref, down_ref), outs, (rows, hidden) = refs[:2], refs[2:-2], refs[-2:]
    units, width = down_ref.shape
    tile = 256 if units % 256 == 0 else units
    tiles = units // tile
    copies = []
    if load:
        for t in range(tiles):
            near = pl.ds(t * tile, tile)
            copies.append(pltpu.make_async_copy(gate_up_far.at[:, near], gate_up_ref.at[:, near], arrived.at[t]))
        copies.append(pltpu.make_async_copy(down_far, down_ref, arrived.at[tiles]))
        for copy in copies:
            copy.start()

    at = 0
    for block, height in zip(blocks, heights):
        rows[at : at + height, :] = block[:height, :]
        at += height

    contract = (((1,), (1,)), ((), ()))
    taken = rows[...]
    for t in range(tiles):
        if load:
            copies[t].wait()
        near = slice(t * tile, (t + 1) * tile)
        gating = lax.dot_general(taken, gate_up_ref[0, near], contract, preferred_element_type=jnp.float32)
        lifted = lax.dot_general(taken, gate_up_ref[1, near], contract, preferred_element_type=jnp.float32)
        hidden[:, near] = (gating / (1.0 + jnp.exp(-gating)) * lifted).astype(jnp.bfloat16)
    if load:
        copies[tiles].wait()
    inner = hidden[...]
    share = outs[0].shape[0]
    tile = 512 if width % 512 == 0 else width
    for low in range(0, width, tile):
        product = jnp.dot(inner, down_ref[:, low : low + tile], preferred_element_type=jnp.float32)
        product = product.astype(jnp.bfloat16)
        for i, out in enumerate(outs):
            out[:, low : low + tile] = product[i * share : (i + 1) * share]


def load_kernel(*refs):
    copies = [pltpu.make_async_copy(far, near, refs[4].at[i]) for i, (far, near) in enumerate(zip(refs[:2], refs[2:4]))]
    for copy in copies:
        copy.start()
    for copy in copies:
        copy.wait()


def loaded(*weights):
    return pl.pallas_call(
        load_kernel,
        out_shape=[jax.ShapeDtypeStruct(array.shape, array.dtype) for array in weights],
        in_specs=[pl.BlockSpec(memory_space=pltpu.HBM)] * 2,
        out_specs=[pl.BlockSpec(memory_space=pltpu.VMEM)] * 2,
        scratch_shapes=[pltpu.SemaphoreType.DMA((2,))],
        compiler_params=pltpu.CompilerParams(vmem_limit_bytes=38 << 20),
        cost_estimate=pl.CostEstimate(flops=1 << 28, bytes_accessed=1 << 20, transcendentals=0),
    )(*weights)


def widen_kernel(gates, out):
    out[...] = jnp.concatenate([gates[...], jnp.zeros((GATE_ROWS, out.shape[1] - gates.shape[1]), out.dtype)], axis=1)


def widened(own, other, width):
    whole = pl.BlockSpec(memory_space=pltpu.VMEM)
    wide = pl.pallas_call(
        widen_kernel,
        out_shape=jax.ShapeDtypeStruct((GATE_ROWS, width), own.dtype),
        in_specs=[whole],
        out_specs=whole,
        compiler_params=pltpu.CompilerParams(vmem_limit_bytes=8 << 20),
        cost_estimate=pl.CostEstimate(flops=1 << 28, bytes_accessed=1 << 20, transcendentals=0),
    )(own)
    size = own.shape[1]
    return jnp.concatenate([wide[:, :size], other, wide[:, 2 * size :]], axis=1)


def half_expert(heights, blocks, weights, load=False, cost=2, split=2):
    height = sum(heights)
    units, width = weights[1].shape
    whole = pl.BlockSpec(memory_space=pltpu.VMEM)
    far = pl.BlockSpec(memory_space=pltpu.HBM)
    outs = [jax.ShapeDtypeStruct((height // split, width), jnp.bfloat16)] * split
    scratch = [pltpu.VMEM((height, width), jnp.bfloat16), pltpu.VMEM((height, units), jnp.bfloat16)]
    if load:
        outs += [jax.ShapeDtypeStruct(array.shape, array.dtype) for array in weights]
        scratch.append(pltpu.SemaphoreType.DMA((units // 256 + 1 if units % 256 == 0 else 2,)))
    return pl.pallas_call(
        functools.partial(half_expert_kernel, tuple(heights), load, split),
        out_shape=outs,
        in_specs=[whole] * len(blocks) + [far if load else whole] * 2,
        out_specs=[whole] * len(outs),
        scratch_shapes=scratch,
        compiler_params=pltpu.CompilerParams(vmem_limit_bytes=(34 if load else 14) << 20),
        cost_estimate=pl.CostEstimate(
            flops=int(cost * height * units * width),
            bytes_accessed=int(cost * units * width),
            transcendentals=0,
        ),
    )(*blocks, *weights)


def weighted_kernel(kind, first, height, low, part_rows, expert_ref, holder, mine, theirs, *refs):
    *arrived, out = refs
    last = holder.shape[0] - GATE_ROWS
    near, far = (holder[last:, (2 * kind + i) * LANES : (2 * kind + i + 1) * LANES].astype(jnp.float32) for i in (0, 1))
    wanted = lax.broadcasted_iota(jnp.int32, near.shape, 0) == expert_ref[0]
    line = jnp.sum(jnp.where(wanted, near + far, 0.0), axis=0, keepdims=True)
    weight = jnp.broadcast_to(line, near.shape).T[first : first + height, :1]
    value = mine[...].astype(jnp.float32) + theirs[first : first + height, :].astype(jnp.float32)
    value = weight * value
    out[:height, :] = value.astype(out.dtype)
    if height < out.shape[0]:
        out[height:, :] = jnp.zeros((out.shape[0] - height, out.shape[1]), out.dtype)
    if arrived:
        part = slice(low, low + part_rows)
        out[part, :] = (value[part] + arrived[0][:part_rows, :].astype(jnp.float32)).astype(out.dtype)


def weighted(expert, holder, kind, mine, theirs, *arrived, first=0, low=0, part=None, more=0, dtype=jnp.bfloat16):
    whole = pl.BlockSpec(memory_space=pltpu.VMEM)
    height = mine.shape[0]
    size = height * mine.shape[1]
    return pl.pallas_call(
        functools.partial(weighted_kernel, kind, first, height, low, part or height),
        out_shape=jax.ShapeDtypeStruct((height + more, mine.shape[1]), dtype),
        in_specs=[pl.BlockSpec(memory_space=pltpu.SMEM)] + [whole] * (3 + len(arrived)),
        out_specs=whole,
        compiler_params=pltpu.CompilerParams(vmem_limit_bytes=10 << 20),
        cost_estimate=pl.CostEstimate(flops=size * 20000, bytes_accessed=size, transcendentals=0),
    )(expert, holder, mine, theirs, *arrived)


def by_tokens(tokens, expert_ids, route_gate, gate_up, down_proj):
    chips = lax.axis_size("blk") // 2
    order, far = snake(chips), chips // 2
    rows = tokens.shape[0]
    half = rows // 2
    chains = (0, 1)

    def moved(steps, swap=False):
        pairs = []
        for place in range(chips):
            for core in (0, 1):
                target = order[(place + steps * (1 - 2 * core)) % chips]
                pairs.append((2 * order[place] + core, 2 * target + (1 - core if swap else core)))
        return pairs

    forth, back, across, cores = moved(1), moved(-1), moved(-1, True), moved(0, True)

    def send(value, pairs, name):
        with jax.named_scope(name):
            return lax.ppermute(value, "blk", pairs)

    def total(*terms):
        return sum(term.astype(jnp.float32) for term in terms)

    def rounded(value):
        return value.astype(jnp.bfloat16)

    def after(value, *earlier):
        return lax.optimization_barrier((value, *earlier))[0]

    expert = jnp.right_shift(lax.axis_index("blk"), 1).astype(jnp.int32).reshape(1)
    ring = [send(tokens, forth, "ring_1_0"), None]
    others = send(tokens, cores, "swap_0_0")
    chosen = jnp.arange(GATE_ROWS, dtype=jnp.int32)[:, None, None] == expert_ids.T[None]
    weight = jnp.sum(jnp.where(chosen, route_gate.T[None], 0.0), axis=1)
    high = lax.reduce_precision(weight, 8, 7)
    gates = jnp.concatenate([high, weight - high], axis=1).astype(jnp.bfloat16)
    packed = jnp.concatenate([others, widened(gates, send(gates, cores, "swap_0_1"), tokens.shape[1])])
    ring[1] = send(packed, forth, "ring_1_1")

    near = loaded(after(gate_up, expert), down_proj)
    ring[0] = after(ring[0], near[1])
    results, holders = {}, {0: packed}
    with jax.named_scope("expert_0"):
        own, given = half_expert([rows] * 2, [after(tokens, ring[0]), packed], near)
    results[0, 0] = own, given
    ring[1] = after(ring[1], own)

    def expert_rows(step, c, inputs, **options):
        with jax.named_scope(f"expert_{step}_{c}"):
            results[step, c] = half_expert([rows] * 2, inputs, near, **options)
        if step == far - 1 or (step, c) == (1, 1):
            give(step, c)
        return results[step, c][0]

    def give(step, c, *earlier):
        kept, given = results[step, c]
        results[step, c] = kept, send(after(given, *earlier) if earlier else given, cores, f"give_{step}_{c}")

    earlier = ring[1]
    for step in range(1, far):
        holders[step] = ring[1]
        swapped = [
            send(block, cores, f"swap_{step}_{c}") for c, block in enumerate(ring[: 1 if step == 1 else 2])
        ]
        blocks = list(ring)
        if step < far - 1:
            ring = [send(block, forth, f"ring_{step + 1}_{c}") for c, block in enumerate(ring)]
        else:
            ring = [send(ring[0][: half + GATE_ROWS], forth, f"ring_{far}_0"), send(ring[1][half:], forth, f"ring_{far}_1")]
        for c in chains:
            if (step, c) == (1, 1):
                delayed = blocks[1]
                earlier = ring[1]
                continue
            if (step, c) == (far - 1, 1):
                last = blocks[1], swapped[1]
                continue
            kept = expert_rows(step, c, [after(blocks[c], earlier), swapped[c]])
            ring[c] = after(ring[c], kept)
            earlier = ring[c]

    with jax.named_scope("expert_far_ring"):
        (given,) = half_expert([half] * 2, ring, near, split=1)
    swapped = [send(block, cores, f"swap_{far}_{c}") for c, block in enumerate(ring)]
    swapped[0] = after(swapped[0], given)
    given = send(given, cores, "give_far")
    with jax.named_scope("expert_far_swapped"):
        (kept,) = half_expert([half] * 2, swapped, near, split=1)

    late = []
    earlier = kept
    for c in chains:
        first = (1 - c) * half
        mine = after(kept[first : first + half], earlier)
        earlier = weighted(expert, ring[1], c, mine, given, first=first, more=GATE_ROWS)
        late.append(send(earlier, back, f"back_{far}_{c}"))
    earlier = expert_rows(far - 1, 1, [after(last[0], earlier), last[1]], cost=0.2)
    sums = []
    for c in chains:
        mine, theirs = results[far - 1, c]
        low = half if c == 0 else 0
        earlier = weighted(expert, holders[far - 1], c, after(mine, earlier), theirs, late[c], low=low, part=half)
        sums.append(send(earlier, back, f"back_{far - 1}_{c}"))
        if c == 0:
            swapped = send(after(delayed, earlier), cores, "swap_1_1")
            for step in range(far - 2, 1, -1):
                for c2 in chains:
                    give(step, c2, earlier)
    give(1, 0, earlier)
    give(0, 0, earlier)
    earlier = expert_rows(1, 1, [after(delayed, earlier), swapped])
    for step in range(far - 2, 0, -1):
        for c in chains:
            mine, theirs = results[step, c]
            earlier = weighted(expert, holders[step], c, after(mine, earlier), theirs, sums[c])
            sums[c] = send(earlier, across if (step, c) == (1, 1) else back, f"back_{step}_{c}")
    own = weighted(expert, packed, 0, *results[0, 0], sums[0], dtype=jnp.float32)
    return rounded(total(own, sums[1]))


def solution(mesh):
    placed = (
        P(("groups", "blk"), None),
        P(("groups", "blk"), None),
        P(("groups", "blk"), None),
        P(None, "blk", None),
        P("blk", None),
    )

    def per_device(tokens, expert_ids, route_gate, gate_up, down_proj):
        experts = mesh.shape["blk"] // 2
        dense = experts <= min(GATE_ROWS, 2 * expert_ids.shape[1]) and tokens.shape[0] == LANES
        body = by_tokens if dense else by_slots
        return body(tokens, expert_ids, route_gate, gate_up, down_proj)

    return jax.shard_map(
        per_device,
        mesh=mesh,
        in_specs=placed,
        out_specs=P(("groups", "blk"), None),
        check_vma=False,
    )
```

```python
import functools

import jax
import jax.numpy as jnp
import numpy as np
from jax import lax
from jax.experimental import pallas as pl
from jax.experimental.pallas import tpu as pltpu
from jax.sharding import PartitionSpec as P

GATE_ROWS, LANES = 8, 128


def expert_half(slot_block, gate_up, down_proj):
    contract = (((1,), (1,)), ((), ()))
    gating = lax.dot_general(slot_block, gate_up[0], contract, preferred_element_type=jnp.float32)
    lifted = lax.dot_general(slot_block, gate_up[1], contract, preferred_element_type=jnp.float32)
    hidden = (jax.nn.silu(gating) * lifted).astype(jnp.bfloat16)
    return jnp.dot(hidden, down_proj, preferred_element_type=jnp.float32).astype(jnp.bfloat16)


def by_slots(tokens, expert_ids, route_gate, gate_up, down_proj):
    tok_count, per_token = expert_ids.shape
    feature_width = tokens.shape[1]
    devices = lax.axis_size("blk")
    experts = devices // 2
    capacity = 3 * tok_count * per_token // devices
    placements = tok_count * per_token
    chosen_ids = expert_ids.reshape(placements)
    onehot = (chosen_ids[:, None] == jnp.arange(experts, dtype=jnp.int32)[None, :]).astype(
        jnp.int32
    )
    ranked = jnp.sum((jnp.cumsum(onehot, axis=0) - 1) * onehot, axis=1)
    slot_index = chosen_ids * capacity + ranked
    token_of = jnp.arange(placements, dtype=jnp.int32) // per_token
    slot_table = jnp.full((experts * capacity,), tok_count, jnp.int32).at[slot_index].set(token_of)
    outgoing = jnp.take(tokens, slot_table, axis=0, mode="fill", fill_value=0)
    outgoing = outgoing.reshape(experts, capacity, feature_width)
    doubled = jnp.repeat(outgoing, 2, axis=0)
    received = lax.all_to_all(doubled, "blk", split_axis=0, concat_axis=0, tiled=True)
    item_count = received.shape[1]
    partial_value = expert_half(received.reshape(-1, feature_width), gate_up, down_proj)
    partial_value = partial_value.reshape(devices, item_count, feature_width)
    returned_rows = lax.all_to_all(partial_value, "blk", split_axis=0, concat_axis=0, tiled=True)
    halves = returned_rows.reshape(experts, 2, capacity, feature_width).astype(jnp.float32)
    results = halves[:, 0] + halves[:, 1]
    flattened = results.reshape(experts * capacity, feature_width)
    picked = jnp.take(flattened, slot_index, axis=0)
    weighted = picked.reshape(tok_count, per_token, feature_width) * route_gate[:, :, None]
    return jnp.sum(weighted, axis=1).astype(jnp.bfloat16)


def snake(chips):
    return list(range(0, chips, 2)) + list(range(chips - 1, 0, -2))


def half_expert_kernel(heights, load, split, *refs):
    blocks, refs = refs[: len(heights)], refs[len(heights) :]
    if load:
        (gate_up_far, down_far), refs = refs[:2], refs[2:]
        outs, (gate_up_ref, down_ref, rows, hidden, arrived) = refs[:split], refs[split:]
    else:
        (gate_up_ref, down_ref), outs, (rows, hidden) = refs[:2], refs[2:-2], refs[-2:]
    units, width = down_ref.shape
    tile = 256 if units % 256 == 0 else units
    tiles = units // tile
    copies = []
    if load:
        for t in range(tiles):
            near = pl.ds(t * tile, tile)
            copies.append(pltpu.make_async_copy(gate_up_far.at[:, near], gate_up_ref.at[:, near], arrived.at[t]))
        copies.append(pltpu.make_async_copy(down_far, down_ref, arrived.at[tiles]))
        for copy in copies:
            copy.start()

    at = 0
    for block, height in zip(blocks, heights):
        rows[at : at + height, :] = block[:height, :]
        at += height

    contract = (((1,), (1,)), ((), ()))
    taken = rows[...]
    for t in range(tiles):
        if load:
            copies[t].wait()
        near = slice(t * tile, (t + 1) * tile)
        gating = lax.dot_general(taken, gate_up_ref[0, near], contract, preferred_element_type=jnp.float32)
        lifted = lax.dot_general(taken, gate_up_ref[1, near], contract, preferred_element_type=jnp.float32)
        hidden[:, near] = (gating / (1.0 + jnp.exp(-gating)) * lifted).astype(jnp.bfloat16)
    if load:
        copies[tiles].wait()
    inner = hidden[...]
    share = outs[0].shape[0]
    tile = 512 if width % 512 == 0 else width
    for low in range(0, width, tile):
        product = jnp.dot(inner, down_ref[:, low : low + tile], preferred_element_type=jnp.float32)
        product = product.astype(jnp.bfloat16)
        for i, out in enumerate(outs):
            out[:, low : low + tile] = product[i * share : (i + 1) * share]


def load_kernel(*refs):
    copies = [pltpu.make_async_copy(far, near, refs[4].at[i]) for i, (far, near) in enumerate(zip(refs[:2], refs[2:4]))]
    for copy in copies:
        copy.start()
    for copy in copies:
        copy.wait()


def loaded(*weights):
    return pl.pallas_call(
        load_kernel,
        out_shape=[jax.ShapeDtypeStruct(array.shape, array.dtype) for array in weights],
        in_specs=[pl.BlockSpec(memory_space=pltpu.HBM)] * 2,
        out_specs=[pl.BlockSpec(memory_space=pltpu.VMEM)] * 2,
        scratch_shapes=[pltpu.SemaphoreType.DMA((2,))],
        compiler_params=pltpu.CompilerParams(vmem_limit_bytes=38 << 20),
        cost_estimate=pl.CostEstimate(flops=1 << 28, bytes_accessed=1 << 20, transcendentals=0),
    )(*weights)


def widen_kernel(gates, out):
    out[...] = jnp.concatenate([gates[...], jnp.zeros((GATE_ROWS, out.shape[1] - gates.shape[1]), out.dtype)], axis=1)


def widened(own, other, width):
    whole = pl.BlockSpec(memory_space=pltpu.VMEM)
    wide = pl.pallas_call(
        widen_kernel,
        out_shape=jax.ShapeDtypeStruct((GATE_ROWS, width), own.dtype),
        in_specs=[whole],
        out_specs=whole,
        compiler_params=pltpu.CompilerParams(vmem_limit_bytes=8 << 20),
        cost_estimate=pl.CostEstimate(flops=1 << 28, bytes_accessed=1 << 20, transcendentals=0),
    )(own)
    size = own.shape[1]
    return jnp.concatenate([wide[:, :size], other, wide[:, 2 * size :]], axis=1)


def half_expert(heights, blocks, weights, load=False, cost=2, split=2):
    height = sum(heights)
    units, width = weights[1].shape
    whole = pl.BlockSpec(memory_space=pltpu.VMEM)
    far = pl.BlockSpec(memory_space=pltpu.HBM)
    outs = [jax.ShapeDtypeStruct((height // split, width), jnp.bfloat16)] * split
    scratch = [pltpu.VMEM((height, width), jnp.bfloat16), pltpu.VMEM((height, units), jnp.bfloat16)]
    if load:
        outs += [jax.ShapeDtypeStruct(array.shape, array.dtype) for array in weights]
        scratch.append(pltpu.SemaphoreType.DMA((units // 256 + 1 if units % 256 == 0 else 2,)))
    return pl.pallas_call(
        functools.partial(half_expert_kernel, tuple(heights), load, split),
        out_shape=outs,
        in_specs=[whole] * len(blocks) + [far if load else whole] * 2,
        out_specs=[whole] * len(outs),
        scratch_shapes=scratch,
        compiler_params=pltpu.CompilerParams(vmem_limit_bytes=(34 if load else 14) << 20),
        cost_estimate=pl.CostEstimate(
            flops=int(cost * height * units * width),
            bytes_accessed=int(cost * units * width),
            transcendentals=0,
        ),
    )(*blocks, *weights)


def weighted_kernel(kind, own, distant, experts_ref, holder, *refs):
    *terms, out = refs
    rows = out.shape[0]
    last = holder.shape[0] - GATE_ROWS
    near, far = (holder[last:, (2 * kind + i) * LANES : (2 * kind + i + 1) * LANES].astype(jnp.float32) for i in (0, 1))

    def weight(place):
        wanted = lax.broadcasted_iota(jnp.int32, near.shape, 0) == experts_ref[place]
        line = jnp.sum(jnp.where(wanted, near + far, 0.0), axis=0, keepdims=True)
        return jnp.broadcast_to(line, near.shape).T[:rows, :1]

    def total(blocks):
        return sum(block[...].astype(jnp.float32) for block in blocks)

    value = weight(0) * total(terms[:own])
    if distant:
        value += weight(1) * total(terms[own : own + distant])
    if own + distant < len(terms):
        value += total(terms[own + distant :])
    out[...] = value.astype(out.dtype)


def weighted(experts, holder, kind, own, distant=(), plain=(), dtype=jnp.bfloat16):
    whole = pl.BlockSpec(memory_space=pltpu.VMEM)
    terms = [*own, *distant, *plain]
    size = own[0].size
    return pl.pallas_call(
        functools.partial(weighted_kernel, kind, len(own), len(distant)),
        out_shape=jax.ShapeDtypeStruct(own[0].shape, dtype),
        in_specs=[pl.BlockSpec(memory_space=pltpu.SMEM)] + [whole] * (1 + len(terms)),
        out_specs=whole,
        compiler_params=pltpu.CompilerParams(vmem_limit_bytes=10 << 20),
        cost_estimate=pl.CostEstimate(flops=size * 20000, bytes_accessed=size, transcendentals=0),
    )(experts, holder, *terms)


def by_tokens(tokens, expert_ids, route_gate, gate_up, down_proj):
    chips = lax.axis_size("blk") // 2
    order, far = snake(chips), chips // 2
    rows = tokens.shape[0]
    half = rows // 2
    chains = (0, 1)

    def moved(steps, swap=False):
        pairs = []
        for place in range(chips):
            for core in (0, 1):
                target = order[(place + steps * (1 - 2 * core)) % chips]
                pairs.append((2 * order[place] + core, 2 * target + (1 - core if swap else core)))
        return pairs

    forth, back, across, cores = moved(1), moved(-1), moved(-1, True), moved(0, True)

    def send(value, pairs, name):
        with jax.named_scope(name):
            return lax.ppermute(value, "blk", pairs)

    def total(*terms):
        return sum(term.astype(jnp.float32) for term in terms)

    def rounded(value):
        return value.astype(jnp.bfloat16)

    def after(value, *earlier):
        return lax.optimization_barrier((value, *earlier))[0]

    table = np.zeros((2 * chips, 2), np.int32)
    for place in range(chips):
        for core in (0, 1):
            table[2 * order[place] + core] = order[place], order[(place + 1 - 2 * core) % chips]
    expert = lax.dynamic_index_in_dim(jnp.asarray(table), lax.axis_index("blk"), 0, keepdims=False)
    ring = [send(tokens, forth, "ring_1_0"), None]
    others = send(tokens, cores, "swap_0_0")
    chosen = jnp.arange(GATE_ROWS, dtype=jnp.int32)[:, None, None] == expert_ids.T[None]
    weight = jnp.sum(jnp.where(chosen, route_gate.T[None], 0.0), axis=1)
    high = lax.reduce_precision(weight, 8, 7)
    gates = jnp.concatenate([high, weight - high], axis=1).astype(jnp.bfloat16)
    packed = jnp.concatenate([others, widened(gates, send(gates, cores, "swap_0_1"), tokens.shape[1])])
    ring[1] = send(packed, forth, "ring_1_1")

    near = loaded(after(gate_up, expert), down_proj)
    ring[0] = after(ring[0], near[1])
    results, holders = {}, {0: packed}
    with jax.named_scope("expert_0"):
        own, given = half_expert([rows] * 2, [after(tokens, ring[0]), packed], near)
    results[0, 0] = own, given
    ring[1] = after(ring[1], own)

    def expert_rows(step, c, inputs, **options):
        with jax.named_scope(f"expert_{step}_{c}"):
            results[step, c] = half_expert([rows] * 2, inputs, near, **options)
        if step == far - 1 or (step, c) == (1, 1):
            give(step, c)
        return results[step, c][0]

    def give(step, c, *earlier):
        kept, given = results[step, c]
        results[step, c] = kept, send(after(given, *earlier) if earlier else given, cores, f"give_{step}_{c}")

    earlier = ring[1]
    for step in range(1, far):
        holders[step] = ring[1]
        swapped = [
            send(block, cores, f"swap_{step}_{c}") for c, block in enumerate(ring[: 1 if step == 1 else 2])
        ]
        blocks = list(ring)
        if step < far - 1:
            ring = [send(block, forth, f"ring_{step + 1}_{c}") for c, block in enumerate(ring)]
        else:
            ring = [send(ring[0], forth, f"ring_{far}_0")]
        for c in chains:
            if (step, c) == (1, 1):
                delayed = blocks[1]
                earlier = ring[1]
                continue
            if (step, c) == (far - 1, 1):
                last = blocks[1], swapped[1]
                continue
            kept = expert_rows(step, c, [after(blocks[c], earlier), swapped[c]])
            place = c if step < far - 1 else 0
            ring[place] = after(ring[place], kept)
            earlier = ring[place]

    with jax.named_scope("expert_far_ring"):
        (given,) = half_expert([rows], ring, near, split=1)
    swapped = send(ring[0], cores, f"swap_{far}")
    mine, theirs = results[far - 1, 0]
    earlier = weighted(expert, holders[far - 1], 0, [after(mine, given), theirs])
    sums = [send(earlier, back, f"back_{far - 1}_0")]
    swapped = after(swapped, earlier)
    given = send(given, cores, "give_far")
    with jax.named_scope("expert_far_swapped"):
        (kept,) = half_expert([rows], [swapped], near, split=1)
    earlier = rounded(total(kept, given))
    sums.append(send(earlier, back, f"back_{far}_1"))
    earlier = expert_rows(far - 1, 1, [after(last[0], earlier), last[1]], cost=0.2)
    for step in range(far - 2, 1, -1):
        for c in chains:
            give(step, c, earlier)
    swapped = send(after(delayed, earlier), cores, "swap_1_1")
    steps = [(step, c) for step in range(far - 1, 0, -1) for c in chains][1:]
    for order_place in range(0, len(steps) - 1, 2):
        steps[order_place : order_place + 2] = steps[order_place : order_place + 2][::-1]
    for step, c in steps:
        mine, theirs = results[step, c]
        far_sum = (step, c) == (far - 1, 1)
        mine = after(mine, earlier, sums[0]) if (step, c) == (1, 1) else after(mine, earlier)
        if far_sum:
            part = weighted(expert, holders[step], c, [mine], [sums[c]], dtype=jnp.float32)
            earlier = weighted(expert, holders[step], c, [after(theirs, part)], plain=[part])
        else:
            earlier = weighted(expert, holders[step], c, [mine, theirs], plain=[sums[c]])
        sums[c] = send(earlier, across if (step, c) == (1, 1) else back, f"back_{step}_{c}")
        if (step, c) == (far - 2, 0):
            give(1, 0, earlier)
        if far_sum:
            give(0, 0, earlier)
            earlier = expert_rows(1, 1, [after(delayed, earlier), swapped])
    own = weighted(expert, packed, 0, results[0, 0], plain=[sums[0]], dtype=jnp.float32)
    return rounded(total(own, sums[1]))


def solution(mesh):
    placed = (
        P(("groups", "blk"), None),
        P(("groups", "blk"), None),
        P(("groups", "blk"), None),
        P(None, "blk", None),
        P("blk", None),
    )

    def per_device(tokens, expert_ids, route_gate, gate_up, down_proj):
        experts = mesh.shape["blk"] // 2
        dense = experts <= min(GATE_ROWS, 2 * expert_ids.shape[1]) and tokens.shape[0] == LANES
        body = by_tokens if dense else by_slots
        return body(tokens, expert_ids, route_gate, gate_up, down_proj)

    return jax.shard_map(
        per_device,
        mesh=mesh,
        in_specs=placed,
        out_specs=P(("groups", "blk"), None),
        check_vma=False,
    )
```

```python
import functools

import jax
import jax.numpy as jnp
import numpy as np
from jax import lax
from jax.experimental import pallas as pl
from jax.experimental.pallas import tpu as pltpu
from jax.sharding import PartitionSpec as P

GATE_ROWS, LANES = 8, 128


def expert_half(slot_block, gate_up, down_proj):
    contract = (((1,), (1,)), ((), ()))
    gating = lax.dot_general(slot_block, gate_up[0], contract, preferred_element_type=jnp.float32)
    lifted = lax.dot_general(slot_block, gate_up[1], contract, preferred_element_type=jnp.float32)
    hidden = (jax.nn.silu(gating) * lifted).astype(jnp.bfloat16)
    return jnp.dot(hidden, down_proj, preferred_element_type=jnp.float32).astype(jnp.bfloat16)


def by_slots(tokens, expert_ids, route_gate, gate_up, down_proj):
    tok_count, per_token = expert_ids.shape
    feature_width = tokens.shape[1]
    devices = lax.axis_size("blk")
    experts = devices // 2
    capacity = 3 * tok_count * per_token // devices
    placements = tok_count * per_token
    chosen_ids = expert_ids.reshape(placements)
    onehot = (chosen_ids[:, None] == jnp.arange(experts, dtype=jnp.int32)[None, :]).astype(
        jnp.int32
    )
    ranked = jnp.sum((jnp.cumsum(onehot, axis=0) - 1) * onehot, axis=1)
    slot_index = chosen_ids * capacity + ranked
    token_of = jnp.arange(placements, dtype=jnp.int32) // per_token
    slot_table = jnp.full((experts * capacity,), tok_count, jnp.int32).at[slot_index].set(token_of)
    outgoing = jnp.take(tokens, slot_table, axis=0, mode="fill", fill_value=0)
    outgoing = outgoing.reshape(experts, capacity, feature_width)
    doubled = jnp.repeat(outgoing, 2, axis=0)
    received = lax.all_to_all(doubled, "blk", split_axis=0, concat_axis=0, tiled=True)
    item_count = received.shape[1]
    partial_value = expert_half(received.reshape(-1, feature_width), gate_up, down_proj)
    partial_value = partial_value.reshape(devices, item_count, feature_width)
    returned_rows = lax.all_to_all(partial_value, "blk", split_axis=0, concat_axis=0, tiled=True)
    halves = returned_rows.reshape(experts, 2, capacity, feature_width).astype(jnp.float32)
    results = halves[:, 0] + halves[:, 1]
    flattened = results.reshape(experts * capacity, feature_width)
    picked = jnp.take(flattened, slot_index, axis=0)
    weighted = picked.reshape(tok_count, per_token, feature_width) * route_gate[:, :, None]
    return jnp.sum(weighted, axis=1).astype(jnp.bfloat16)


def snake(chips):
    return list(range(0, chips, 2)) + list(range(chips - 1, 0, -2))


def half_expert_kernel(heights, load, split, *refs):
    blocks, refs = refs[: len(heights)], refs[len(heights) :]
    if load:
        (gate_up_far, down_far), refs = refs[:2], refs[2:]
        outs, (gate_up_ref, down_ref, rows, hidden, arrived) = refs[:split], refs[split:]
    else:
        (gate_up_ref, down_ref), outs, (rows, hidden) = refs[:2], refs[2:-2], refs[-2:]
    units, width = down_ref.shape
    tile = 256 if units % 256 == 0 else units
    tiles = units // tile
    copies = []
    if load:
        for t in range(tiles):
            near = pl.ds(t * tile, tile)
            copies.append(pltpu.make_async_copy(gate_up_far.at[:, near], gate_up_ref.at[:, near], arrived.at[t]))
        copies.append(pltpu.make_async_copy(down_far, down_ref, arrived.at[tiles]))
        for copy in copies:
            copy.start()

    at = 0
    for block, height in zip(blocks, heights):
        rows[at : at + height, :] = block[:height, :]
        at += height

    contract = (((1,), (1,)), ((), ()))
    taken = rows[...]
    for t in range(tiles):
        if load:
            copies[t].wait()
        near = slice(t * tile, (t + 1) * tile)
        gating = lax.dot_general(taken, gate_up_ref[0, near], contract, preferred_element_type=jnp.float32)
        lifted = lax.dot_general(taken, gate_up_ref[1, near], contract, preferred_element_type=jnp.float32)
        hidden[:, near] = (gating / (1.0 + jnp.exp(-gating)) * lifted).astype(jnp.bfloat16)
    if load:
        copies[tiles].wait()
    inner = hidden[...]
    share = outs[0].shape[0]
    tile = 512 if width % 512 == 0 else width
    for low in range(0, width, tile):
        product = jnp.dot(inner, down_ref[:, low : low + tile], preferred_element_type=jnp.float32)
        product = product.astype(jnp.bfloat16)
        for i, out in enumerate(outs):
            out[:, low : low + tile] = product[i * share : (i + 1) * share]


def load_kernel(*refs):
    copies = [pltpu.make_async_copy(far, near, refs[4].at[i]) for i, (far, near) in enumerate(zip(refs[:2], refs[2:4]))]
    for copy in copies:
        copy.start()
    for copy in copies:
        copy.wait()


def loaded(*weights):
    return pl.pallas_call(
        load_kernel,
        out_shape=[jax.ShapeDtypeStruct(array.shape, array.dtype) for array in weights],
        in_specs=[pl.BlockSpec(memory_space=pltpu.HBM)] * 2,
        out_specs=[pl.BlockSpec(memory_space=pltpu.VMEM)] * 2,
        scratch_shapes=[pltpu.SemaphoreType.DMA((2,))],
        compiler_params=pltpu.CompilerParams(vmem_limit_bytes=38 << 20),
        cost_estimate=pl.CostEstimate(flops=1 << 28, bytes_accessed=1 << 20, transcendentals=0),
    )(*weights)


def widen_kernel(gates, out):
    out[...] = jnp.concatenate([gates[...], jnp.zeros((GATE_ROWS, out.shape[1] - gates.shape[1]), out.dtype)], axis=1)


def widened(own, other, width):
    whole = pl.BlockSpec(memory_space=pltpu.VMEM)
    wide = pl.pallas_call(
        widen_kernel,
        out_shape=jax.ShapeDtypeStruct((GATE_ROWS, width), own.dtype),
        in_specs=[whole],
        out_specs=whole,
        compiler_params=pltpu.CompilerParams(vmem_limit_bytes=8 << 20),
        cost_estimate=pl.CostEstimate(flops=1 << 28, bytes_accessed=1 << 20, transcendentals=0),
    )(own)
    size = own.shape[1]
    return jnp.concatenate([wide[:, :size], other, wide[:, 2 * size :]], axis=1)


def half_expert(heights, blocks, weights, load=False, cost=2, split=2):
    height = sum(heights)
    units, width = weights[1].shape
    whole = pl.BlockSpec(memory_space=pltpu.VMEM)
    far = pl.BlockSpec(memory_space=pltpu.HBM)
    outs = [jax.ShapeDtypeStruct((height // split, width), jnp.bfloat16)] * split
    scratch = [pltpu.VMEM((height, width), jnp.bfloat16), pltpu.VMEM((height, units), jnp.bfloat16)]
    if load:
        outs += [jax.ShapeDtypeStruct(array.shape, array.dtype) for array in weights]
        scratch.append(pltpu.SemaphoreType.DMA((units // 256 + 1 if units % 256 == 0 else 2,)))
    return pl.pallas_call(
        functools.partial(half_expert_kernel, tuple(heights), load, split),
        out_shape=outs,
        in_specs=[whole] * len(blocks) + [far if load else whole] * 2,
        out_specs=[whole] * len(outs),
        scratch_shapes=scratch,
        compiler_params=pltpu.CompilerParams(vmem_limit_bytes=(34 if load else 14) << 20),
        cost_estimate=pl.CostEstimate(
            flops=int(cost * height * units * width),
            bytes_accessed=int(cost * units * width),
            transcendentals=0,
        ),
    )(*blocks, *weights)


def weighted_kernel(kind, own, distant, *refs):
    experts, holder, terms, out = refs[: 1 + bool(distant)], refs[1 + bool(distant)], refs[2 + bool(distant) : -1], refs[-1]
    rows = out.shape[0]
    last = holder.shape[0] - GATE_ROWS
    near, far = (holder[last:, (2 * kind + i) * LANES : (2 * kind + i + 1) * LANES].astype(jnp.float32) for i in (0, 1))

    def weight(place):
        wanted = lax.broadcasted_iota(jnp.int32, near.shape, 0) == experts[place][0]
        line = jnp.sum(jnp.where(wanted, near + far, 0.0), axis=0, keepdims=True)
        return jnp.broadcast_to(line, near.shape).T[:rows, :1]

    def total(blocks):
        return sum(block[...].astype(jnp.float32) for block in blocks)

    value = weight(0) * total(terms[:own])
    if distant:
        value += weight(1) * total(terms[own : own + distant])
    if own + distant < len(terms):
        value += total(terms[own + distant :])
    out[...] = value.astype(out.dtype)


def weighted(experts, holder, kind, own, distant=(), plain=(), dtype=jnp.bfloat16):
    whole = pl.BlockSpec(memory_space=pltpu.VMEM)
    terms = [*own, *distant, *plain]
    experts = experts[: 1 + bool(distant)]
    size = own[0].size
    return pl.pallas_call(
        functools.partial(weighted_kernel, kind, len(own), len(distant)),
        out_shape=jax.ShapeDtypeStruct(own[0].shape, dtype),
        in_specs=[pl.BlockSpec(memory_space=pltpu.SMEM)] * len(experts) + [whole] * (1 + len(terms)),
        out_specs=whole,
        compiler_params=pltpu.CompilerParams(vmem_limit_bytes=10 << 20),
        cost_estimate=pl.CostEstimate(flops=size * 20000, bytes_accessed=size, transcendentals=0),
    )(*experts, holder, *terms)


def by_tokens(tokens, expert_ids, route_gate, gate_up, down_proj):
    chips = lax.axis_size("blk") // 2
    order, far = snake(chips), chips // 2
    rows = tokens.shape[0]
    half = rows // 2
    chains = (0, 1)

    def moved(steps, swap=False):
        pairs = []
        for place in range(chips):
            for core in (0, 1):
                target = order[(place + steps * (1 - 2 * core)) % chips]
                pairs.append((2 * order[place] + core, 2 * target + (1 - core if swap else core)))
        return pairs

    forth, back, across, cores = moved(1), moved(-1), moved(-1, True), moved(0, True)

    def send(value, pairs, name):
        with jax.named_scope(name):
            return lax.ppermute(value, "blk", pairs)

    def total(*terms):
        return sum(term.astype(jnp.float32) for term in terms)

    def rounded(value):
        return value.astype(jnp.bfloat16)

    def after(value, *earlier):
        return lax.optimization_barrier((value, *earlier))[0]

    device = lax.axis_index("blk").astype(jnp.int32)
    chip, core = jnp.right_shift(device, 1), jnp.bitwise_and(device, 1)
    odd = jnp.bitwise_and(chip, 1)
    place = jnp.where(odd == 1, chips - 1 - jnp.right_shift(chip, 1), jnp.right_shift(chip, 1))
    ahead = place + 1 - 2 * core
    ahead = jnp.where(ahead < 0, chips - 1, jnp.where(ahead == chips, 0, ahead))
    ahead = jnp.where(ahead < far, 2 * ahead, 2 * (chips - 1 - ahead) + 1)
    expert = [chip.reshape(1), ahead.reshape(1)]
    ring = [send(tokens, forth, "ring_1_0"), None]
    others = send(tokens, cores, "swap_0_0")
    chosen = jnp.arange(GATE_ROWS, dtype=jnp.int32)[:, None, None] == expert_ids.T[None]
    weight = jnp.sum(jnp.where(chosen, route_gate.T[None], 0.0), axis=1)
    high = lax.reduce_precision(weight, 8, 7)
    gates = jnp.concatenate([high, weight - high], axis=1).astype(jnp.bfloat16)
    packed = jnp.concatenate([others, widened(gates, send(gates, cores, "swap_0_1"), tokens.shape[1])])
    ring[1] = send(packed, forth, "ring_1_1")

    near = loaded(after(gate_up, *expert), down_proj)
    ring[0] = after(ring[0], near[1])
    results, holders = {}, {0: packed}
    with jax.named_scope("expert_0"):
        own, given = half_expert([rows] * 2, [after(tokens, ring[0]), packed], near)
    results[0, 0] = own, given
    ring[1] = after(ring[1], own)

    def expert_rows(step, c, inputs, **options):
        with jax.named_scope(f"expert_{step}_{c}"):
            results[step, c] = half_expert([rows] * 2, inputs, near, **options)
        if step == far - 1 or (step, c) == (1, 1):
            give(step, c)
        return results[step, c][0]

    def give(step, c, *earlier):
        kept, given = results[step, c]
        results[step, c] = kept, send(after(given, *earlier) if earlier else given, cores, f"give_{step}_{c}")

    earlier = ring[1]
    for step in range(1, far):
        holders[step] = ring[1]
        swapped = [
            send(block, cores, f"swap_{step}_{c}") for c, block in enumerate(ring[: 1 if step == 1 else 2])
        ]
        blocks = list(ring)
        if step < far - 1:
            ring = [send(block, forth, f"ring_{step + 1}_{c}") for c, block in enumerate(ring)]
        else:
            ring = [send(ring[0], forth, f"ring_{far}_0")]
        for c in chains:
            if (step, c) == (1, 1):
                delayed = blocks[1]
                earlier = ring[1]
                continue
            if (step, c) == (far - 1, 1):
                last = blocks[1], swapped[1]
                continue
            kept = expert_rows(step, c, [after(blocks[c], earlier), swapped[c]])
            place = c if step < far - 1 else 0
            ring[place] = after(ring[place], kept)
            earlier = ring[place]

    with jax.named_scope("expert_far_ring"):
        (given,) = half_expert([rows], ring, near, split=1)
    swapped = send(ring[0], cores, f"swap_{far}")
    swapped = after(swapped, given)
    given = send(given, cores, "give_far")
    with jax.named_scope("expert_far_swapped"):
        (kept,) = half_expert([rows], [swapped], near, split=1)
    earlier = rounded(total(kept, given))
    sums = [None, send(earlier, back, f"back_{far}_1")]
    mine, theirs = results[far - 1, 0]
    earlier = weighted(expert, holders[far - 1], 0, [after(mine, earlier), theirs])
    sums[0] = send(earlier, back, f"back_{far - 1}_0")
    earlier = expert_rows(far - 1, 1, [after(last[0], earlier), last[1]], cost=0.2)
    for step in range(far - 2, 1, -1):
        for c in chains:
            give(step, c, earlier)
    swapped = send(after(delayed, earlier), cores, "swap_1_1")
    steps = [(step, c) for step in range(far - 1, 0, -1) for c in chains][1:]
    for step, c in steps:
        mine, theirs = results[step, c]
        far_sum = (step, c) == (far - 1, 1)
        mine = after(mine, earlier)
        if far_sum:
            part = weighted(expert, holders[step], c, [mine], [sums[c]], dtype=jnp.float32)
            earlier = weighted(expert, holders[step], c, [after(theirs, part)], plain=[part])
        else:
            earlier = weighted(expert, holders[step], c, [mine, theirs], plain=[sums[c]])
        sums[c] = send(earlier, across if (step, c) == (1, 1) else back, f"back_{step}_{c}")
        if (step, c) == (far - 2, 0):
            give(1, 0, earlier)
        if far_sum:
            give(0, 0, earlier)
            earlier = expert_rows(1, 1, [after(delayed, earlier), swapped])
    own = weighted(expert, packed, 0, results[0, 0], plain=[sums[0]], dtype=jnp.float32)
    return rounded(total(own, sums[1]))


def solution(mesh):
    placed = (
        P(("groups", "blk"), None),
        P(("groups", "blk"), None),
        P(("groups", "blk"), None),
        P(None, "blk", None),
        P("blk", None),
    )

    def per_device(tokens, expert_ids, route_gate, gate_up, down_proj):
        experts = mesh.shape["blk"] // 2
        dense = experts <= min(GATE_ROWS, 2 * expert_ids.shape[1]) and tokens.shape[0] == LANES
        body = by_tokens if dense else by_slots
        return body(tokens, expert_ids, route_gate, gate_up, down_proj)

    return jax.shard_map(
        per_device,
        mesh=mesh,
        in_specs=placed,
        out_specs=P(("groups", "blk"), None),
        check_vma=False,
    )
```

```python
import functools

import jax
import jax.numpy as jnp
import numpy as np
from jax import lax
from jax.experimental import pallas as pl
from jax.experimental.pallas import tpu as pltpu
from jax.sharding import PartitionSpec as P

GATE_ROWS, LANES = 8, 128


def expert_half(slot_block, gate_up, down_proj):
    contract = (((1,), (1,)), ((), ()))
    gating = lax.dot_general(slot_block, gate_up[0], contract, preferred_element_type=jnp.float32)
    lifted = lax.dot_general(slot_block, gate_up[1], contract, preferred_element_type=jnp.float32)
    hidden = (jax.nn.silu(gating) * lifted).astype(jnp.bfloat16)
    return jnp.dot(hidden, down_proj, preferred_element_type=jnp.float32).astype(jnp.bfloat16)


def by_slots(tokens, expert_ids, route_gate, gate_up, down_proj):
    tok_count, per_token = expert_ids.shape
    feature_width = tokens.shape[1]
    devices = lax.axis_size("blk")
    experts = devices // 2
    capacity = 3 * tok_count * per_token // devices
    placements = tok_count * per_token
    chosen_ids = expert_ids.reshape(placements)
    onehot = (chosen_ids[:, None] == jnp.arange(experts, dtype=jnp.int32)[None, :]).astype(
        jnp.int32
    )
    ranked = jnp.sum((jnp.cumsum(onehot, axis=0) - 1) * onehot, axis=1)
    slot_index = chosen_ids * capacity + ranked
    token_of = jnp.arange(placements, dtype=jnp.int32) // per_token
    slot_table = jnp.full((experts * capacity,), tok_count, jnp.int32).at[slot_index].set(token_of)
    outgoing = jnp.take(tokens, slot_table, axis=0, mode="fill", fill_value=0)
    outgoing = outgoing.reshape(experts, capacity, feature_width)
    doubled = jnp.repeat(outgoing, 2, axis=0)
    received = lax.all_to_all(doubled, "blk", split_axis=0, concat_axis=0, tiled=True)
    item_count = received.shape[1]
    partial_value = expert_half(received.reshape(-1, feature_width), gate_up, down_proj)
    partial_value = partial_value.reshape(devices, item_count, feature_width)
    returned_rows = lax.all_to_all(partial_value, "blk", split_axis=0, concat_axis=0, tiled=True)
    halves = returned_rows.reshape(experts, 2, capacity, feature_width).astype(jnp.float32)
    results = halves[:, 0] + halves[:, 1]
    flattened = results.reshape(experts * capacity, feature_width)
    picked = jnp.take(flattened, slot_index, axis=0)
    weighted = picked.reshape(tok_count, per_token, feature_width) * route_gate[:, :, None]
    return jnp.sum(weighted, axis=1).astype(jnp.bfloat16)


def snake(chips):
    return list(range(0, chips, 2)) + list(range(chips - 1, 0, -2))


def half_expert_kernel(heights, load, split, *refs):
    blocks, refs = refs[: len(heights)], refs[len(heights) :]
    if load:
        (gate_up_far, down_far), refs = refs[:2], refs[2:]
        outs, (gate_up_ref, down_ref, rows, hidden, arrived) = refs[:split], refs[split:]
    else:
        (gate_up_ref, down_ref), outs, (rows, hidden) = refs[:2], refs[2:-2], refs[-2:]
    units, width = down_ref.shape
    tile = 256 if units % 256 == 0 else units
    tiles = units // tile
    copies = []
    if load:
        for t in range(tiles):
            near = pl.ds(t * tile, tile)
            copies.append(pltpu.make_async_copy(gate_up_far.at[:, near], gate_up_ref.at[:, near], arrived.at[t]))
        copies.append(pltpu.make_async_copy(down_far, down_ref, arrived.at[tiles]))
        for copy in copies:
            copy.start()

    at = 0
    for block, height in zip(blocks, heights):
        rows[at : at + height, :] = block[:height, :]
        at += height

    contract = (((1,), (1,)), ((), ()))
    taken = rows[...]
    for t in range(tiles):
        if load:
            copies[t].wait()
        near = slice(t * tile, (t + 1) * tile)
        gating = lax.dot_general(taken, gate_up_ref[0, near], contract, preferred_element_type=jnp.float32)
        lifted = lax.dot_general(taken, gate_up_ref[1, near], contract, preferred_element_type=jnp.float32)
        hidden[:, near] = (gating / (1.0 + jnp.exp(-gating)) * lifted).astype(jnp.bfloat16)
    if load:
        copies[tiles].wait()
    inner = hidden[...]
    share = outs[0].shape[0]
    tile = 512 if width % 512 == 0 else width
    for low in range(0, width, tile):
        product = jnp.dot(inner, down_ref[:, low : low + tile], preferred_element_type=jnp.float32)
        product = product.astype(jnp.bfloat16)
        for i, out in enumerate(outs):
            out[:, low : low + tile] = product[i * share : (i + 1) * share]


def load_kernel(*refs):
    copies = [pltpu.make_async_copy(far, near, refs[4].at[i]) for i, (far, near) in enumerate(zip(refs[:2], refs[2:4]))]
    for copy in copies:
        copy.start()
    for copy in copies:
        copy.wait()


def loaded(*weights):
    return pl.pallas_call(
        load_kernel,
        out_shape=[jax.ShapeDtypeStruct(array.shape, array.dtype) for array in weights],
        in_specs=[pl.BlockSpec(memory_space=pltpu.HBM)] * 2,
        out_specs=[pl.BlockSpec(memory_space=pltpu.VMEM)] * 2,
        scratch_shapes=[pltpu.SemaphoreType.DMA((2,))],
        compiler_params=pltpu.CompilerParams(vmem_limit_bytes=38 << 20),
        cost_estimate=pl.CostEstimate(flops=1 << 28, bytes_accessed=1 << 20, transcendentals=0),
    )(*weights)


def widen_kernel(gates, out):
    out[...] = jnp.concatenate([gates[...], jnp.zeros((GATE_ROWS, out.shape[1] - gates.shape[1]), out.dtype)], axis=1)


def widened(own, other, width):
    whole = pl.BlockSpec(memory_space=pltpu.VMEM)
    wide = pl.pallas_call(
        widen_kernel,
        out_shape=jax.ShapeDtypeStruct((GATE_ROWS, width), own.dtype),
        in_specs=[whole],
        out_specs=whole,
        compiler_params=pltpu.CompilerParams(vmem_limit_bytes=8 << 20),
        cost_estimate=pl.CostEstimate(flops=1 << 28, bytes_accessed=1 << 20, transcendentals=0),
    )(own)
    size = own.shape[1]
    return jnp.concatenate([wide[:, :size], other, wide[:, 2 * size :]], axis=1)


def half_expert(heights, blocks, weights, load=False, cost=2, split=2):
    height = sum(heights)
    units, width = weights[1].shape
    whole = pl.BlockSpec(memory_space=pltpu.VMEM)
    far = pl.BlockSpec(memory_space=pltpu.HBM)
    outs = [jax.ShapeDtypeStruct((height // split, width), jnp.bfloat16)] * split
    scratch = [pltpu.VMEM((height, width), jnp.bfloat16), pltpu.VMEM((height, units), jnp.bfloat16)]
    if load:
        outs += [jax.ShapeDtypeStruct(array.shape, array.dtype) for array in weights]
        scratch.append(pltpu.SemaphoreType.DMA((units // 256 + 1 if units % 256 == 0 else 2,)))
    return pl.pallas_call(
        functools.partial(half_expert_kernel, tuple(heights), load, split),
        out_shape=outs,
        in_specs=[whole] * len(blocks) + [far if load else whole] * 2,
        out_specs=[whole] * len(outs),
        scratch_shapes=scratch,
        compiler_params=pltpu.CompilerParams(vmem_limit_bytes=(34 if load else 14) << 20),
        cost_estimate=pl.CostEstimate(
            flops=int(cost * height * units * width),
            bytes_accessed=int(cost * units * width),
            transcendentals=0,
        ),
    )(*blocks, *weights)


def weighted_kernel(kind, own, distant, *refs):
    experts, holder, terms, out = refs[: 1 + bool(distant)], refs[1 + bool(distant)], refs[2 + bool(distant) : -1], refs[-1]
    rows = out.shape[0]
    last = holder.shape[0] - GATE_ROWS
    near, far = (holder[last:, (2 * kind + i) * LANES : (2 * kind + i + 1) * LANES].astype(jnp.float32) for i in (0, 1))

    def weight(place):
        wanted = lax.broadcasted_iota(jnp.int32, near.shape, 0) == experts[place][0]
        line = jnp.sum(jnp.where(wanted, near + far, 0.0), axis=0, keepdims=True)
        return jnp.broadcast_to(line, near.shape).T[:rows, :1]

    def total(blocks):
        return sum(block[...].astype(jnp.float32) for block in blocks)

    value = weight(0) * total(terms[:own])
    if distant:
        value += weight(1) * total(terms[own : own + distant])
    if own + distant < len(terms):
        value += total(terms[own + distant :])
    out[...] = value.astype(out.dtype)


def weighted(experts, holder, kind, own, distant=(), plain=(), dtype=jnp.bfloat16):
    whole = pl.BlockSpec(memory_space=pltpu.VMEM)
    terms = [*own, *distant, *plain]
    experts = experts[: 1 + bool(distant)]
    size = own[0].size
    return pl.pallas_call(
        functools.partial(weighted_kernel, kind, len(own), len(distant)),
        out_shape=jax.ShapeDtypeStruct(own[0].shape, dtype),
        in_specs=[pl.BlockSpec(memory_space=pltpu.SMEM)] * len(experts) + [whole] * (1 + len(terms)),
        out_specs=whole,
        compiler_params=pltpu.CompilerParams(vmem_limit_bytes=10 << 20),
        cost_estimate=pl.CostEstimate(flops=size * 20000, bytes_accessed=size, transcendentals=0),
    )(*experts, holder, *terms)


def by_tokens(tokens, expert_ids, route_gate, gate_up, down_proj):
    chips = lax.axis_size("blk") // 2
    order, far = snake(chips), chips // 2
    rows = tokens.shape[0]
    half = rows // 2
    chains = (0, 1)

    def moved(steps, swap=False):
        pairs = []
        for place in range(chips):
            for core in (0, 1):
                target = order[(place + steps * (1 - 2 * core)) % chips]
                pairs.append((2 * order[place] + core, 2 * target + (1 - core if swap else core)))
        return pairs

    forth, back, across, cores = moved(1), moved(-1), moved(-1, True), moved(0, True)

    def send(value, pairs, name):
        with jax.named_scope(name):
            return lax.ppermute(value, "blk", pairs)

    def total(*terms):
        return sum(term.astype(jnp.float32) for term in terms)

    def rounded(value):
        return value.astype(jnp.bfloat16)

    def after(value, *earlier):
        return lax.optimization_barrier((value, *earlier))[0]

    device = lax.axis_index("blk").astype(jnp.int32)
    chip, core = jnp.right_shift(device, 1), jnp.bitwise_and(device, 1)
    odd = jnp.bitwise_and(chip, 1)
    place = jnp.where(odd == 1, chips - 1 - jnp.right_shift(chip, 1), jnp.right_shift(chip, 1))
    ahead = place + 1 - 2 * core
    ahead = jnp.where(ahead < 0, chips - 1, jnp.where(ahead == chips, 0, ahead))
    ahead = jnp.where(ahead < far, 2 * ahead, 2 * (chips - 1 - ahead) + 1)
    expert = [chip.reshape(1), ahead.reshape(1)]
    ring = [send(tokens, forth, "ring_1_0"), None]
    others = send(tokens, cores, "swap_0_0")
    chosen = jnp.arange(GATE_ROWS, dtype=jnp.int32)[:, None, None] == expert_ids.T[None]
    weight = jnp.sum(jnp.where(chosen, route_gate.T[None], 0.0), axis=1)
    high = lax.reduce_precision(weight, 8, 7)
    gates = jnp.concatenate([high, weight - high], axis=1).astype(jnp.bfloat16)
    packed = jnp.concatenate([others, widened(gates, send(gates, cores, "swap_0_1"), tokens.shape[1])])
    ring[1] = send(packed, forth, "ring_1_1")

    near = loaded(after(gate_up, *expert), down_proj)
    ring[0] = after(ring[0], near[1])
    results, holders = {}, {0: packed}
    with jax.named_scope("expert_0"):
        own, given = half_expert([rows] * 2, [after(tokens, ring[0]), packed], near)
    results[0, 0] = own, given
    ring[1] = after(ring[1], own)

    def expert_rows(step, c, inputs, **options):
        with jax.named_scope(f"expert_{step}_{c}"):
            results[step, c] = half_expert([rows] * 2, inputs, near, **options)
        if step == far - 1 or (step, c) == (1, 1):
            give(step, c)
        return results[step, c][0]

    def give(step, c, *earlier):
        kept, given = results[step, c]
        results[step, c] = kept, send(after(given, *earlier) if earlier else given, cores, f"give_{step}_{c}")

    earlier = ring[1]
    for step in range(1, far - 1):
        holders[step] = ring[1]
        swapped = [
            send(block, cores, f"swap_{step}_{c}") for c, block in enumerate(ring[: 1 if step == 1 else 2])
        ]
        blocks = list(ring)
        ring[0] = send(blocks[0], forth, f"ring_{step + 1}_0")
        if step < far - 2:
            ring[1] = send(blocks[1], forth, f"ring_{step + 1}_1")
        for c in chains:
            if (step, c) == (1, 1):
                delayed = blocks[1]
                earlier = ring[1]
                continue
            kept = expert_rows(step, c, [after(blocks[c], earlier), swapped[c]])
            if (step, c) == (far - 2, 1):
                ring[1] = send(after(blocks[1], kept), forth, f"ring_{step + 1}_1")
            else:
                ring[c] = after(ring[c], kept)
                earlier = ring[c]
    holders[far - 1] = blocks[1] = ring[1]
    swapped = send(ring[0], cores, f"swap_{far - 1}_0")
    block, ring = ring[0], [send(ring[0], forth, f"ring_{far}_0")]
    kept = expert_rows(far - 1, 0, [after(block, kept), swapped])
    ring[0] = after(ring[0], kept)

    with jax.named_scope("expert_far_ring"):
        (given,) = half_expert([rows], ring, near, split=1, cost=0.3)
    swapped = send(ring[0], cores, f"swap_{far}")
    swapped = after(swapped, given)
    given = send(given, cores, "give_far")
    with jax.named_scope("expert_far_swapped"):
        (kept,) = half_expert([rows], [swapped], near, split=1, cost=0.3)
    last = blocks[1], send(after(blocks[1], kept), cores, f"swap_{far - 1}_1")
    earlier = rounded(total(kept, given))
    sums = [None, send(earlier, back, f"back_{far}_1")]
    mine, theirs = results[far - 1, 0]
    earlier = weighted(expert, holders[far - 1], 0, [after(mine, earlier), theirs])
    sums[0] = send(earlier, back, f"back_{far - 1}_0")
    earlier = expert_rows(far - 1, 1, [after(last[0], earlier), last[1]], cost=0.2)
    for step in range(far - 2, 1, -1):
        for c in chains:
            give(step, c, earlier)
    swapped = send(after(delayed, earlier), cores, "swap_1_1")
    steps = [(step, c) for step in range(far - 1, 0, -1) for c in chains][1:]
    for step, c in steps:
        mine, theirs = results[step, c]
        far_sum = (step, c) == (far - 1, 1)
        mine = after(mine, earlier)
        if far_sum:
            part = weighted(expert, holders[step], c, [mine], [sums[c]], dtype=jnp.float32)
            earlier = weighted(expert, holders[step], c, [after(theirs, part)], plain=[part])
        else:
            earlier = weighted(expert, holders[step], c, [mine, theirs], plain=[sums[c]])
        sums[c] = send(earlier, across if (step, c) == (1, 1) else back, f"back_{step}_{c}")
        if (step, c) == (far - 2, 0):
            give(1, 0, earlier)
        if far_sum:
            give(0, 0, earlier)
            earlier = expert_rows(1, 1, [after(delayed, earlier), swapped])
    own = weighted(expert, packed, 0, results[0, 0], plain=[sums[0]], dtype=jnp.float32)
    return rounded(total(own, sums[1]))


def solution(mesh):
    placed = (
        P(("groups", "blk"), None),
        P(("groups", "blk"), None),
        P(("groups", "blk"), None),
        P(None, "blk", None),
        P("blk", None),
    )

    def per_device(tokens, expert_ids, route_gate, gate_up, down_proj):
        experts = mesh.shape["blk"] // 2
        dense = experts <= min(GATE_ROWS, 2 * expert_ids.shape[1]) and tokens.shape[0] == LANES
        body = by_tokens if dense else by_slots
        return body(tokens, expert_ids, route_gate, gate_up, down_proj)

    return jax.shard_map(
        per_device,
        mesh=mesh,
        in_specs=placed,
        out_specs=P(("groups", "blk"), None),
        check_vma=False,
    )
```

```python
import functools

import jax
import jax.numpy as jnp
import numpy as np
from jax import lax
from jax.experimental import pallas as pl
from jax.experimental.pallas import tpu as pltpu
from jax.sharding import PartitionSpec as P

GATE_ROWS, LANES = 16, 128


def expert_half(slot_block, gate_up, down_proj):
    contract = (((1,), (1,)), ((), ()))
    gating = lax.dot_general(slot_block, gate_up[0], contract, preferred_element_type=jnp.float32)
    lifted = lax.dot_general(slot_block, gate_up[1], contract, preferred_element_type=jnp.float32)
    hidden = (jax.nn.silu(gating) * lifted).astype(jnp.bfloat16)
    return jnp.dot(hidden, down_proj, preferred_element_type=jnp.float32).astype(jnp.bfloat16)


def by_slots(tokens, expert_ids, route_gate, gate_up, down_proj):
    tok_count, per_token = expert_ids.shape
    feature_width = tokens.shape[1]
    devices = lax.axis_size("blk")
    experts = devices // 2
    capacity = 3 * tok_count * per_token // devices
    placements = tok_count * per_token
    chosen_ids = expert_ids.reshape(placements)
    onehot = (chosen_ids[:, None] == jnp.arange(experts, dtype=jnp.int32)[None, :]).astype(
        jnp.int32
    )
    ranked = jnp.sum((jnp.cumsum(onehot, axis=0) - 1) * onehot, axis=1)
    slot_index = chosen_ids * capacity + ranked
    token_of = jnp.arange(placements, dtype=jnp.int32) // per_token
    slot_table = jnp.full((experts * capacity,), tok_count, jnp.int32).at[slot_index].set(token_of)
    outgoing = jnp.take(tokens, slot_table, axis=0, mode="fill", fill_value=0)
    outgoing = outgoing.reshape(experts, capacity, feature_width)
    doubled = jnp.repeat(outgoing, 2, axis=0)
    received = lax.all_to_all(doubled, "blk", split_axis=0, concat_axis=0, tiled=True)
    item_count = received.shape[1]
    partial_value = expert_half(received.reshape(-1, feature_width), gate_up, down_proj)
    partial_value = partial_value.reshape(devices, item_count, feature_width)
    returned_rows = lax.all_to_all(partial_value, "blk", split_axis=0, concat_axis=0, tiled=True)
    halves = returned_rows.reshape(experts, 2, capacity, feature_width).astype(jnp.float32)
    results = halves[:, 0] + halves[:, 1]
    flattened = results.reshape(experts * capacity, feature_width)
    picked = jnp.take(flattened, slot_index, axis=0)
    weighted = picked.reshape(tok_count, per_token, feature_width) * route_gate[:, :, None]
    return jnp.sum(weighted, axis=1).astype(jnp.bfloat16)


def snake(chips):
    return list(range(0, chips, 2)) + list(range(chips - 1, 0, -2))


def half_expert_kernel(heights, load, split, *refs):
    blocks, refs = refs[: len(heights)], refs[len(heights) :]
    if load:
        (gate_up_far, down_far), refs = refs[:2], refs[2:]
        outs, (gate_up_ref, down_ref, rows, hidden, arrived) = refs[:split], refs[split:]
    else:
        (gate_up_ref, down_ref), outs, (rows, hidden) = refs[:2], refs[2:-2], refs[-2:]
    units, width = down_ref.shape
    tile = 256 if units % 256 == 0 else units
    tiles = units // tile
    copies = []
    if load:
        for t in range(tiles):
            near = pl.ds(t * tile, tile)
            copies.append(pltpu.make_async_copy(gate_up_far.at[:, near], gate_up_ref.at[:, near], arrived.at[t]))
        copies.append(pltpu.make_async_copy(down_far, down_ref, arrived.at[tiles]))
        for copy in copies:
            copy.start()

    at = 0
    for block, height in zip(blocks, heights):
        rows[at : at + height, :] = block[:height, :]
        at += height

    contract = (((1,), (1,)), ((), ()))
    taken = rows[...]
    for t in range(tiles):
        if load:
            copies[t].wait()
        near = slice(t * tile, (t + 1) * tile)
        gating = lax.dot_general(taken, gate_up_ref[0, near], contract, preferred_element_type=jnp.float32)
        lifted = lax.dot_general(taken, gate_up_ref[1, near], contract, preferred_element_type=jnp.float32)
        hidden[:, near] = (gating / (1.0 + jnp.exp(-gating)) * lifted).astype(jnp.bfloat16)
    if load:
        copies[tiles].wait()
    inner = hidden[...]
    share = outs[0].shape[0]
    tile = 512 if width % 512 == 0 else width
    for low in range(0, width, tile):
        product = jnp.dot(inner, down_ref[:, low : low + tile], preferred_element_type=jnp.float32)
        product = product.astype(jnp.bfloat16)
        for i, out in enumerate(outs):
            out[:, low : low + tile] = product[i * share : (i + 1) * share]


def load_kernel(*refs):
    copies = [pltpu.make_async_copy(far, near, refs[4].at[i]) for i, (far, near) in enumerate(zip(refs[:2], refs[2:4]))]
    for copy in copies:
        copy.start()
    for copy in copies:
        copy.wait()


def loaded(*weights):
    return pl.pallas_call(
        load_kernel,
        out_shape=[jax.ShapeDtypeStruct(array.shape, array.dtype) for array in weights],
        in_specs=[pl.BlockSpec(memory_space=pltpu.HBM)] * 2,
        out_specs=[pl.BlockSpec(memory_space=pltpu.VMEM)] * 2,
        scratch_shapes=[pltpu.SemaphoreType.DMA((2,))],
        compiler_params=pltpu.CompilerParams(vmem_limit_bytes=38 << 20),
        cost_estimate=pl.CostEstimate(flops=1 << 28, bytes_accessed=1 << 20, transcendentals=0),
    )(*weights)


def widen_kernel(gates, out):
    out[...] = jnp.concatenate([gates[...], jnp.zeros((GATE_ROWS, out.shape[1] - gates.shape[1]), out.dtype)], axis=1)


def widened(own, other, width):
    whole = pl.BlockSpec(memory_space=pltpu.VMEM)
    wide = pl.pallas_call(
        widen_kernel,
        out_shape=jax.ShapeDtypeStruct((GATE_ROWS, width), own.dtype),
        in_specs=[whole],
        out_specs=whole,
        compiler_params=pltpu.CompilerParams(vmem_limit_bytes=8 << 20),
        cost_estimate=pl.CostEstimate(flops=1 << 28, bytes_accessed=1 << 20, transcendentals=0),
    )(own)
    size = own.shape[1]
    return jnp.concatenate([wide[:, :size], other, wide[:, 2 * size :]], axis=1)


def half_expert(heights, blocks, weights, load=False, cost=2, split=2):
    height = sum(heights)
    units, width = weights[1].shape
    whole = pl.BlockSpec(memory_space=pltpu.VMEM)
    far = pl.BlockSpec(memory_space=pltpu.HBM)
    outs = [jax.ShapeDtypeStruct((height // split, width), jnp.bfloat16)] * split
    scratch = [pltpu.VMEM((height, width), jnp.bfloat16), pltpu.VMEM((height, units), jnp.bfloat16)]
    if load:
        outs += [jax.ShapeDtypeStruct(array.shape, array.dtype) for array in weights]
        scratch.append(pltpu.SemaphoreType.DMA((units // 256 + 1 if units % 256 == 0 else 2,)))
    return pl.pallas_call(
        functools.partial(half_expert_kernel, tuple(heights), load, split),
        out_shape=outs,
        in_specs=[whole] * len(blocks) + [far if load else whole] * 2,
        out_specs=[whole] * len(outs),
        scratch_shapes=scratch,
        compiler_params=pltpu.CompilerParams(vmem_limit_bytes=(34 if load else 14) << 20),
        cost_estimate=pl.CostEstimate(
            flops=int(cost * height * units * width),
            bytes_accessed=int(cost * units * width),
            transcendentals=0,
        ),
    )(*blocks, *weights)


def weighted_kernel(kind, own, distant, *refs):
    experts, holder, terms, out = refs[: 1 + bool(distant)], refs[1 + bool(distant)], refs[2 + bool(distant) : -1], refs[-1]
    rows = out.shape[0]
    last = holder.shape[0] - GATE_ROWS
    near, far = (holder[last:, (2 * kind + i) * LANES : (2 * kind + i + 1) * LANES].astype(jnp.float32) for i in (0, 1))

    def weight(place):
        wanted = lax.broadcasted_iota(jnp.int32, near.shape, 0) == experts[place][0]
        line = jnp.sum(jnp.where(wanted, near + far, 0.0), axis=0, keepdims=True)
        return jnp.broadcast_to(line, near.shape).T[:rows, :1]

    def total(blocks):
        return sum(block[...].astype(jnp.float32) for block in blocks)

    value = weight(0) * total(terms[:own])
    if distant:
        value += weight(1) * total(terms[own : own + distant])
    if own + distant < len(terms):
        value += total(terms[own + distant :])
    out[...] = value.astype(out.dtype)


def weighted(experts, holder, kind, own, distant=(), plain=(), dtype=jnp.bfloat16):
    whole = pl.BlockSpec(memory_space=pltpu.VMEM)
    terms = [*own, *distant, *plain]
    experts = experts[: 1 + bool(distant)]
    size = own[0].size
    return pl.pallas_call(
        functools.partial(weighted_kernel, kind, len(own), len(distant)),
        out_shape=jax.ShapeDtypeStruct(own[0].shape, dtype),
        in_specs=[pl.BlockSpec(memory_space=pltpu.SMEM)] * len(experts) + [whole] * (1 + len(terms)),
        out_specs=whole,
        compiler_params=pltpu.CompilerParams(vmem_limit_bytes=10 << 20),
        cost_estimate=pl.CostEstimate(flops=size * 20000, bytes_accessed=size, transcendentals=0),
    )(*experts, holder, *terms)


def by_tokens(tokens, expert_ids, route_gate, gate_up, down_proj):
    chips = lax.axis_size("blk") // 2
    order, far = snake(chips), chips // 2
    rows = tokens.shape[0]
    half = rows // 2
    chains = (0, 1)

    def moved(steps, swap=False):
        pairs = []
        for place in range(chips):
            for core in (0, 1):
                target = order[(place + steps * (1 - 2 * core)) % chips]
                pairs.append((2 * order[place] + core, 2 * target + (1 - core if swap else core)))
        return pairs

    forth, back, across, cores = moved(1), moved(-1), moved(-1, True), moved(0, True)

    def send(value, pairs, name):
        with jax.named_scope(name):
            return lax.ppermute(value, "blk", pairs)

    def total(*terms):
        return sum(term.astype(jnp.float32) for term in terms)

    def rounded(value):
        return value.astype(jnp.bfloat16)

    def after(value, *earlier):
        return lax.optimization_barrier((value, *earlier))[0]

    device = lax.axis_index("blk").astype(jnp.int32)
    chip, core = jnp.right_shift(device, 1), jnp.bitwise_and(device, 1)
    odd = jnp.bitwise_and(chip, 1)
    place = jnp.where(odd == 1, chips - 1 - jnp.right_shift(chip, 1), jnp.right_shift(chip, 1))
    ahead = place + 1 - 2 * core
    ahead = jnp.where(ahead < 0, chips - 1, jnp.where(ahead == chips, 0, ahead))
    ahead = jnp.where(ahead < far, 2 * ahead, 2 * (chips - 1 - ahead) + 1)
    expert = [chip.reshape(1), ahead.reshape(1)]
    ring = [send(tokens, forth, "ring_1_0"), None]
    others = send(tokens, cores, "swap_0_0")
    chosen = jnp.arange(GATE_ROWS, dtype=jnp.int32)[:, None, None] == expert_ids.T[None]
    weight = jnp.sum(jnp.where(chosen, route_gate.T[None], 0.0), axis=1)
    high = lax.reduce_precision(weight, 8, 7)
    gates = jnp.concatenate([high, weight - high], axis=1).astype(jnp.bfloat16)
    packed = jnp.concatenate([others, widened(gates, send(gates, cores, "swap_0_1"), tokens.shape[1])])
    ring[1] = send(packed, forth, "ring_1_1")

    near = loaded(after(gate_up, *expert), down_proj)
    ring[0] = after(ring[0], near[1])
    results, holders = {}, {0: packed}
    with jax.named_scope("expert_0"):
        own, given = half_expert([rows] * 2, [after(tokens, ring[0]), packed], near)
    results[0, 0] = own, given
    ring[1] = after(ring[1], own)

    def expert_rows(step, c, inputs, **options):
        with jax.named_scope(f"expert_{step}_{c}"):
            results[step, c] = half_expert([rows] * 2, inputs, near, **options)
        if step == far - 1 or (step, c) == (1, 1):
            give(step, c)
        return results[step, c][0]

    def give(step, c, *earlier):
        kept, given = results[step, c]
        results[step, c] = kept, send(after(given, *earlier) if earlier else given, cores, f"give_{step}_{c}")

    earlier = ring[1]
    for step in range(1, far - 1):
        holders[step] = ring[1]
        swapped = [
            send(block, cores, f"swap_{step}_{c}") for c, block in enumerate(ring[: 1 if step == 1 else 2])
        ]
        blocks = list(ring)
        ring[0] = send(blocks[0], forth, f"ring_{step + 1}_0")
        if step < far - 2:
            ring[1] = send(blocks[1], forth, f"ring_{step + 1}_1")
        for c in chains:
            if (step, c) == (1, 1):
                delayed = blocks[1]
                earlier = ring[1]
                continue
            kept = expert_rows(step, c, [after(blocks[c], earlier), swapped[c]])
            if (step, c) == (far - 2, 1):
                ring[1] = send(after(blocks[1], kept), forth, f"ring_{step + 1}_1")
            else:
                ring[c] = after(ring[c], kept)
                earlier = ring[c]
    holders[far - 1] = blocks[1] = ring[1]
    swapped = send(ring[0], cores, f"swap_{far - 1}_0")
    block, ring = ring[0], [send(ring[0], forth, f"ring_{far}_0")]
    kept = expert_rows(far - 1, 0, [after(block, kept), swapped])
    ring[0] = after(ring[0], kept)

    with jax.named_scope("expert_far_ring"):
        (given,) = half_expert([rows], ring, near, split=1, cost=0.3)
    swapped = send(ring[0], cores, f"swap_{far}")
    swapped = after(swapped, given)
    given = send(given, cores, "give_far")
    with jax.named_scope("expert_far_swapped"):
        (kept,) = half_expert([rows], [swapped], near, split=1, cost=0.3)
    last = blocks[1], send(after(blocks[1], kept), cores, f"swap_{far - 1}_1")
    earlier = rounded(total(kept, given))
    sums = [None, send(earlier, back, f"back_{far}_1")]
    mine, theirs = results[far - 1, 0]
    earlier = weighted(expert, holders[far - 1], 0, [after(mine, earlier), theirs])
    sums[0] = send(earlier, back, f"back_{far - 1}_0")
    earlier = expert_rows(far - 1, 1, [after(last[0], earlier), last[1]], cost=0.2)
    for step in range(far - 2, 1, -1):
        for c in chains:
            give(step, c, earlier)
    swapped = send(after(delayed, earlier), cores, "swap_1_1")
    steps = [(step, c) for step in range(far - 1, 0, -1) for c in chains][1:]
    for step, c in steps:
        mine, theirs = results[step, c]
        far_sum = (step, c) == (far - 1, 1)
        mine = after(mine, earlier)
        if far_sum:
            part = weighted(expert, holders[step], c, [mine], [sums[c]], dtype=jnp.float32)
            earlier = weighted(expert, holders[step], c, [after(theirs, part)], plain=[part])
        else:
            earlier = weighted(expert, holders[step], c, [mine, theirs], plain=[sums[c]])
        sums[c] = send(earlier, across if (step, c) == (1, 1) else back, f"back_{step}_{c}")
        if (step, c) == (far - 2, 0):
            give(1, 0, earlier)
        if far_sum:
            give(0, 0, earlier)
            earlier = expert_rows(1, 1, [after(delayed, earlier), swapped])
    own = weighted(expert, packed, 0, results[0, 0], plain=[sums[0]], dtype=jnp.float32)
    return rounded(total(own, sums[1]))


def solution(mesh):
    placed = (
        P(("groups", "blk"), None),
        P(("groups", "blk"), None),
        P(("groups", "blk"), None),
        P(None, "blk", None),
        P("blk", None),
    )

    def per_device(tokens, expert_ids, route_gate, gate_up, down_proj):
        experts = mesh.shape["blk"] // 2
        dense = experts <= min(GATE_ROWS, 2 * expert_ids.shape[1]) and tokens.shape[0] == LANES
        body = by_tokens if dense else by_slots
        return body(tokens, expert_ids, route_gate, gate_up, down_proj)

    return jax.shard_map(
        per_device,
        mesh=mesh,
        in_specs=placed,
        out_specs=P(("groups", "blk"), None),
        check_vma=False,
    )
```

```python
import functools

import jax
import jax.numpy as jnp
import numpy as np
from jax import lax
from jax.experimental import pallas as pl
from jax.experimental.pallas import tpu as pltpu
from jax.sharding import PartitionSpec as P

GATE_ROWS, LANES = 16, 128


def expert_half(slot_block, gate_up, down_proj):
    contract = (((1,), (1,)), ((), ()))
    gating = lax.dot_general(slot_block, gate_up[0], contract, preferred_element_type=jnp.float32)
    lifted = lax.dot_general(slot_block, gate_up[1], contract, preferred_element_type=jnp.float32)
    hidden = (jax.nn.silu(gating) * lifted).astype(jnp.bfloat16)
    return jnp.dot(hidden, down_proj, preferred_element_type=jnp.float32).astype(jnp.bfloat16)


def by_slots(tokens, expert_ids, route_gate, gate_up, down_proj):
    tok_count, per_token = expert_ids.shape
    feature_width = tokens.shape[1]
    devices = lax.axis_size("blk")
    experts = devices // 2
    capacity = 3 * tok_count * per_token // devices
    placements = tok_count * per_token
    chosen_ids = expert_ids.reshape(placements)
    onehot = (chosen_ids[:, None] == jnp.arange(experts, dtype=jnp.int32)[None, :]).astype(
        jnp.int32
    )
    ranked = jnp.sum((jnp.cumsum(onehot, axis=0) - 1) * onehot, axis=1)
    slot_index = chosen_ids * capacity + ranked
    token_of = jnp.arange(placements, dtype=jnp.int32) // per_token
    slot_table = jnp.full((experts * capacity,), tok_count, jnp.int32).at[slot_index].set(token_of)
    outgoing = jnp.take(tokens, slot_table, axis=0, mode="fill", fill_value=0)
    outgoing = outgoing.reshape(experts, capacity, feature_width)
    doubled = jnp.repeat(outgoing, 2, axis=0)
    received = lax.all_to_all(doubled, "blk", split_axis=0, concat_axis=0, tiled=True)
    item_count = received.shape[1]
    partial_value = expert_half(received.reshape(-1, feature_width), gate_up, down_proj)
    partial_value = partial_value.reshape(devices, item_count, feature_width)
    returned_rows = lax.all_to_all(partial_value, "blk", split_axis=0, concat_axis=0, tiled=True)
    halves = returned_rows.reshape(experts, 2, capacity, feature_width).astype(jnp.float32)
    results = halves[:, 0] + halves[:, 1]
    flattened = results.reshape(experts * capacity, feature_width)
    picked = jnp.take(flattened, slot_index, axis=0)
    weighted = picked.reshape(tok_count, per_token, feature_width) * route_gate[:, :, None]
    return jnp.sum(weighted, axis=1).astype(jnp.bfloat16)


def snake(chips):
    return list(range(0, chips, 2)) + list(range(chips - 1, 0, -2))


def half_expert_kernel(heights, load, split, *refs):
    blocks, refs = refs[: len(heights)], refs[len(heights) :]
    if load:
        (gate_up_far, down_far), refs = refs[:2], refs[2:]
        outs, (gate_up_ref, down_ref, rows, hidden, arrived) = refs[:split], refs[split:]
    else:
        (gate_up_ref, down_ref), outs, (rows, hidden) = refs[:2], refs[2:-2], refs[-2:]
    units, width = down_ref.shape
    tile = 256 if units % 256 == 0 else units
    tiles = units // tile
    copies = []
    if load:
        for t in range(tiles):
            near = pl.ds(t * tile, tile)
            copies.append(pltpu.make_async_copy(gate_up_far.at[:, near], gate_up_ref.at[:, near], arrived.at[t]))
        copies.append(pltpu.make_async_copy(down_far, down_ref, arrived.at[tiles]))
        for copy in copies:
            copy.start()

    at = 0
    for block, height in zip(blocks, heights):
        rows[at : at + height, :] = block[:height, :]
        at += height

    contract = (((1,), (1,)), ((), ()))
    taken = rows[...]
    for t in range(tiles):
        if load:
            copies[t].wait()
        near = slice(t * tile, (t + 1) * tile)
        gating = lax.dot_general(taken, gate_up_ref[0, near], contract, preferred_element_type=jnp.float32)
        lifted = lax.dot_general(taken, gate_up_ref[1, near], contract, preferred_element_type=jnp.float32)
        hidden[:, near] = (gating / (1.0 + jnp.exp(-gating)) * lifted).astype(jnp.bfloat16)
    if load:
        copies[tiles].wait()
    inner = hidden[...]
    share = outs[0].shape[0]
    tile = 512 if width % 512 == 0 else width
    for low in range(0, width, tile):
        product = jnp.dot(inner, down_ref[:, low : low + tile], preferred_element_type=jnp.float32)
        product = product.astype(jnp.bfloat16)
        for i, out in enumerate(outs):
            out[:, low : low + tile] = product[i * share : (i + 1) * share]


def load_kernel(*refs):
    copies = [pltpu.make_async_copy(far, near, refs[4].at[i]) for i, (far, near) in enumerate(zip(refs[:2], refs[2:4]))]
    for copy in copies:
        copy.start()
    for copy in copies:
        copy.wait()


def loaded(*weights):
    return pl.pallas_call(
        load_kernel,
        out_shape=[jax.ShapeDtypeStruct(array.shape, array.dtype) for array in weights],
        in_specs=[pl.BlockSpec(memory_space=pltpu.HBM)] * 2,
        out_specs=[pl.BlockSpec(memory_space=pltpu.VMEM)] * 2,
        scratch_shapes=[pltpu.SemaphoreType.DMA((2,))],
        compiler_params=pltpu.CompilerParams(vmem_limit_bytes=38 << 20),
        cost_estimate=pl.CostEstimate(flops=1 << 28, bytes_accessed=1 << 20, transcendentals=0),
    )(*weights)


def widen_kernel(gates, out):
    out[...] = jnp.concatenate([gates[...], jnp.zeros((GATE_ROWS, out.shape[1] - gates.shape[1]), out.dtype)], axis=1)


def widened(own, other, width):
    whole = pl.BlockSpec(memory_space=pltpu.VMEM)
    wide = pl.pallas_call(
        widen_kernel,
        out_shape=jax.ShapeDtypeStruct((GATE_ROWS, width), own.dtype),
        in_specs=[whole],
        out_specs=whole,
        compiler_params=pltpu.CompilerParams(vmem_limit_bytes=8 << 20),
        cost_estimate=pl.CostEstimate(flops=1 << 28, bytes_accessed=1 << 20, transcendentals=0),
    )(own)
    size = own.shape[1]
    return jnp.concatenate([wide[:, :size], other, wide[:, 2 * size :]], axis=1)


def half_expert(heights, blocks, weights, load=False, cost=2, split=2):
    height = sum(heights)
    units, width = weights[1].shape
    whole = pl.BlockSpec(memory_space=pltpu.VMEM)
    far = pl.BlockSpec(memory_space=pltpu.HBM)
    outs = [jax.ShapeDtypeStruct((height // split, width), jnp.bfloat16)] * split
    scratch = [pltpu.VMEM((height, width), jnp.bfloat16), pltpu.VMEM((height, units), jnp.bfloat16)]
    if load:
        outs += [jax.ShapeDtypeStruct(array.shape, array.dtype) for array in weights]
        scratch.append(pltpu.SemaphoreType.DMA((units // 256 + 1 if units % 256 == 0 else 2,)))
    return pl.pallas_call(
        functools.partial(half_expert_kernel, tuple(heights), load, split),
        out_shape=outs,
        in_specs=[whole] * len(blocks) + [far if load else whole] * 2,
        out_specs=[whole] * len(outs),
        scratch_shapes=scratch,
        compiler_params=pltpu.CompilerParams(vmem_limit_bytes=(34 if load else 14) << 20),
        cost_estimate=pl.CostEstimate(
            flops=int(cost * height * units * width),
            bytes_accessed=int(cost * units * width),
            transcendentals=0,
        ),
    )(*blocks, *weights)


def weighted_kernel(kind, own, distant, *refs):
    experts, holder, terms, out = refs[: 1 + bool(distant)], refs[1 + bool(distant)], refs[2 + bool(distant) : -1], refs[-1]
    rows = out.shape[0]
    last = holder.shape[0] - GATE_ROWS
    near, far = (holder[last:, (2 * kind + i) * LANES : (2 * kind + i + 1) * LANES].astype(jnp.float32) for i in (0, 1))

    def weight(place):
        wanted = lax.broadcasted_iota(jnp.int32, near.shape, 0) == experts[place][0]
        line = jnp.sum(jnp.where(wanted, near + far, 0.0), axis=0, keepdims=True)
        return jnp.broadcast_to(line, near.shape).T[:rows, :1]

    def total(blocks):
        return sum(block[...].astype(jnp.float32) for block in blocks)

    value = weight(0) * total(terms[:own])
    if distant:
        value += weight(1) * total(terms[own : own + distant])
    if own + distant < len(terms):
        value += total(terms[own + distant :])
    out[...] = value.astype(out.dtype)


def weighted(experts, holder, kind, own, distant=(), plain=(), dtype=jnp.bfloat16):
    whole = pl.BlockSpec(memory_space=pltpu.VMEM)
    terms = [*own, *distant, *plain]
    experts = experts[: 1 + bool(distant)]
    size = own[0].size
    return pl.pallas_call(
        functools.partial(weighted_kernel, kind, len(own), len(distant)),
        out_shape=jax.ShapeDtypeStruct(own[0].shape, dtype),
        in_specs=[pl.BlockSpec(memory_space=pltpu.SMEM)] * len(experts) + [whole] * (1 + len(terms)),
        out_specs=whole,
        compiler_params=pltpu.CompilerParams(vmem_limit_bytes=10 << 20),
        cost_estimate=pl.CostEstimate(flops=size * 20000, bytes_accessed=size, transcendentals=0),
    )(*experts, holder, *terms)


def last_sum_kernel(own, arrived, out, parts, done):
    chunks, height = parts.shape[:2]
    copies = []
    for i in range(chunks):
        near = slice(i * height, (i + 1) * height)
        parts[i] = (own[near, :] + arrived[near, :].astype(jnp.float32)).astype(out.dtype)
        copies.append(pltpu.make_async_copy(parts.at[i], out.at[pl.ds(i * height, height)], done.at[i]))
        copies[-1].start()
    for copy in copies:
        copy.wait()


def last_sum(own, arrived):
    whole = pl.BlockSpec(memory_space=pltpu.VMEM)
    rows, width = own.shape
    chunks = 4
    return pl.pallas_call(
        last_sum_kernel,
        out_shape=jax.ShapeDtypeStruct((rows, width), jnp.bfloat16),
        in_specs=[whole, whole],
        out_specs=pl.BlockSpec(memory_space=pltpu.HBM),
        scratch_shapes=[
            pltpu.VMEM((chunks, rows // chunks, width), jnp.bfloat16),
            pltpu.SemaphoreType.DMA((chunks,)),
        ],
        compiler_params=pltpu.CompilerParams(vmem_limit_bytes=8 << 20),
    )(own, arrived)


def by_tokens(tokens, expert_ids, route_gate, gate_up, down_proj):
    chips = lax.axis_size("blk") // 2
    order, far = snake(chips), chips // 2
    rows = tokens.shape[0]
    half = rows // 2
    chains = (0, 1)

    def moved(steps, swap=False):
        pairs = []
        for place in range(chips):
            for core in (0, 1):
                target = order[(place + steps * (1 - 2 * core)) % chips]
                pairs.append((2 * order[place] + core, 2 * target + (1 - core if swap else core)))
        return pairs

    forth, back, across, cores = moved(1), moved(-1), moved(-1, True), moved(0, True)

    def send(value, pairs, name):
        with jax.named_scope(name):
            return lax.ppermute(value, "blk", pairs)

    def total(*terms):
        return sum(term.astype(jnp.float32) for term in terms)

    def rounded(value):
        return value.astype(jnp.bfloat16)

    def after(value, *earlier):
        return lax.optimization_barrier((value, *earlier))[0]

    device = lax.axis_index("blk").astype(jnp.int32)
    chip, core = jnp.right_shift(device, 1), jnp.bitwise_and(device, 1)
    odd = jnp.bitwise_and(chip, 1)
    place = jnp.where(odd == 1, chips - 1 - jnp.right_shift(chip, 1), jnp.right_shift(chip, 1))
    ahead = place + 1 - 2 * core
    ahead = jnp.where(ahead < 0, chips - 1, jnp.where(ahead == chips, 0, ahead))
    ahead = jnp.where(ahead < far, 2 * ahead, 2 * (chips - 1 - ahead) + 1)
    expert = [chip.reshape(1), ahead.reshape(1)]
    ring = [send(tokens, forth, "ring_1_0"), None]
    others = send(tokens, cores, "swap_0_0")
    chosen = jnp.arange(GATE_ROWS, dtype=jnp.int32)[:, None, None] == expert_ids.T[None]
    weight = jnp.sum(jnp.where(chosen, route_gate.T[None], 0.0), axis=1)
    high = lax.reduce_precision(weight, 8, 7)
    gates = jnp.concatenate([high, weight - high], axis=1).astype(jnp.bfloat16)
    packed = jnp.concatenate([others, widened(gates, send(gates, cores, "swap_0_1"), tokens.shape[1])])
    ring[1] = send(packed, forth, "ring_1_1")

    near = loaded(after(gate_up, *expert), down_proj)
    ring[0] = after(ring[0], near[1])
    results, holders = {}, {0: packed}
    with jax.named_scope("expert_0"):
        own, given = half_expert([rows] * 2, [after(tokens, ring[0]), packed], near)
    results[0, 0] = own, given
    ring[1] = after(ring[1], own)

    def expert_rows(step, c, inputs, **options):
        with jax.named_scope(f"expert_{step}_{c}"):
            results[step, c] = half_expert([rows] * 2, inputs, near, **options)
        if step == far - 1 or (step, c) == (1, 1):
            give(step, c)
        return results[step, c][0]

    def give(step, c, *earlier):
        kept, given = results[step, c]
        results[step, c] = kept, send(after(given, *earlier) if earlier else given, cores, f"give_{step}_{c}")

    earlier = ring[1]
    for step in range(1, far - 1):
        holders[step] = ring[1]
        swapped = [
            send(block, cores, f"swap_{step}_{c}") for c, block in enumerate(ring[: 1 if step == 1 else 2])
        ]
        blocks = list(ring)
        ring[0] = send(blocks[0], forth, f"ring_{step + 1}_0")
        if step < far - 2:
            ring[1] = send(blocks[1], forth, f"ring_{step + 1}_1")
        for c in chains:
            if (step, c) == (1, 1):
                delayed = blocks[1]
                earlier = ring[1]
                continue
            kept = expert_rows(step, c, [after(blocks[c], earlier), swapped[c]])
            if (step, c) == (far - 2, 1):
                ring[1] = send(after(blocks[1], kept), forth, f"ring_{step + 1}_1")
            else:
                ring[c] = after(ring[c], kept)
                earlier = ring[c]
    holders[far - 1] = blocks[1] = ring[1]
    swapped = send(ring[0], cores, f"swap_{far - 1}_0")
    block, ring = ring[0], [send(ring[0], forth, f"ring_{far}_0")]
    kept = expert_rows(far - 1, 0, [after(block, kept), swapped])
    ring[0] = after(ring[0], kept)

    with jax.named_scope("expert_far_ring"):
        (given,) = half_expert([rows], ring, near, split=1, cost=0.3)
    swapped = send(ring[0], cores, f"swap_{far}")
    swapped = after(swapped, given)
    given = send(given, cores, "give_far")
    with jax.named_scope("expert_far_swapped"):
        (kept,) = half_expert([rows], [swapped], near, split=1, cost=0.3)
    last = blocks[1], send(after(blocks[1], kept), cores, f"swap_{far - 1}_1")
    earlier = rounded(total(kept, given))
    sums = [None, send(earlier, back, f"back_{far}_1")]
    mine, theirs = results[far - 1, 0]
    earlier = weighted(expert, holders[far - 1], 0, [after(mine, earlier), theirs])
    sums[0] = send(earlier, back, f"back_{far - 1}_0")
    earlier = expert_rows(far - 1, 1, [after(last[0], earlier), last[1]], cost=0.2)
    for step in range(far - 2, 1, -1):
        for c in chains:
            give(step, c, earlier)
    swapped = send(after(delayed, earlier), cores, "swap_1_1")
    steps = [(step, c) for step in range(far - 1, 0, -1) for c in chains][1:]
    for step, c in steps:
        mine, theirs = results[step, c]
        far_sum = (step, c) == (far - 1, 1)
        mine = after(mine, earlier)
        if far_sum:
            part = weighted(expert, holders[step], c, [mine], [sums[c]], dtype=jnp.float32)
            earlier = weighted(expert, holders[step], c, [after(theirs, part)], plain=[part])
        else:
            earlier = weighted(expert, holders[step], c, [mine, theirs], plain=[sums[c]])
        sums[c] = send(earlier, across if (step, c) == (1, 1) else back, f"back_{step}_{c}")
        if (step, c) == (far - 2, 0):
            give(1, 0, earlier)
        if far_sum:
            give(0, 0, earlier)
            earlier = expert_rows(1, 1, [after(delayed, earlier), swapped])
    own = weighted(expert, packed, 0, results[0, 0], plain=[sums[0]], dtype=jnp.float32)
    return last_sum(own, sums[1])


def solution(mesh):
    placed = (
        P(("groups", "blk"), None),
        P(("groups", "blk"), None),
        P(("groups", "blk"), None),
        P(None, "blk", None),
        P("blk", None),
    )

    def per_device(tokens, expert_ids, route_gate, gate_up, down_proj):
        experts = mesh.shape["blk"] // 2
        dense = experts <= min(GATE_ROWS, 2 * expert_ids.shape[1]) and tokens.shape[0] == LANES
        body = by_tokens if dense else by_slots
        return body(tokens, expert_ids, route_gate, gate_up, down_proj)

    return jax.shard_map(
        per_device,
        mesh=mesh,
        in_specs=placed,
        out_specs=P(("groups", "blk"), None),
        check_vma=False,
    )
```

```python
import functools

import jax
import jax.numpy as jnp
import numpy as np
from jax import lax
from jax.experimental import pallas as pl
from jax.experimental.pallas import tpu as pltpu
from jax.sharding import PartitionSpec as P

GATE_ROWS, LANES = 16, 128


def expert_half(slot_block, gate_up, down_proj):
    contract = (((1,), (1,)), ((), ()))
    gating = lax.dot_general(slot_block, gate_up[0], contract, preferred_element_type=jnp.float32)
    lifted = lax.dot_general(slot_block, gate_up[1], contract, preferred_element_type=jnp.float32)
    hidden = (jax.nn.silu(gating) * lifted).astype(jnp.bfloat16)
    return jnp.dot(hidden, down_proj, preferred_element_type=jnp.float32).astype(jnp.bfloat16)


def by_slots(tokens, expert_ids, route_gate, gate_up, down_proj):
    tok_count, per_token = expert_ids.shape
    feature_width = tokens.shape[1]
    devices = lax.axis_size("blk")
    experts = devices // 2
    capacity = 3 * tok_count * per_token // devices
    placements = tok_count * per_token
    chosen_ids = expert_ids.reshape(placements)
    onehot = (chosen_ids[:, None] == jnp.arange(experts, dtype=jnp.int32)[None, :]).astype(
        jnp.int32
    )
    ranked = jnp.sum((jnp.cumsum(onehot, axis=0) - 1) * onehot, axis=1)
    slot_index = chosen_ids * capacity + ranked
    token_of = jnp.arange(placements, dtype=jnp.int32) // per_token
    slot_table = jnp.full((experts * capacity,), tok_count, jnp.int32).at[slot_index].set(token_of)
    outgoing = jnp.take(tokens, slot_table, axis=0, mode="fill", fill_value=0)
    outgoing = outgoing.reshape(experts, capacity, feature_width)
    doubled = jnp.repeat(outgoing, 2, axis=0)
    received = lax.all_to_all(doubled, "blk", split_axis=0, concat_axis=0, tiled=True)
    item_count = received.shape[1]
    partial_value = expert_half(received.reshape(-1, feature_width), gate_up, down_proj)
    partial_value = partial_value.reshape(devices, item_count, feature_width)
    returned_rows = lax.all_to_all(partial_value, "blk", split_axis=0, concat_axis=0, tiled=True)
    halves = returned_rows.reshape(experts, 2, capacity, feature_width).astype(jnp.float32)
    results = halves[:, 0] + halves[:, 1]
    flattened = results.reshape(experts * capacity, feature_width)
    picked = jnp.take(flattened, slot_index, axis=0)
    weighted = picked.reshape(tok_count, per_token, feature_width) * route_gate[:, :, None]
    return jnp.sum(weighted, axis=1).astype(jnp.bfloat16)


def snake(chips):
    return list(range(0, chips, 2)) + list(range(chips - 1, 0, -2))


def half_expert_kernel(heights, load, split, *refs):
    blocks, refs = refs[: len(heights)], refs[len(heights) :]
    if load:
        (gate_up_far, down_far), refs = refs[:2], refs[2:]
        outs, (gate_up_ref, down_ref, rows, hidden, arrived) = refs[:split], refs[split:]
    else:
        (gate_up_ref, down_ref), outs, (rows, hidden) = refs[:2], refs[2:-2], refs[-2:]
    units, width = down_ref.shape
    small = len(heights) == 1
    tile = 256 if units % 256 == 0 and not small else units
    tiles = units // tile
    copies = []
    if load:
        for t in range(tiles):
            near = pl.ds(t * tile, tile)
            copies.append(pltpu.make_async_copy(gate_up_far.at[:, near], gate_up_ref.at[:, near], arrived.at[t]))
        copies.append(pltpu.make_async_copy(down_far, down_ref, arrived.at[tiles]))
        for copy in copies:
            copy.start()

    at = 0
    for block, height in zip(blocks, heights):
        if not small:
            rows[at : at + height, :] = block[:height, :]
        at += height

    contract = (((1,), (1,)), ((), ()))
    taken = blocks[0][...] if small else rows[...]
    for t in range(tiles):
        if load:
            copies[t].wait()
        near = slice(t * tile, (t + 1) * tile)
        gating = lax.dot_general(taken, gate_up_ref[0, near], contract, preferred_element_type=jnp.float32)
        lifted = lax.dot_general(taken, gate_up_ref[1, near], contract, preferred_element_type=jnp.float32)
        hidden[:, near] = (gating / (1.0 + jnp.exp(-gating)) * lifted).astype(jnp.bfloat16)
    if load:
        copies[tiles].wait()
    inner = hidden[...]
    share = outs[0].shape[0]
    tile = 512 if width % 512 == 0 and not small else width
    for low in range(0, width, tile):
        product = jnp.dot(inner, down_ref[:, low : low + tile], preferred_element_type=jnp.float32)
        product = product.astype(jnp.bfloat16)
        for i, out in enumerate(outs):
            out[:, low : low + tile] = product[i * share : (i + 1) * share]


def load_kernel(*refs):
    copies = [pltpu.make_async_copy(far, near, refs[4].at[i]) for i, (far, near) in enumerate(zip(refs[:2], refs[2:4]))]
    for copy in copies:
        copy.start()
    for copy in copies:
        copy.wait()


def loaded(*weights):
    return pl.pallas_call(
        load_kernel,
        out_shape=[jax.ShapeDtypeStruct(array.shape, array.dtype) for array in weights],
        in_specs=[pl.BlockSpec(memory_space=pltpu.HBM)] * 2,
        out_specs=[pl.BlockSpec(memory_space=pltpu.VMEM)] * 2,
        scratch_shapes=[pltpu.SemaphoreType.DMA((2,))],
        compiler_params=pltpu.CompilerParams(vmem_limit_bytes=38 << 20),
        cost_estimate=pl.CostEstimate(flops=1 << 28, bytes_accessed=1 << 20, transcendentals=0),
    )(*weights)


def widen_kernel(gates, out):
    out[...] = jnp.concatenate([gates[...], jnp.zeros((GATE_ROWS, out.shape[1] - gates.shape[1]), out.dtype)], axis=1)


def widened(own, other, width):
    whole = pl.BlockSpec(memory_space=pltpu.VMEM)
    wide = pl.pallas_call(
        widen_kernel,
        out_shape=jax.ShapeDtypeStruct((GATE_ROWS, width), own.dtype),
        in_specs=[whole],
        out_specs=whole,
        compiler_params=pltpu.CompilerParams(vmem_limit_bytes=8 << 20),
        cost_estimate=pl.CostEstimate(flops=1 << 28, bytes_accessed=1 << 20, transcendentals=0),
    )(own)
    size = own.shape[1]
    return jnp.concatenate([wide[:, :size], other, wide[:, 2 * size :]], axis=1)


def half_expert(heights, blocks, weights, load=False, cost=2, split=2):
    height = sum(heights)
    units, width = weights[1].shape
    whole = pl.BlockSpec(memory_space=pltpu.VMEM)
    far = pl.BlockSpec(memory_space=pltpu.HBM)
    outs = [jax.ShapeDtypeStruct((height // split, width), jnp.bfloat16)] * split
    scratch = [pltpu.VMEM((height, width), jnp.bfloat16), pltpu.VMEM((height, units), jnp.bfloat16)]
    if load:
        outs += [jax.ShapeDtypeStruct(array.shape, array.dtype) for array in weights]
        scratch.append(pltpu.SemaphoreType.DMA((units // 256 + 1 if units % 256 == 0 else 2,)))
    return pl.pallas_call(
        functools.partial(half_expert_kernel, tuple(heights), load, split),
        out_shape=outs,
        in_specs=[whole] * len(blocks) + [far if load else whole] * 2,
        out_specs=[whole] * len(outs),
        scratch_shapes=scratch,
        compiler_params=pltpu.CompilerParams(vmem_limit_bytes=(34 if load else 14) << 20),
        cost_estimate=pl.CostEstimate(
            flops=int(cost * height * units * width),
            bytes_accessed=int(cost * units * width),
            transcendentals=0,
        ),
    )(*blocks, *weights)


def weighted_kernel(kind, own, distant, *refs):
    experts, holder, terms, out = refs[: 1 + bool(distant)], refs[1 + bool(distant)], refs[2 + bool(distant) : -1], refs[-1]
    rows = out.shape[0]
    last = holder.shape[0] - GATE_ROWS
    near, far = (holder[last:, (2 * kind + i) * LANES : (2 * kind + i + 1) * LANES].astype(jnp.float32) for i in (0, 1))

    def weight(place):
        wanted = lax.broadcasted_iota(jnp.int32, near.shape, 0) == experts[place][0]
        line = jnp.sum(jnp.where(wanted, near + far, 0.0), axis=0, keepdims=True)
        return jnp.broadcast_to(line, near.shape).T[:rows, :1]

    def total(blocks):
        return sum(block[...].astype(jnp.float32) for block in blocks)

    value = weight(0) * total(terms[:own])
    if distant:
        value += weight(1) * total(terms[own : own + distant])
    if own + distant < len(terms):
        value += total(terms[own + distant :])
    out[...] = value.astype(out.dtype)


def weighted(experts, holder, kind, own, distant=(), plain=(), dtype=jnp.bfloat16):
    whole = pl.BlockSpec(memory_space=pltpu.VMEM)
    terms = [*own, *distant, *plain]
    experts = experts[: 1 + bool(distant)]
    size = own[0].size
    return pl.pallas_call(
        functools.partial(weighted_kernel, kind, len(own), len(distant)),
        out_shape=jax.ShapeDtypeStruct(own[0].shape, dtype),
        in_specs=[pl.BlockSpec(memory_space=pltpu.SMEM)] * len(experts) + [whole] * (1 + len(terms)),
        out_specs=whole,
        compiler_params=pltpu.CompilerParams(vmem_limit_bytes=10 << 20),
        cost_estimate=pl.CostEstimate(flops=size * 20000, bytes_accessed=size, transcendentals=0),
    )(*experts, holder, *terms)


def last_sum_kernel(own, arrived, out, parts, done):
    chunks, height = parts.shape[:2]
    copies = []
    for i in range(chunks):
        near = slice(i * height, (i + 1) * height)
        parts[i] = (own[near, :] + arrived[near, :].astype(jnp.float32)).astype(out.dtype)
        copies.append(pltpu.make_async_copy(parts.at[i], out.at[pl.ds(i * height, height)], done.at[i]))
        copies[-1].start()
    for copy in copies:
        copy.wait()


def last_sum(own, arrived):
    whole = pl.BlockSpec(memory_space=pltpu.VMEM)
    rows, width = own.shape
    chunks = 4
    return pl.pallas_call(
        last_sum_kernel,
        out_shape=jax.ShapeDtypeStruct((rows, width), jnp.bfloat16),
        in_specs=[whole, whole],
        out_specs=pl.BlockSpec(memory_space=pltpu.HBM),
        scratch_shapes=[
            pltpu.VMEM((chunks, rows // chunks, width), jnp.bfloat16),
            pltpu.SemaphoreType.DMA((chunks,)),
        ],
        compiler_params=pltpu.CompilerParams(vmem_limit_bytes=8 << 20),
    )(own, arrived)


def by_tokens(tokens, expert_ids, route_gate, gate_up, down_proj):
    chips = lax.axis_size("blk") // 2
    order, far = snake(chips), chips // 2
    rows = tokens.shape[0]
    half = rows // 2
    chains = (0, 1)

    def moved(steps, swap=False):
        pairs = []
        for place in range(chips):
            for core in (0, 1):
                target = order[(place + steps * (1 - 2 * core)) % chips]
                pairs.append((2 * order[place] + core, 2 * target + (1 - core if swap else core)))
        return pairs

    forth, back, across, cores = moved(1), moved(-1), moved(-1, True), moved(0, True)

    def send(value, pairs, name):
        with jax.named_scope(name):
            return lax.ppermute(value, "blk", pairs)

    def total(*terms):
        return sum(term.astype(jnp.float32) for term in terms)

    def rounded(value):
        return value.astype(jnp.bfloat16)

    def after(value, *earlier):
        return lax.optimization_barrier((value, *earlier))[0]

    device = lax.axis_index("blk").astype(jnp.int32)
    chip, core = jnp.right_shift(device, 1), jnp.bitwise_and(device, 1)
    odd = jnp.bitwise_and(chip, 1)
    place = jnp.where(odd == 1, chips - 1 - jnp.right_shift(chip, 1), jnp.right_shift(chip, 1))
    ahead = place + 1 - 2 * core
    ahead = jnp.where(ahead < 0, chips - 1, jnp.where(ahead == chips, 0, ahead))
    ahead = jnp.where(ahead < far, 2 * ahead, 2 * (chips - 1 - ahead) + 1)
    expert = [chip.reshape(1), ahead.reshape(1)]
    ring = [send(tokens, forth, "ring_1_0"), None]
    others = send(tokens, cores, "swap_0_0")
    chosen = jnp.arange(GATE_ROWS, dtype=jnp.int32)[:, None, None] == expert_ids.T[None]
    weight = jnp.sum(jnp.where(chosen, route_gate.T[None], 0.0), axis=1)
    high = lax.reduce_precision(weight, 8, 7)
    gates = jnp.concatenate([high, weight - high], axis=1).astype(jnp.bfloat16)
    packed = jnp.concatenate([others, widened(gates, send(gates, cores, "swap_0_1"), tokens.shape[1])])
    ring[1] = send(packed, forth, "ring_1_1")

    near = loaded(after(gate_up, *expert), down_proj)
    ring[0] = after(ring[0], near[1])
    results, holders = {}, {0: packed}
    with jax.named_scope("expert_0"):
        own, given = half_expert([rows] * 2, [after(tokens, ring[0]), packed], near)
    results[0, 0] = own, given
    ring[1] = after(ring[1], own)

    def expert_rows(step, c, inputs, **options):
        with jax.named_scope(f"expert_{step}_{c}"):
            results[step, c] = half_expert([rows] * 2, inputs, near, **options)
        if step == far - 1 or (step, c) == (1, 1):
            give(step, c)
        return results[step, c][0]

    def give(step, c, *earlier):
        kept, given = results[step, c]
        results[step, c] = kept, send(after(given, *earlier) if earlier else given, cores, f"give_{step}_{c}")

    earlier = ring[1]
    for step in range(1, far - 1):
        holders[step] = ring[1]
        swapped = [
            send(block, cores, f"swap_{step}_{c}") for c, block in enumerate(ring[: 1 if step == 1 else 2])
        ]
        blocks = list(ring)
        ring[0] = send(blocks[0], forth, f"ring_{step + 1}_0")
        if step < far - 2:
            ring[1] = send(blocks[1], forth, f"ring_{step + 1}_1")
        for c in chains:
            if (step, c) == (1, 1):
                delayed = blocks[1]
                earlier = ring[1]
                continue
            kept = expert_rows(step, c, [after(blocks[c], earlier), swapped[c]])
            if (step, c) == (far - 2, 1):
                ring[1] = send(after(blocks[1], kept), forth, f"ring_{step + 1}_1")
            else:
                ring[c] = after(ring[c], kept)
                earlier = ring[c]
    holders[far - 1] = blocks[1] = ring[1]
    swapped = send(ring[0], cores, f"swap_{far - 1}_0")
    block, ring = ring[0], [send(ring[0], forth, f"ring_{far}_0")]
    kept = expert_rows(far - 1, 0, [after(block, kept), swapped])
    ring[0] = after(ring[0], kept)

    with jax.named_scope("expert_far_ring"):
        (given,) = half_expert([rows], ring, near, split=1, cost=0.3)
    swapped = send(ring[0], cores, f"swap_{far}")
    swapped = after(swapped, given)
    given = send(given, cores, "give_far")
    with jax.named_scope("expert_far_swapped"):
        (kept,) = half_expert([rows], [swapped], near, split=1, cost=0.3)
    last = blocks[1], send(after(blocks[1], kept), cores, f"swap_{far - 1}_1")
    earlier = rounded(total(kept, given))
    sums = [None, send(earlier, back, f"back_{far}_1")]
    mine, theirs = results[far - 1, 0]
    earlier = weighted(expert, holders[far - 1], 0, [after(mine, earlier), theirs])
    sums[0] = send(earlier, back, f"back_{far - 1}_0")
    earlier = expert_rows(far - 1, 1, [after(last[0], earlier), last[1]], cost=0.2)
    for step in range(far - 2, 1, -1):
        for c in chains:
            give(step, c, earlier)
    swapped = send(after(delayed, earlier), cores, "swap_1_1")
    steps = [(step, c) for step in range(far - 1, 0, -1) for c in chains][1:]
    for step, c in steps:
        mine, theirs = results[step, c]
        far_sum = (step, c) == (far - 1, 1)
        mine = after(mine, earlier)
        if far_sum:
            part = weighted(expert, holders[step], c, [mine], [sums[c]], dtype=jnp.float32)
            earlier = weighted(expert, holders[step], c, [after(theirs, part)], plain=[part])
        else:
            earlier = weighted(expert, holders[step], c, [mine, theirs], plain=[sums[c]])
        sums[c] = send(earlier, across if (step, c) == (1, 1) else back, f"back_{step}_{c}")
        if (step, c) == (far - 2, 0):
            give(1, 0, earlier)
        if far_sum:
            give(0, 0, earlier)
            earlier = expert_rows(1, 1, [after(delayed, earlier), swapped])
    own = weighted(expert, packed, 0, results[0, 0], plain=[sums[0]], dtype=jnp.float32)
    return last_sum(own, sums[1])


def solution(mesh):
    placed = (
        P(("groups", "blk"), None),
        P(("groups", "blk"), None),
        P(("groups", "blk"), None),
        P(None, "blk", None),
        P("blk", None),
    )

    def per_device(tokens, expert_ids, route_gate, gate_up, down_proj):
        experts = mesh.shape["blk"] // 2
        dense = experts <= min(GATE_ROWS, 2 * expert_ids.shape[1]) and tokens.shape[0] == LANES
        body = by_tokens if dense else by_slots
        return body(tokens, expert_ids, route_gate, gate_up, down_proj)

    return jax.shard_map(
        per_device,
        mesh=mesh,
        in_specs=placed,
        out_specs=P(("groups", "blk"), None),
        check_vma=False,
    )
```
